32 devices in a mesh: seq: 8 (over z, y), head: 4 (over x, core).
Axes of the slice: x: 2, y: 2, z: 4, core: 2. Of those that a mesh axis runs over, the one named last changes fastest.
Arguments:
- queries: bfloat16 [3072, 1536], P('seq', 'head'), may hold values from -34.5 to 34.5
- out_grad: bfloat16 [3072, 1536], P('seq', 'head'), may hold values from -48 to 48
- tile_mask: int32 [24, 2], P('seq'), may hold values from 0 to 1, as said below
- slot_caption: int32 [8, 2], replicated, may hold values from 0 to 2, as said below
- caption_cache: bfloat16 [2, 16, 512, 1536], P(None, 'seq', None, 'head'), may hold values from -6.1 to 6.1, as said below
- key_weight: bfloat16 [1536, 1536], P(None, 'head'), may hold values from -0.15625 to 0.15625
- value_weight: bfloat16 [1536, 1536], P(None, 'head'), may hold values from -0.15625 to 0.15625
Outputs:
- query_grad: bfloat16 [3072, 1536], P('seq', 'head')
- text_grad: bfloat16 [2, 512, 1536], P(None, 'seq', 'head')
The draws below stay inside these ranges and needn't reach their ends.
Inputs may be any that keep to these rules, and one draw needn't show every extreme that they name: `tile_mask`: each row has exactly one 1; it marks the slot of its seq index whose caption the tile reads. `slot_caption`: row d lists the captions that the tiles of seq index d read, each once; one entry always names a caption, the other names another caption or is 2 for an empty slot, and no tile points to an empty slot. A caption's tiles are consecutive and lie on consecutive seq indices; a seq index holds at most one caption boundary; every caption is read. `caption_cache`: slots that hold the same caption hold equal copies of its keys and values.
All inputs are finite; a program needn't handle non-finite values.
Results may differ from the reference program's by a relative error of at most 0.0096.
Values may be sent and summed in bfloat16 or wider, within the bound.
No kernel may reach another device: no remote copies, remote signals or barrier semaphores. Data moves between devices by JAX's collectives and lax.ppermute only.
A program may use at most 64 MiB of HBM per device.

```python
import jax
import jax.numpy as jnp
from jax import lax

D = 1536
HEADS = 12
DH = 128
L = 512
TILE = 128
SLOTS = 2
SPAN = 4
TOKENS = 3072
TILES_DEV = 3
CAPS = 2
HD = 1536
N_SEQ = 8


def caption_layout(key):
    base_key = jax.random.fold_in(key, 101)
    offsets = jax.random.randint(jax.random.fold_in(base_key, 1), (N_SEQ,), 0, TILES_DEV)
    forced = jax.random.randint(jax.random.fold_in(base_key, 2), (), 1, TILES_DEV)
    swapped = jax.random.randint(jax.random.fold_in(base_key, 4), (N_SEQ,), 0, 2).astype(jnp.int32)
    device = jnp.arange(N_SEQ, dtype=jnp.int32)
    starts = (device % SPAN == 0) & (device > 0)
    offsets = jnp.where(device == SPAN, forced, offsets)
    offsets = jnp.where(starts, offsets, 0).astype(jnp.int32)
    labels = jax.random.permutation(jax.random.fold_in(base_key, 3), CAPS).astype(jnp.int32)
    tile_index = jnp.arange(N_SEQ * TILES_DEV, dtype=jnp.int32)
    tile_device = tile_index // TILES_DEV
    local_index = tile_index % TILES_DEV
    later_part = (local_index >= offsets[tile_device]).astype(jnp.int32)
    own_slot = jnp.where(swapped[tile_device] == 1, 1 - later_part, later_part).astype(jnp.int32)
    device_group = device // SPAN
    earlier = jnp.where(offsets > 0, labels[jnp.maximum(device_group - 1, 0)], CAPS)
    current = labels[device_group]
    first_col = jnp.where(swapped == 1, current, earlier)
    second_col = jnp.where(swapped == 1, earlier, current)
    slot_table = jnp.stack([first_col, second_col], axis=1).astype(jnp.int32)
    return (own_slot, slot_table)


def caption_values(key):
    base_key = jax.random.fold_in(key, 202)
    drawn = jnp.clip(jax.random.normal(base_key, (2, CAPS, L, HD), jnp.float32), -6.0, 6.0)
    return drawn


def draw_tile_mask(key, part):
    own_slot, slot_table = caption_layout(key)
    return (own_slot[:, None] == jnp.arange(SLOTS, dtype=jnp.int32)[None, :]).astype(jnp.int32)


def draw_slot_caption(key, part):
    own_slot, slot_table = caption_layout(key)
    return slot_table


def draw_caption_cache(key, part):
    drawn = caption_values(key)
    own_slot, slot_table = caption_layout(key)
    picked = jnp.minimum(slot_table, CAPS - 1).reshape(-1)
    return drawn[:, picked].astype(jnp.bfloat16)


def draw_queries(key, part):
    base_key = jax.random.fold_in(key, 404)
    result = jnp.clip(jax.random.normal(base_key, (TOKENS, HD), jnp.float32), -6.0, 6.0)
    return result.astype(jnp.bfloat16)


def block_scale(rng, dims, cuts, least, top_value):
    def one(dim, shards_of):
        heights = jax.random.uniform(jax.random.fold_in(jax.random.fold_in(rng, 6), dim), (shards_of,), jnp.float32, least / len(cuts), top_value / len(cuts))
        return jnp.repeat(jnp.exp(heights), dims[dim] // shards_of).reshape((-1,) + (1,) * (len(dims) - dim - 1))

    loudness = one(*cuts[0])
    for cut in cuts[1:]:
        loudness = loudness * one(*cut)
    return loudness


def gaussian(stream_key, shape, scale, reach, split=(), kind=jnp.bfloat16):
    values = scale * jax.random.normal(stream_key, shape, jnp.float32)
    if split:
        values = values * block_scale(stream_key, shape, split, -0.22, 0.18)
    return jnp.clip(values, -reach, reach).astype(kind)


def setup_inputs(seed: int = 0) -> dict:
    arg_keys = jax.random.split(jax.random.key(seed), 8)
    queries = draw_queries(jax.random.fold_in(arg_keys[7], 71), 0)
    out_grad = gaussian(arg_keys[1], (TOKENS, HD), 8.0, 48.0, ((0, 8), (1, 4)))
    tile_mask = draw_tile_mask(jax.random.fold_in(arg_keys[7], 71), 0)
    slot_caption = draw_slot_caption(jax.random.fold_in(arg_keys[7], 71), 0)
    caption_cache = draw_caption_cache(jax.random.fold_in(arg_keys[7], 71), 0)
    key_weight = gaussian(arg_keys[5], (D, HD), D ** -0.5, 0.15625, ((1, 4),))
    value_weight = gaussian(arg_keys[6], (D, HD), D ** -0.5, 0.15625, ((1, 4),))
    return dict(queries=queries, out_grad=out_grad, tile_mask=tile_mask, slot_caption=slot_caption, caption_cache=caption_cache, key_weight=key_weight, value_weight=value_weight)


def tile_gradients(query_tiles, grad_tiles, slot_mask, cache_rows):
    highest = lax.Precision.HIGHEST
    inv_root = 1.0 / (DH ** 0.5)
    slot_index = jnp.sum(slot_mask * jnp.arange(SLOTS, dtype=jnp.int32)[None, :], axis=1)
    key_rows = cache_rows[0][slot_index].astype(jnp.float32)
    value_rows = cache_rows[1][slot_index].astype(jnp.float32)
    query_f = query_tiles.astype(jnp.float32)
    grad_f = grad_tiles.astype(jnp.float32)
    scores = jnp.einsum("tqhe,tjhe->thqj", query_f, key_rows, precision=highest) * inv_root
    row_max = jnp.max(scores, axis=-1, keepdims=True)
    exp_scores = jnp.exp(scores - row_max)
    attention = exp_scores / jnp.sum(exp_scores, axis=-1, keepdims=True)
    attention_lo = attention.astype(jnp.bfloat16).astype(jnp.float32)
    context = jnp.einsum("thqj,tjhe->tqhe", attention_lo, value_rows, precision=highest)
    row_dot = jnp.transpose(jnp.sum(grad_f * context, axis=-1), (0, 2, 1))
    attention_grad = jnp.einsum("tqhe,tjhe->thqj", grad_f, value_rows, precision=highest)
    score_grad = attention * (attention_grad - row_dot[..., None])
    score_lo = score_grad.astype(jnp.bfloat16).astype(jnp.float32)
    query_grad = (jnp.einsum("thqj,tjhe->tqhe", score_lo, key_rows, precision=highest) * inv_root).astype(jnp.bfloat16)
    key_pieces = jnp.einsum("thqj,tqhe->tjhe", score_lo, query_f, precision=highest) * inv_root
    value_pieces = jnp.einsum("thqj,tqhe->tjhe", attention_lo, grad_f, precision=highest)
    slot_onehot = slot_mask.astype(jnp.float32)
    key_part = jnp.einsum("ts,tjhe->sjhe", slot_onehot, key_pieces, precision=highest).astype(jnp.bfloat16)
    value_part = jnp.einsum("ts,tjhe->sjhe", slot_onehot, value_pieces, precision=highest).astype(jnp.bfloat16)
    return query_grad, key_part, value_part


def reference(queries, out_grad, tile_mask, slot_caption, caption_cache, key_weight, value_weight):
    highest = lax.Precision.HIGHEST
    query_all = queries.reshape(N_SEQ, TILES_DEV, TILE, HEADS, DH)
    grad_all = out_grad.reshape(N_SEQ, TILES_DEV, TILE, HEADS, DH)
    mask_all = tile_mask.reshape(N_SEQ, TILES_DEV, SLOTS)

    def device_step(totals, device):
        cache_rows = lax.dynamic_slice_in_dim(caption_cache, device * SLOTS, SLOTS, axis=1)
        cache_rows = cache_rows.reshape(2, SLOTS, L, HEADS, DH)
        query_grad, key_part, value_part = tile_gradients(query_all[device], grad_all[device], mask_all[device], cache_rows)
        captions_of = slot_caption[device]
        live_mask = (captions_of < CAPS).astype(jnp.float32)[:, None, None, None]
        clamped = jnp.minimum(captions_of, CAPS - 1).astype(jnp.int32)
        totals = totals.at[0, clamped].add(key_part.astype(jnp.float32) * live_mask)
        totals = totals.at[1, clamped].add(value_part.astype(jnp.float32) * live_mask)
        return totals, query_grad

    start = jnp.zeros((2, CAPS, L, HEADS, DH), jnp.float32)
    totals, query_grads = lax.scan(device_step, start, jnp.arange(N_SEQ, dtype=jnp.int32))
    key_total = totals[0].reshape(CAPS * L, HD)
    value_total = totals[1].reshape(CAPS * L, HD)
    text_grad = jnp.dot(key_total, key_weight.astype(jnp.float32).T, precision=highest)
    text_grad = text_grad + jnp.dot(value_total, value_weight.astype(jnp.float32).T, precision=highest)
    text_grad = text_grad.reshape(CAPS, L, D).astype(jnp.bfloat16)
    return query_grads.reshape(TOKENS, HD), text_grad
```

```python
import functools
import math

import jax
import jax.numpy as jnp
from jax import lax
from jax.experimental import pallas as pl
from jax.experimental.pallas import tpu as pltpu
from jax.sharding import PartitionSpec as P

DH = 128
L = 512
TILE = 128
SPAN = 4
F32 = jnp.float32
BF16 = jnp.bfloat16
VMEM_LIMIT = 48 * 1024 * 1024


def dot(a, b, contract):
    return lax.dot_general(a, b, ((contract[:1], contract[1:]), ((), ())), preferred_element_type=F32)


def tile_slot(mask_ref, tile):
    return mask_ref[1, tile]


def held(caps_ref, d, captions):
    first, second = caps_ref[0, d], caps_ref[1, d]
    single = jnp.logical_or(first == captions, second == captions)
    return single, jnp.where(first == captions, second, first)


def main_slot(caps_ref, me, captions):
    single, caption = held(caps_ref, me, captions)
    _, other = held(caps_ref, jnp.bitwise_xor(me, 1), captions)
    first = caps_ref[0, me]
    return jnp.where(single, jnp.where(first == captions, 1, 0), jnp.where(first == other, 1, 0))


def backward(key, value, query, grad):
    scores = dot(key, query, (1, 1))
    top = jnp.max(scores, axis=0, keepdims=True)
    exps = jnp.exp((scores - top) * (1.0 / math.sqrt(DH)))
    attention = exps / jnp.sum(exps, axis=0, keepdims=True)
    attention_lo = attention.astype(BF16)
    attention_grad = dot(value, grad, (1, 1))
    row_dot = jnp.sum(attention_lo.astype(F32) * attention_grad, axis=0, keepdims=True)
    score_lo = (attention * (attention_grad - row_dot)).astype(BF16)
    return attention_lo, score_lo


def ship_kernel(captions, tiles, mask_ref, caps_ref, q_ref, g_ref, out_ref):
    me = lax.axis_index("seq")
    mine = main_slot(caps_ref, me, captions)
    odd = jnp.bitwise_and(me, 1)
    for i in range(tiles - 1):
        tile = i + 1 - odd
        keep = (tile_slot(mask_ref, tile) != mine).astype(F32).astype(BF16)
        rows = pl.ds(pl.multiple_of(tile * TILE, TILE), TILE)
        out_ref[0, i * TILE : (i + 1) * TILE, :] = q_ref[rows, :] * keep
        out_ref[1, i * TILE : (i + 1) * TILE, :] = g_ref[rows, :] * keep


def own_kernel(captions, tiles, mask_ref, caps_ref, q_ref, g_ref, cache_ref, dq_ref, part_ref, key_t):
    me = lax.axis_index("seq")
    mine = main_slot(caps_ref, me, captions)
    inv_root = 1.0 / math.sqrt(DH)
    for s in range(cache_ref.shape[1]):
        key_t[s] = cache_ref[0, s].T
    probs, grads, queries, outs = [], [], [], []
    for t in range(tiles):
        slot = tile_slot(mask_ref, t)
        rows = slice(t * TILE, (t + 1) * TILE)
        query, grad = q_ref[rows, :], g_ref[rows, :]
        attention_lo, score_lo = backward(cache_ref[0, slot], cache_ref[1, slot], query, grad)
        dq_t = dot(key_t[slot], score_lo, (1, 0)) * inv_root
        dq_ref[rows, :] = dq_t.T.astype(BF16)
        keep = (slot == mine).astype(F32).astype(BF16)
        probs.append(attention_lo)
        grads.append(score_lo)
        queries.append(query * keep)
        outs.append(grad * keep)
    part_ref[0] = dot(jnp.concatenate(grads, axis=1), jnp.concatenate(queries, axis=0), (1, 0)) * inv_root
    part_ref[1] = dot(jnp.concatenate(probs, axis=1), jnp.concatenate(outs, axis=0), (1, 0))


def text_kernel(
    captions, heads, head_devices, caps_ref, recv_ref, part_ref, cache_hbm, wk_hbm, wv_hbm, out_ref,
    key_buf, value_buf, wk_buf, wv_buf, both, sems,
):
    me, col = lax.axis_index("seq"), lax.axis_index("head")
    mine = main_slot(caps_ref, me, captions)
    copies = [
        pltpu.make_async_copy(cache_hbm.at[0, mine], key_buf, sems.at[0]),
        pltpu.make_async_copy(cache_hbm.at[1, mine], value_buf, sems.at[1]),
        pltpu.make_async_copy(wk_hbm, wk_buf, sems.at[2]),
        pltpu.make_async_copy(wv_hbm, wv_buf, sems.at[3]),
    ]
    for c in copies:
        c.start()
    copies[0].wait()
    copies[1].wait()
    inv_root = 1.0 / math.sqrt(DH)
    width = heads * DH
    tiles = recv_ref.shape[1] // TILE
    for h in range(heads):
        cols = slice(h * DH, (h + 1) * DH)
        key, value = key_buf[:, cols], value_buf[:, cols]
        probs, grads = [], []
        for t in range(tiles):
            rows = slice(t * TILE, (t + 1) * TILE)
            attention_lo, score_lo = backward(key, value, recv_ref[0, rows, cols], recv_ref[1, rows, cols])
            probs.append(attention_lo)
            grads.append(score_lo)
        dk = dot(jnp.concatenate(grads, axis=1), recv_ref[0, :, cols], (1, 0)) * inv_root
        dv = dot(jnp.concatenate(probs, axis=1), recv_ref[1, :, cols], (1, 0))
        both[:, cols] = (part_ref[0, :, cols] + dk).astype(BF16)
        both[:, width + h * DH : width + (h + 1) * DH] = (part_ref[1, :, cols] + dv).astype(BF16)
    copies[2].wait()
    copies[3].wait()
    rows_out = out_ref.shape[2] * out_ref.shape[1]
    for rel in range(head_devices):
        rows = pl.ds(pl.multiple_of(jnp.bitwise_xor(col, rel) * width, width), width)
        text = dot(both[:, :width], wk_buf[rows, :], (1, 1)) + dot(both[:, width:], wv_buf[rows, :], (1, 1))
        out_ref[rel] = text.astype(BF16).reshape(out_ref.shape[1:])


def swap(array, axis, bit):
    n = lax.axis_size(axis)
    return lax.ppermute(array, axis, [(i, i ^ bit) for i in range(n)])


def shards_pairs(queries, out_grad, tile_mask, slot_caption, caption_cache, key_weight, value_weight):
    rows_here, width = queries.shape
    heads = width // DH
    tiles = rows_here // TILE
    slots = tile_mask.shape[1]
    seq_count, head_devices = lax.axis_size("seq"), lax.axis_size("head")
    captions = seq_count // SPAN
    block_rows = L // seq_count
    mask_t, caps_t = tile_mask.T, slot_caption.T
    smem = pl.BlockSpec(memory_space=pltpu.SMEM)
    vmem = pl.BlockSpec(memory_space=pltpu.VMEM)
    hbm = pl.BlockSpec(memory_space=pl.ANY)

    shipped = pl.pallas_call(
        functools.partial(ship_kernel, captions, tiles),
        out_shape=jax.ShapeDtypeStruct((2, (tiles - 1) * TILE, width), BF16),
        in_specs=[smem, smem, vmem, vmem],
        out_specs=vmem,
        compiler_params=pltpu.CompilerParams(vmem_limit_bytes=VMEM_LIMIT),
        name="ship",
    )(mask_t, caps_t, queries, out_grad)
    received = swap(shipped, "seq", 1)

    query_grad, part = pl.pallas_call(
        functools.partial(own_kernel, captions, tiles),
        grid=(heads,),
        out_shape=(
            jax.ShapeDtypeStruct((rows_here, width), BF16),
            jax.ShapeDtypeStruct((2, L, width), F32),
        ),
        in_specs=[
            smem,
            smem,
            pl.BlockSpec((rows_here, DH), lambda h: (0, h)),
            pl.BlockSpec((rows_here, DH), lambda h: (0, h)),
            pl.BlockSpec((2, slots, L, DH), lambda h: (0, 0, 0, h)),
        ],
        out_specs=(
            pl.BlockSpec((rows_here, DH), lambda h: (0, h)),
            pl.BlockSpec((2, L, DH), lambda h: (0, 0, h)),
        ),
        scratch_shapes=[pltpu.VMEM((slots, DH, L), BF16)],
        compiler_params=pltpu.CompilerParams(vmem_limit_bytes=VMEM_LIMIT),
        cost_estimate=pl.CostEstimate(
            flops=12 * rows_here * L * width, bytes_accessed=4_000_000, transcendentals=rows_here * L * heads
        ),
        name="own_tiles",
    )(mask_t, caps_t, queries, out_grad, caption_cache)

    text = pl.pallas_call(
        functools.partial(text_kernel, captions, heads, head_devices),
        out_shape=jax.ShapeDtypeStruct((head_devices, seq_count, block_rows, width), BF16),
        in_specs=[smem, vmem, vmem, hbm, hbm, hbm],
        out_specs=vmem,
        scratch_shapes=[
            pltpu.VMEM((L, width), BF16),
            pltpu.VMEM((L, width), BF16),
            pltpu.VMEM(key_weight.shape, BF16),
            pltpu.VMEM(value_weight.shape, BF16),
            pltpu.VMEM((L, 2 * width), BF16),
            pltpu.SemaphoreType.DMA((4,)),
        ],
        compiler_params=pltpu.CompilerParams(vmem_limit_bytes=VMEM_LIMIT),
        name="text",
    )(caps_t, received, part, caption_cache, key_weight, value_weight)

    bit = 1
    while bit < head_devices:
        text = text.reshape((-1, 2) + text.shape[1:])
        kept, sent = text[:, 0], text[:, 1]
        text = (kept.astype(F32) + swap(sent, "head", bit).astype(F32)).astype(BF16)
        bit *= 2
    arrived = lax.all_to_all(text[0], "seq", split_axis=0, concat_axis=0, tiled=True)
    table = slot_caption
    single = jnp.any(table == captions, axis=1)
    only = jnp.min(table, axis=1)
    partner = jnp.arange(seq_count) ^ 1
    mains = jnp.where(single, only, jnp.sum(table, axis=1) - only[partner])
    chosen = mains[None, :] == jnp.arange(captions)[:, None]
    text_grad = jnp.sum(
        jnp.where(chosen[:, :, None, None], arrived[None].astype(F32), 0.0), axis=1
    ).astype(BF16)
    return query_grad, text_grad


def shards_general(queries, out_grad, tile_mask, slot_caption, caption_cache, key_weight, value_weight):
    highest = lax.Precision.HIGHEST
    rows_here, width = queries.shape
    head_count = width // DH
    tile_count = rows_here // TILE
    slot_count = tile_mask.shape[1]
    inv_root = 1.0 / math.sqrt(DH)
    query_tiles = queries.reshape(tile_count, TILE, head_count, DH)
    grad_tiles = out_grad.reshape(tile_count, TILE, head_count, DH)
    slot_onehot = tile_mask.astype(jnp.float32)
    slot_lo = tile_mask.astype(jnp.bfloat16)
    key_rows = jnp.einsum(
        "ts,sjc->tjc", slot_lo, caption_cache[0], preferred_element_type=jnp.float32
    )
    key_rows = key_rows.astype(jnp.bfloat16).reshape(tile_count, L, head_count, DH)
    value_rows = jnp.einsum(
        "ts,sjc->tjc", slot_lo, caption_cache[1], preferred_element_type=jnp.float32
    )
    value_rows = value_rows.astype(jnp.bfloat16).reshape(tile_count, L, head_count, DH)
    scores = (
        jnp.einsum("tqhe,tjhe->thqj", query_tiles, key_rows, preferred_element_type=jnp.float32)
        * inv_root
    )
    row_max = jnp.max(scores, axis=-1, keepdims=True)
    exp_scores = jnp.exp(scores - row_max)
    attention = exp_scores / jnp.sum(exp_scores, axis=-1, keepdims=True)
    attention_lo = attention.astype(jnp.bfloat16)
    context = jnp.einsum(
        "thqj,tjhe->tqhe", attention_lo, value_rows, preferred_element_type=jnp.float32
    )
    row_dot = jnp.transpose(jnp.sum(grad_tiles.astype(jnp.float32) * context, axis=-1), (0, 2, 1))
    attention_grad = jnp.einsum(
        "tqhe,tjhe->thqj", grad_tiles, value_rows, preferred_element_type=jnp.float32
    )
    score_grad = attention * (attention_grad - row_dot[..., None])
    score_lo = score_grad.astype(jnp.bfloat16)
    query_grad = (
        jnp.einsum("thqj,tjhe->tqhe", score_lo, key_rows, preferred_element_type=jnp.float32)
        * inv_root
    )
    query_grad = query_grad.astype(jnp.bfloat16).reshape(rows_here, width)
    key_pieces = (
        jnp.einsum("thqj,tqhe->tjhe", score_lo, query_tiles, preferred_element_type=jnp.float32)
        * inv_root
    )
    value_pieces = jnp.einsum(
        "thqj,tqhe->tjhe", attention_lo, grad_tiles, preferred_element_type=jnp.float32
    )
    key_part = jnp.einsum("ts,tjhe->sjhe", slot_onehot, key_pieces, precision=highest)
    key_part = key_part.astype(jnp.bfloat16).reshape(slot_count, L, width)
    value_part = jnp.einsum("ts,tjhe->sjhe", slot_onehot, value_pieces, precision=highest)
    value_part = value_part.astype(jnp.bfloat16).reshape(slot_count, L, width)
    seq_count = lax.axis_size("seq")
    caption_count = seq_count // SPAN
    block_rows = L // seq_count
    features = key_weight.shape[0]
    flat_table = slot_caption.T.reshape(1, slot_count * seq_count)
    selector = (flat_table == jnp.arange(caption_count, dtype=jnp.int32)[:, None]).astype(
        jnp.float32
    )
    payload = jnp.stack([key_part, value_part]).reshape(2, slot_count, seq_count, block_rows, width)
    received = lax.all_to_all(payload, "seq", split_axis=2, concat_axis=2, tiled=True)
    received = received.reshape(2, slot_count * seq_count, block_rows * width).astype(jnp.float32)
    merged = jnp.einsum("cm,kmx->kcx", selector, received, precision=highest)
    merged = merged.reshape(2, caption_count * block_rows, width)
    summed = jnp.dot(merged[0], key_weight.astype(jnp.float32).T, precision=highest)
    summed = summed + jnp.dot(merged[1], value_weight.astype(jnp.float32).T, precision=highest)
    summed = summed.reshape(caption_count, block_rows, features)
    text_grad = lax.psum_scatter(summed, "head", scatter_dimension=2, tiled=True).astype(
        jnp.bfloat16
    )
    return (query_grad, text_grad)


def solution(mesh):
    seq_count, head_devices = mesh.shape["seq"], mesh.shape["head"]
    pairs = seq_count // SPAN <= 2 and seq_count % 2 == 0 and head_devices & (head_devices - 1) == 0
    placed = (
        P("seq", "head"),
        P("seq", "head"),
        P("seq", None),
        P(),
        P(None, "seq", None, "head"),
        P(None, "head"),
        P(None, "head"),
    )
    return jax.shard_map(
        shards_pairs if pairs else shards_general,
        mesh=mesh,
        in_specs=placed,
        out_specs=(P("seq", "head"), P(None, "seq", "head")),
        check_vma=False,
    )
```

```python
import functools
import math

import jax
import jax.numpy as jnp
from jax import lax
from jax.experimental import pallas as pl
from jax.experimental.pallas import tpu as pltpu
from jax.sharding import PartitionSpec as P

DH = 128
L = 512
TILE = 128
SPAN = 4
F32 = jnp.float32
BF16 = jnp.bfloat16
INV_ROOT = 1.0 / math.sqrt(DH)
KERNEL_LIMIT = 32 * 1024 * 1024
SMALL_LIMIT = 8 * 1024 * 1024


def dot(a, b, contract):
    return lax.dot_general(a, b, ((contract[:1], contract[1:]), ((), ())), preferred_element_type=F32)


def held(caps_ref, d, captions):
    first, second = caps_ref[0, d], caps_ref[1, d]
    single = jnp.logical_or(first == captions, second == captions)
    return single, jnp.where(first == captions, second, first)


def main_slot(caps_ref, d, captions):
    single, _ = held(caps_ref, d, captions)
    _, other = held(caps_ref, jnp.bitwise_xor(d, 1), captions)
    first = caps_ref[0, d]
    return jnp.where(single, jnp.where(first == captions, 1, 0), jnp.where(first == other, 1, 0))


def backward(key, value, query, grad):
    scores = dot(key, query, (1, 1))
    top = jnp.max(scores, axis=0, keepdims=True)
    exps = jnp.exp((scores - top) * INV_ROOT)
    attention = exps * (1.0 / jnp.sum(exps, axis=0, keepdims=True))
    attention_lo = attention.astype(BF16)
    attention_grad = dot(value, grad, (1, 1))
    row_dot = jnp.sum(attention_lo.astype(F32) * attention_grad, axis=0, keepdims=True)
    score_lo = (attention * (attention_grad - row_dot)).astype(BF16)
    return attention_lo, score_lo


def fetch(pairs, sems):
    copies = [pltpu.make_async_copy(a, b, sems.at[i]) for i, (a, b) in enumerate(pairs)]
    for c in copies:
        c.start()
    return copies


def stage_kernel(captions, tiles, mask_hbm, caps_hbm, q_hbm, g_hbm, *refs):
    *sent, mains_ref, mask_ref, caps_ref, q_buf, g_buf, sems = refs
    me = lax.axis_index("seq")
    first = 1 - jnp.bitwise_and(me, 1)
    rows = pl.ds(pl.multiple_of(first * TILE, TILE), (tiles - 1) * TILE)
    copies = fetch(
        [(mask_hbm, mask_ref), (caps_hbm, caps_ref), (q_hbm.at[rows], q_buf), (g_hbm.at[rows], g_buf)], sems
    )
    for c in copies:
        c.wait()
    mine = main_slot(caps_ref, me, captions)
    for i, out in enumerate(sent):
        keep = (mask_ref[mine, first + i] == 0).astype(F32).astype(BF16)
        at = slice(i * TILE, (i + 1) * TILE)
        out[0] = q_buf[at, :] * keep
        out[1] = g_buf[at, :] * keep
    for k in range(mains_ref.shape[0]):
        source = jnp.bitwise_xor(me, k)
        main = caps_ref[main_slot(caps_ref, source, captions), source]
        mains_ref[k : k + 1, :] = jnp.full((1, mains_ref.shape[1]), main, jnp.int32)


def own_kernel(
    captions, tiles, heads, mask_hbm, caps_hbm, q_hbm, g_hbm, cache_hbm, dq_ref, part_ref, main_ref,
    mask_ref, caps_ref, q_buf, g_buf, cache_buf, sems,
):
    me = lax.axis_index("seq")
    pairs = [(mask_hbm, mask_ref), (caps_hbm, caps_ref), (q_hbm, q_buf), (g_hbm, g_buf)]
    pairs += [(cache_hbm.at[:, :, :, pl.ds(h * DH, DH)], cache_buf.at[h]) for h in range(heads)]
    copies = fetch(pairs, sems)
    for c in copies[:4]:
        c.wait()
    mine = main_slot(caps_ref, me, captions)
    slots = [jnp.where(mask_ref[1, t] == 1, 1, 0) for t in range(tiles)]
    keeps = [(slot == mine).astype(F32).astype(BF16) for slot in slots]
    for h in range(heads):
        cols = slice(h * DH, (h + 1) * DH)
        copies[4 + h].wait()
        probs, grads, queries, outs = [], [], [], []
        for t in range(tiles):
            rows = slice(t * TILE, (t + 1) * TILE)
            query, grad = q_buf[rows, cols], g_buf[rows, cols]
            key, value = cache_buf[h, 0, slots[t]], cache_buf[h, 1, slots[t]]
            attention_lo, score_lo = backward(key, value, query, grad)
            dq_ref[rows, cols] = (dot(key.T, score_lo, (1, 0)) * INV_ROOT).T.astype(BF16)
            probs.append(attention_lo)
            grads.append(score_lo)
            queries.append(query * keeps[t])
            outs.append(grad * keeps[t])
        part_ref[0, :, cols] = dot(jnp.concatenate(grads, axis=1), jnp.concatenate(queries, axis=0), (1, 0))
        part_ref[1, :, cols] = dot(jnp.concatenate(probs, axis=1), jnp.concatenate(outs, axis=0), (1, 0))
        main_ref[0, :, cols] = cache_buf[h, 0, mine]
        main_ref[1, :, cols] = cache_buf[h, 1, mine]


def shipped(heads, recv_ref, main_ref, h):
    cols = slice(h * DH, (h + 1) * DH)
    query, grad = recv_ref[0, :, cols], recv_ref[1, :, cols]
    attention_lo, score_lo = backward(main_ref[0, :, cols], main_ref[1, :, cols], query, grad)
    return dot(score_lo, query, (1, 0)), dot(attention_lo, grad, (1, 0))


def shipped_kernel(heads, recv_ref, main_ref, part_ref, out_ref):
    for h in range(heads):
        cols = slice(h * DH, (h + 1) * DH)
        dk, dv = shipped(heads, recv_ref, main_ref, h)
        out_ref[0, :, cols] = part_ref[0, :, cols] + dk
        out_ref[1, :, cols] = part_ref[1, :, cols] + dv


def project(both_ref, wk_ref, wv_ref, rel, outs):
    width = both_ref.shape[1] // 2
    rows = pl.ds(pl.multiple_of(jnp.bitwise_xor(lax.axis_index("head"), rel) * width, width), width)
    text = dot(both_ref[:, :width], wk_ref[rows, :], (1, 1)) + dot(both_ref[:, width:], wv_ref[rows, :], (1, 1))
    text = text.astype(BF16)
    at = 0
    for out in outs:
        out[...] = text[at : at + out.shape[0] * out.shape[1]].reshape(out.shape)
        at += out.shape[0] * out.shape[1]


def first_text_kernel(heads, blocks, chunks, recv_ref, main_ref, part_ref, wk_ref, wv_ref, both_ref, *outs):
    me = lax.axis_index("seq")
    width = heads * DH
    block_rows = L // blocks
    for h in range(heads):
        cols = slice(h * DH, (h + 1) * DH)
        dk, dv = shipped(heads, recv_ref, main_ref, h)
        dk = ((part_ref[0, :, cols] + dk) * INV_ROOT).astype(BF16)
        dv = (part_ref[1, :, cols] + dv).astype(BF16)
        for s in range(blocks):
            rows = pl.ds(pl.multiple_of(jnp.bitwise_xor(me, s) * block_rows, block_rows), block_rows)
            both_ref[rows, h * DH : (h + 1) * DH] = dk[s * block_rows : (s + 1) * block_rows]
            both_ref[rows, width + h * DH : width + (h + 1) * DH] = dv[s * block_rows : (s + 1) * block_rows]
    project(both_ref, wk_ref, wv_ref, 3, outs[:chunks])
    project(both_ref, wk_ref, wv_ref, 2, outs[chunks:])


def second_text_kernel(chunks, both_ref, wk_ref, wv_ref, *outs):
    project(both_ref, wk_ref, wv_ref, 1, outs[:chunks])
    project(both_ref, wk_ref, wv_ref, 0, outs[chunks:])


def add_kernel(a_ref, b_ref, out_ref):
    out_ref[...] = (a_ref[...].astype(F32) + b_ref[...].astype(F32)).astype(BF16)


def split_add_kernel(a_ref, b_ref, *outs):
    for i, out in enumerate(outs):
        out[...] = (a_ref[i].astype(F32) + b_ref[i].astype(F32)).astype(BF16)


def final_kernel(mains_ref, *refs):
    *blocks, out_ref = refs
    captions = out_ref.shape[0]
    totals = [0.0] * captions
    for k, block in enumerate(blocks):
        value = block[...].astype(F32)
        main = jnp.tile(mains_ref[k : k + 1, :], (1, value.shape[1] // mains_ref.shape[1]))
        for c in range(captions):
            totals[c] += jnp.where(main == c, value, 0.0)
    for c in range(captions):
        out_ref[c] = totals[c].astype(BF16)


def swap(array, axis, bit):
    n = lax.axis_size(axis)
    return lax.ppermute(array, axis, [(i, i ^ bit) for i in range(n)])


def call(kernel, name, out_shape, operands, specs, scratch=(), limit=SMALL_LIMIT, hint_us=1.0):
    vmem = pl.BlockSpec(memory_space=pltpu.VMEM)
    return pl.pallas_call(
        kernel,
        out_shape=out_shape,
        in_specs=specs,
        out_specs=jax.tree.map(lambda _: vmem, out_shape),
        scratch_shapes=scratch,
        compiler_params=pltpu.CompilerParams(vmem_limit_bytes=limit),
        cost_estimate=pl.CostEstimate(flops=0, bytes_accessed=int(hint_us * 3_600_000), transcendentals=0),
        name=name,
    )(*operands)


def shards_pairs(queries, out_grad, tile_mask, slot_caption, caption_cache, key_weight, value_weight):
    rows_here, width = queries.shape
    heads = width // DH
    tiles = rows_here // TILE
    slots = tile_mask.shape[1]
    seq_count, head_devices = lax.axis_size("seq"), lax.axis_size("head")
    captions = seq_count // SPAN
    block_rows = L // seq_count
    chunks = 2
    per = seq_count // chunks
    held_back = [
        pltpu.with_memory_space_constraint(x, pltpu.HBM)
        for x in (tile_mask.T, slot_caption.T, queries, out_grad, caption_cache)
    ]
    mask_t, caps_t = held_back[:2]
    vmem = pl.BlockSpec(memory_space=pltpu.VMEM)
    hbm = pl.BlockSpec(memory_space=pltpu.HBM)
    scalars = [pltpu.SMEM(mask_t.shape, jnp.int32), pltpu.SMEM(caps_t.shape, jnp.int32)]

    def like(*shape, dtype=BF16):
        return jax.ShapeDtypeStruct(shape, dtype)

    *sent, mains = call(
        functools.partial(stage_kernel, captions, tiles),
        "stage",
        (like(2, TILE, width),) * (tiles - 1) + (like(seq_count, 128, dtype=jnp.int32),),
        held_back[:4],
        [hbm] * 4,
        scalars + [pltpu.VMEM(((tiles - 1) * TILE, width), BF16)] * 2 + [pltpu.SemaphoreType.DMA((4,))],
    )
    received = [swap(x, "seq", 1) for x in sent]

    query_grad, part, main = call(
        functools.partial(own_kernel, captions, tiles, heads),
        "own_tiles",
        (like(rows_here, width), like(2, L, width, dtype=F32), like(2, L, width)),
        held_back,
        [hbm] * 5,
        scalars
        + [pltpu.VMEM((rows_here, width), BF16)] * 2
        + [pltpu.VMEM((heads, 2, slots, L, DH), BF16), pltpu.SemaphoreType.DMA((4 + heads,))],
        limit=KERNEL_LIMIT,
        hint_us=5.0,
    )
    for tile in received[:-1]:
        part = call(
            functools.partial(shipped_kernel, heads),
            "shipped_tile",
            like(2, L, width, dtype=F32),
            (tile, main, part),
            [vmem] * 3,
            limit=KERNEL_LIMIT,
            hint_us=2.0,
        )
    piece = like(per, block_rows, width)
    both, *pieces = call(
        functools.partial(first_text_kernel, heads, seq_count, chunks),
        "first_text",
        (like(L, 2 * width),) + (piece,) * (2 * chunks),
        (received[-1], main, part, key_weight, value_weight),
        [vmem] * 5,
        limit=KERNEL_LIMIT,
        hint_us=3.0,
    )
    sent_x, kept_x = pieces[:chunks], pieces[chunks:]
    pieces = call(
        functools.partial(second_text_kernel, chunks),
        "second_text",
        (piece,) * (2 * chunks),
        (both, key_weight, value_weight),
        [vmem] * 3,
        limit=KERNEL_LIMIT,
        hint_us=1.0,
    )
    sent_own, kept_own = pieces[:chunks], pieces[chunks:]

    def add(a, b):
        return call(add_kernel, "add", like(*a.shape), (a, b), [vmem] * 2)

    order = range(chunks - 1, -1, -1)
    far = {c: add(kept_x[c], swap(sent_x[c], "head", 1)) for c in order}
    near = {c: add(kept_own[c], swap(sent_own[c], "head", 1)) for c in order}
    arrived = [None] * seq_count
    before = None
    for c in order:
        if before is not None:
            before, far[c] = lax.optimization_barrier((before, far[c]))
        if before is not None:
            finish(before, near, arrived, per, call, like, vmem, c + 1)
        before = swap(far[c], "head", 2)
    finish(before, near, arrived, per, call, like, vmem, 0)
    text_grad = call(
        final_kernel, "final", like(captions, block_rows, width), (mains, *arrived), [vmem] * (1 + seq_count)
    )
    return query_grad, text_grad


def finish(came, near, arrived, per, call, like, vmem, c):
    blocks = call(split_add_kernel, "split_add", (like(*came.shape[1:]),) * per, (near[c], came), [vmem] * 2)
    for i in range(per):
        k = c * per + i
        arrived[k] = swap(blocks[i], "seq", k) if k else blocks[i]


def shards_general(queries, out_grad, tile_mask, slot_caption, caption_cache, key_weight, value_weight):
    highest = lax.Precision.HIGHEST
    rows_here, width = queries.shape
    head_count = width // DH
    tile_count = rows_here // TILE
    slot_count = tile_mask.shape[1]
    inv_root = 1.0 / math.sqrt(DH)
    query_tiles = queries.reshape(tile_count, TILE, head_count, DH)
    grad_tiles = out_grad.reshape(tile_count, TILE, head_count, DH)
    slot_onehot = tile_mask.astype(jnp.float32)
    slot_lo = tile_mask.astype(jnp.bfloat16)
    key_rows = jnp.einsum(
        "ts,sjc->tjc", slot_lo, caption_cache[0], preferred_element_type=jnp.float32
    )
    key_rows = key_rows.astype(jnp.bfloat16).reshape(tile_count, L, head_count, DH)
    value_rows = jnp.einsum(
        "ts,sjc->tjc", slot_lo, caption_cache[1], preferred_element_type=jnp.float32
    )
    value_rows = value_rows.astype(jnp.bfloat16).reshape(tile_count, L, head_count, DH)
    scores = (
        jnp.einsum("tqhe,tjhe->thqj", query_tiles, key_rows, preferred_element_type=jnp.float32)
        * inv_root
    )
    row_max = jnp.max(scores, axis=-1, keepdims=True)
    exp_scores = jnp.exp(scores - row_max)
    attention = exp_scores / jnp.sum(exp_scores, axis=-1, keepdims=True)
    attention_lo = attention.astype(jnp.bfloat16)
    context = jnp.einsum(
        "thqj,tjhe->tqhe", attention_lo, value_rows, preferred_element_type=jnp.float32
    )
    row_dot = jnp.transpose(jnp.sum(grad_tiles.astype(jnp.float32) * context, axis=-1), (0, 2, 1))
    attention_grad = jnp.einsum(
        "tqhe,tjhe->thqj", grad_tiles, value_rows, preferred_element_type=jnp.float32
    )
    score_grad = attention * (attention_grad - row_dot[..., None])
    score_lo = score_grad.astype(jnp.bfloat16)
    query_grad = (
        jnp.einsum("thqj,tjhe->tqhe", score_lo, key_rows, preferred_element_type=jnp.float32)
        * inv_root
    )
    query_grad = query_grad.astype(jnp.bfloat16).reshape(rows_here, width)
    key_pieces = (
        jnp.einsum("thqj,tqhe->tjhe", score_lo, query_tiles, preferred_element_type=jnp.float32)
        * inv_root
    )
    value_pieces = jnp.einsum(
        "thqj,tqhe->tjhe", attention_lo, grad_tiles, preferred_element_type=jnp.float32
    )
    key_part = jnp.einsum("ts,tjhe->sjhe", slot_onehot, key_pieces, precision=highest)
    key_part = key_part.astype(jnp.bfloat16).reshape(slot_count, L, width)
    value_part = jnp.einsum("ts,tjhe->sjhe", slot_onehot, value_pieces, precision=highest)
    value_part = value_part.astype(jnp.bfloat16).reshape(slot_count, L, width)
    seq_count = lax.axis_size("seq")
    caption_count = seq_count // SPAN
    block_rows = L // seq_count
    features = key_weight.shape[0]
    flat_table = slot_caption.T.reshape(1, slot_count * seq_count)
    selector = (flat_table == jnp.arange(caption_count, dtype=jnp.int32)[:, None]).astype(
        jnp.float32
    )
    payload = jnp.stack([key_part, value_part]).reshape(2, slot_count, seq_count, block_rows, width)
    received = lax.all_to_all(payload, "seq", split_axis=2, concat_axis=2, tiled=True)
    received = received.reshape(2, slot_count * seq_count, block_rows * width).astype(jnp.float32)
    merged = jnp.einsum("cm,kmx->kcx", selector, received, precision=highest)
    merged = merged.reshape(2, caption_count * block_rows, width)
    summed = jnp.dot(merged[0], key_weight.astype(jnp.float32).T, precision=highest)
    summed = summed + jnp.dot(merged[1], value_weight.astype(jnp.float32).T, precision=highest)
    summed = summed.reshape(caption_count, block_rows, features)
    text_grad = lax.psum_scatter(summed, "head", scatter_dimension=2, tiled=True).astype(
        jnp.bfloat16
    )
    return (query_grad, text_grad)


def solution(mesh):
    seq_count, head_devices = mesh.shape["seq"], mesh.shape["head"]
    pairs = seq_count // SPAN <= 2 and seq_count % 2 == 0 and head_devices & (head_devices - 1) == 0
    placed = (
        P("seq", "head"),
        P("seq", "head"),
        P("seq", None),
        P(),
        P(None, "seq", None, "head"),
        P(None, "head"),
        P(None, "head"),
    )
    return jax.shard_map(
        shards_pairs if pairs else shards_general,
        mesh=mesh,
        in_specs=placed,
        out_specs=(P("seq", "head"), P(None, "seq", "head")),
        check_vma=False,
    )
```

```python
import functools
import math

import jax
import jax.numpy as jnp
from jax import lax
from jax.experimental import pallas as pl
from jax.experimental.pallas import tpu as pltpu
from jax.sharding import PartitionSpec as P

DH = 128
L = 512
TILE = 128
SPAN = 4
F32 = jnp.float32
BF16 = jnp.bfloat16
INV_ROOT = 1.0 / math.sqrt(DH)
CHUNK = 2
KERNEL_LIMIT = 32 * 1024 * 1024
SMALL_LIMIT = 8 * 1024 * 1024


def dot(a, b, contract):
    return lax.dot_general(a, b, ((contract[:1], contract[1:]), ((), ())), preferred_element_type=F32)


def held(caps_ref, d, captions):
    first, second = caps_ref[0, d], caps_ref[1, d]
    single = jnp.logical_or(first == captions, second == captions)
    return single, jnp.where(first == captions, second, first)


def main_slot(caps_ref, d, captions):
    single, _ = held(caps_ref, d, captions)
    _, other = held(caps_ref, jnp.bitwise_xor(d, 1), captions)
    first = caps_ref[0, d]
    return jnp.where(single, jnp.where(first == captions, 1, 0), jnp.where(first == other, 1, 0))


def backward(key, value, query, grad):
    scores = dot(key, query, (1, 1))
    top = jnp.max(scores, axis=0, keepdims=True)
    exps = jnp.exp((scores - top) * INV_ROOT)
    attention = exps * (1.0 / jnp.sum(exps, axis=0, keepdims=True))
    attention_lo = attention.astype(BF16)
    attention_grad = dot(value, grad, (1, 1))
    row_dot = jnp.sum(attention_lo.astype(F32) * attention_grad, axis=0, keepdims=True)
    score_lo = (attention * (attention_grad - row_dot)).astype(BF16)
    return attention_lo, score_lo


def fetch(pairs, sems):
    copies = [pltpu.make_async_copy(a, b, sems.at[i]) for i, (a, b) in enumerate(pairs)]
    for c in copies:
        c.start()
    return copies


def stage_kernel(captions, tiles, mask_hbm, caps_hbm, q_hbm, g_hbm, *refs):
    *sent, mains_ref, mask_ref, caps_ref, q_buf, g_buf, sems = refs
    me = lax.axis_index("seq")
    first = 1 - jnp.bitwise_and(me, 1)
    rows = pl.ds(pl.multiple_of(first * TILE, TILE), (tiles - 1) * TILE)
    copies = fetch(
        [(mask_hbm, mask_ref), (caps_hbm, caps_ref), (q_hbm.at[rows], q_buf), (g_hbm.at[rows], g_buf)], sems
    )
    for c in copies:
        c.wait()
    mine = main_slot(caps_ref, me, captions)
    for i, out in enumerate(sent):
        keep = (mask_ref[mine, first + i] == 0).astype(F32).astype(BF16)
        at = slice(i * TILE, (i + 1) * TILE)
        out[0] = q_buf[at, :] * keep
        out[1] = g_buf[at, :] * keep
    for k in range(mains_ref.shape[0]):
        source = jnp.bitwise_xor(me, k)
        main = caps_ref[main_slot(caps_ref, source, captions), source]
        mains_ref[k : k + 1, :] = jnp.full((1, mains_ref.shape[1]), main, jnp.int32)


def own_kernel(
    captions, tiles, heads, mask_hbm, caps_hbm, q_hbm, g_hbm, cache_hbm, dq_hbm, part_ref, main_ref,
    mask_ref, caps_ref, q_buf, g_buf, cache_buf, dq_buf, sems, out_sems,
):
    me = lax.axis_index("seq")
    pairs = [(mask_hbm, mask_ref), (caps_hbm, caps_ref), (q_hbm, q_buf), (g_hbm, g_buf)]
    pairs += [(cache_hbm.at[:, :, :, pl.ds(h * DH, DH)], cache_buf.at[h]) for h in range(heads)]
    copies = fetch(pairs, sems)
    for c in copies[:4]:
        c.wait()
    mine = main_slot(caps_ref, me, captions)
    slots = [jnp.where(mask_ref[1, t] == 1, 1, 0) for t in range(tiles)]
    keeps = [(slot == mine).astype(F32).astype(BF16) for slot in slots]
    stores = []
    for h in range(heads):
        cols = slice(h * DH, (h + 1) * DH)
        copies[4 + h].wait()
        probs, grads, queries, outs = [], [], [], []
        for t in range(tiles):
            rows = slice(t * TILE, (t + 1) * TILE)
            query, grad = q_buf[rows, cols], g_buf[rows, cols]
            key, value = cache_buf[h, 0, slots[t]], cache_buf[h, 1, slots[t]]
            attention_lo, score_lo = backward(key, value, query, grad)
            probs.append(attention_lo)
            grads.append(score_lo)
            queries.append(query * keeps[t])
            outs.append(grad * keeps[t])
        score_grads = jnp.concatenate(grads, axis=1)
        dq_main = dot(cache_buf[h, 0, mine].T, score_grads, (1, 0)) * INV_ROOT
        dq_other = dot(cache_buf[h, 0, 1 - mine].T, score_grads, (1, 0)) * INV_ROOT
        for t in range(tiles):
            rows = slice(t * TILE, (t + 1) * TILE)
            dq_t = jnp.where(slots[t] == mine, dq_main[:, rows], dq_other[:, rows])
            dq_buf[h, rows, :] = dq_t.astype(BF16).T
        store = pltpu.make_async_copy(dq_buf.at[h], dq_hbm.at[:, pl.ds(h * DH, DH)], out_sems.at[h])
        store.start()
        stores.append(store)
        part_ref[0, :, cols] = dot(score_grads, jnp.concatenate(queries, axis=0), (1, 0))
        part_ref[1, :, cols] = dot(jnp.concatenate(probs, axis=1), jnp.concatenate(outs, axis=0), (1, 0))
        main_ref[0, :, cols] = cache_buf[h, 0, mine]
        main_ref[1, :, cols] = cache_buf[h, 1, mine]
    for store in stores:
        store.wait()


def shipped(heads, recv_ref, main_ref, h):
    cols = slice(h * DH, (h + 1) * DH)
    query, grad = recv_ref[0, :, cols], recv_ref[1, :, cols]
    attention_lo, score_lo = backward(main_ref[0, :, cols], main_ref[1, :, cols], query, grad)
    return dot(score_lo, query, (1, 0)), dot(attention_lo, grad, (1, 0))


def shipped_kernel(heads, recv_ref, main_ref, part_ref, out_ref):
    for h in range(heads):
        cols = slice(h * DH, (h + 1) * DH)
        dk, dv = shipped(heads, recv_ref, main_ref, h)
        out_ref[0, :, cols] = part_ref[0, :, cols] + dk
        out_ref[1, :, cols] = part_ref[1, :, cols] + dv


def project(both_ref, wk_ref, wv_ref, rel, out_ref):
    width = both_ref.shape[1] // 2
    rows = pl.ds(pl.multiple_of(jnp.bitwise_xor(lax.axis_index("head"), rel) * width, width), width)
    text = dot(both_ref[:, :width], wk_ref[rows, :], (1, 1)) + dot(both_ref[:, width:], wv_ref[rows, :], (1, 1))
    out_ref[...] = text.astype(BF16).reshape(out_ref.shape)


def first_text_kernel(heads, blocks, recv_ref, main_ref, part_ref, wk_ref, wv_ref, both_ref, sent_ref, kept_ref):
    me = lax.axis_index("seq")
    width = heads * DH
    block_rows = L // blocks
    for h in range(heads):
        cols = slice(h * DH, (h + 1) * DH)
        dk, dv = shipped(heads, recv_ref, main_ref, h)
        dk = ((part_ref[0, :, cols] + dk) * INV_ROOT).astype(BF16)
        dv = (part_ref[1, :, cols] + dv).astype(BF16)
        for s in range(blocks):
            rows = pl.ds(pl.multiple_of(jnp.bitwise_xor(me, s) * block_rows, block_rows), block_rows)
            both_ref[rows, h * DH : (h + 1) * DH] = dk[s * block_rows : (s + 1) * block_rows]
            both_ref[rows, width + h * DH : width + (h + 1) * DH] = dv[s * block_rows : (s + 1) * block_rows]
    project(both_ref, wk_ref, wv_ref, 3, sent_ref)
    project(both_ref, wk_ref, wv_ref, 2, kept_ref)


def second_text_kernel(both_ref, wk_ref, wv_ref, sent_ref, kept_ref):
    project(both_ref, wk_ref, wv_ref, 1, sent_ref)
    project(both_ref, wk_ref, wv_ref, 0, kept_ref)


def pair_kernel(kept_ref, came_ref, *outs):
    at = 0
    for out in outs:
        part = slice(at, at + out.shape[0])
        out[...] = (kept_ref[part].astype(F32) + came_ref[part].astype(F32)).astype(BF16)
        at += out.shape[0]


def cross_kernel(first, kept_ref, came_ref, crossed_ref, *outs):
    for i, out in enumerate(outs):
        pair = (kept_ref[first + i].astype(F32) + came_ref[first + i].astype(F32)).astype(BF16)
        out[...] = (pair.astype(F32) + crossed_ref[i].astype(F32)).astype(BF16)


def final_kernel(order, mains_ref, *refs):
    *blocks, out_ref = refs
    captions = out_ref.shape[0]
    totals = [0.0] * captions
    for k, block in zip(order, blocks, strict=True):
        value = block[...].astype(F32)
        main = jnp.tile(mains_ref[k : k + 1, :], (1, value.shape[1] // mains_ref.shape[1]))
        for c in range(captions):
            totals[c] += jnp.where(main == c, value, 0.0)
    for c in range(captions):
        out_ref[c] = totals[c].astype(BF16)


def swap(array, axis, bit):
    n = lax.axis_size(axis)
    return lax.ppermute(array, axis, [(i, i ^ bit) for i in range(n)])


def call(kernel, name, out_shape, operands, specs, scratch=(), limit=SMALL_LIMIT, hint_us=1.0, out_specs=None):
    vmem = pl.BlockSpec(memory_space=pltpu.VMEM)
    return pl.pallas_call(
        kernel,
        out_shape=out_shape,
        in_specs=specs,
        out_specs=out_specs or jax.tree.map(lambda _: vmem, out_shape),
        scratch_shapes=scratch,
        compiler_params=pltpu.CompilerParams(vmem_limit_bytes=limit),
        cost_estimate=pl.CostEstimate(flops=0, bytes_accessed=int(hint_us * 3_600_000), transcendentals=0),
        name=name,
    )(*operands)


def shards_pairs(queries, out_grad, tile_mask, slot_caption, caption_cache, key_weight, value_weight):
    rows_here, width = queries.shape
    heads = width // DH
    tiles = rows_here // TILE
    slots = tile_mask.shape[1]
    seq_count, head_devices = lax.axis_size("seq"), lax.axis_size("head")
    captions = seq_count // SPAN
    block_rows = L // seq_count
    held_back = [
        pltpu.with_memory_space_constraint(x, pltpu.HBM)
        for x in (tile_mask.T, slot_caption.T, queries, out_grad, caption_cache)
    ]
    mask_t, caps_t = held_back[:2]
    vmem = pl.BlockSpec(memory_space=pltpu.VMEM)
    hbm = pl.BlockSpec(memory_space=pltpu.HBM)
    scalars = [pltpu.SMEM(mask_t.shape, jnp.int32), pltpu.SMEM(caps_t.shape, jnp.int32)]

    def like(*shape, dtype=BF16):
        return jax.ShapeDtypeStruct(shape, dtype)

    *sent, mains = call(
        functools.partial(stage_kernel, captions, tiles),
        "stage",
        (like(2, TILE, width),) * (tiles - 1) + (like(seq_count, 128, dtype=jnp.int32),),
        held_back[:4],
        [hbm] * 4,
        scalars + [pltpu.VMEM(((tiles - 1) * TILE, width), BF16)] * 2 + [pltpu.SemaphoreType.DMA((4,))],
    )
    received = [swap(x, "seq", 1) for x in sent]

    query_grad, part, main = call(
        functools.partial(own_kernel, captions, tiles, heads),
        "own_tiles",
        (like(rows_here, width), like(2, L, width, dtype=F32), like(2, L, width)),
        held_back,
        [hbm] * 5,
        scalars
        + [pltpu.VMEM((rows_here, width), BF16)] * 2
        + [
            pltpu.VMEM((heads, 2, slots, L, DH), BF16),
            pltpu.VMEM((heads, rows_here, DH), BF16),
            pltpu.SemaphoreType.DMA((4 + heads,)),
            pltpu.SemaphoreType.DMA((heads,)),
        ],
        limit=KERNEL_LIMIT,
        hint_us=5.0,
        out_specs=(hbm, vmem, vmem),
    )
    for tile in received[:-1]:
        part = call(
            functools.partial(shipped_kernel, heads),
            "shipped_tile",
            like(2, L, width, dtype=F32),
            (tile, main, part),
            [vmem] * 3,
            limit=KERNEL_LIMIT,
            hint_us=2.0,
        )
    blocks = like(seq_count, block_rows, width)
    both, sent, kept = call(
        functools.partial(first_text_kernel, heads, seq_count),
        "first_text",
        (like(L, 2 * width), blocks, blocks),
        (received[-1], main, part, key_weight, value_weight),
        [vmem] * 5,
        limit=KERNEL_LIMIT,
        hint_us=3.0,
    )
    sent_own, kept_own = call(
        second_text_kernel,
        "second_text",
        (blocks, blocks),
        (both, key_weight, value_weight),
        [vmem] * 3,
        limit=KERNEL_LIMIT,
        hint_us=1.0,
    )
    far = call(
        pair_kernel,
        "pair",
        (like(CHUNK, block_rows, width),) * (seq_count // CHUNK),
        (kept, swap(sent, "head", 1)),
        [vmem] * 2,
    )
    came_own = swap(sent_own, "head", 1)
    order, arrived = [], []
    half = seq_count // 2
    for i in [*range(half // CHUNK, seq_count // CHUNK), *reversed(range(half // CHUNK))]:
        first = i * CHUNK
        mine = call(
            functools.partial(cross_kernel, first),
            "cross",
            (like(block_rows, width),) * CHUNK,
            (kept_own, came_own, swap(far[i], "head", 2)),
            [vmem] * 3,
        )
        for k, block in reversed(list(enumerate(mine, first))):
            order.append(k)
            arrived.append(swap(block, "seq", k) if k else block)
    text_grad = call(
        functools.partial(final_kernel, order),
        "final",
        like(captions, block_rows, width),
        (mains, *arrived),
        [vmem] * (1 + seq_count),
    )
    return query_grad, text_grad


def shards_general(queries, out_grad, tile_mask, slot_caption, caption_cache, key_weight, value_weight):
    highest = lax.Precision.HIGHEST
    rows_here, width = queries.shape
    head_count = width // DH
    tile_count = rows_here // TILE
    slot_count = tile_mask.shape[1]
    inv_root = 1.0 / math.sqrt(DH)
    query_tiles = queries.reshape(tile_count, TILE, head_count, DH)
    grad_tiles = out_grad.reshape(tile_count, TILE, head_count, DH)
    slot_onehot = tile_mask.astype(jnp.float32)
    slot_lo = tile_mask.astype(jnp.bfloat16)
    key_rows = jnp.einsum(
        "ts,sjc->tjc", slot_lo, caption_cache[0], preferred_element_type=jnp.float32
    )
    key_rows = key_rows.astype(jnp.bfloat16).reshape(tile_count, L, head_count, DH)
    value_rows = jnp.einsum(
        "ts,sjc->tjc", slot_lo, caption_cache[1], preferred_element_type=jnp.float32
    )
    value_rows = value_rows.astype(jnp.bfloat16).reshape(tile_count, L, head_count, DH)
    scores = (
        jnp.einsum("tqhe,tjhe->thqj", query_tiles, key_rows, preferred_element_type=jnp.float32)
        * inv_root
    )
    row_max = jnp.max(scores, axis=-1, keepdims=True)
    exp_scores = jnp.exp(scores - row_max)
    attention = exp_scores / jnp.sum(exp_scores, axis=-1, keepdims=True)
    attention_lo = attention.astype(jnp.bfloat16)
    context = jnp.einsum(
        "thqj,tjhe->tqhe", attention_lo, value_rows, preferred_element_type=jnp.float32
    )
    row_dot = jnp.transpose(jnp.sum(grad_tiles.astype(jnp.float32) * context, axis=-1), (0, 2, 1))
    attention_grad = jnp.einsum(
        "tqhe,tjhe->thqj", grad_tiles, value_rows, preferred_element_type=jnp.float32
    )
    score_grad = attention * (attention_grad - row_dot[..., None])
    score_lo = score_grad.astype(jnp.bfloat16)
    query_grad = (
        jnp.einsum("thqj,tjhe->tqhe", score_lo, key_rows, preferred_element_type=jnp.float32)
        * inv_root
    )
    query_grad = query_grad.astype(jnp.bfloat16).reshape(rows_here, width)
    key_pieces = (
        jnp.einsum("thqj,tqhe->tjhe", score_lo, query_tiles, preferred_element_type=jnp.float32)
        * inv_root
    )
    value_pieces = jnp.einsum(
        "thqj,tqhe->tjhe", attention_lo, grad_tiles, preferred_element_type=jnp.float32
    )
    key_part = jnp.einsum("ts,tjhe->sjhe", slot_onehot, key_pieces, precision=highest)
    key_part = key_part.astype(jnp.bfloat16).reshape(slot_count, L, width)
    value_part = jnp.einsum("ts,tjhe->sjhe", slot_onehot, value_pieces, precision=highest)
    value_part = value_part.astype(jnp.bfloat16).reshape(slot_count, L, width)
    seq_count = lax.axis_size("seq")
    caption_count = seq_count // SPAN
    block_rows = L // seq_count
    features = key_weight.shape[0]
    flat_table = slot_caption.T.reshape(1, slot_count * seq_count)
    selector = (flat_table == jnp.arange(caption_count, dtype=jnp.int32)[:, None]).astype(
        jnp.float32
    )
    payload = jnp.stack([key_part, value_part]).reshape(2, slot_count, seq_count, block_rows, width)
    received = lax.all_to_all(payload, "seq", split_axis=2, concat_axis=2, tiled=True)
    received = received.reshape(2, slot_count * seq_count, block_rows * width).astype(jnp.float32)
    merged = jnp.einsum("cm,kmx->kcx", selector, received, precision=highest)
    merged = merged.reshape(2, caption_count * block_rows, width)
    summed = jnp.dot(merged[0], key_weight.astype(jnp.float32).T, precision=highest)
    summed = summed + jnp.dot(merged[1], value_weight.astype(jnp.float32).T, precision=highest)
    summed = summed.reshape(caption_count, block_rows, features)
    text_grad = lax.psum_scatter(summed, "head", scatter_dimension=2, tiled=True).astype(
        jnp.bfloat16
    )
    return (query_grad, text_grad)


def solution(mesh):
    seq_count, head_devices = mesh.shape["seq"], mesh.shape["head"]
    pairs = seq_count // SPAN <= 2 and seq_count % 2 == 0 and head_devices & (head_devices - 1) == 0
    placed = (
        P("seq", "head"),
        P("seq", "head"),
        P("seq", None),
        P(),
        P(None, "seq", None, "head"),
        P(None, "head"),
        P(None, "head"),
    )
    return jax.shard_map(
        shards_pairs if pairs else shards_general,
        mesh=mesh,
        in_specs=placed,
        out_specs=(P("seq", "head"), P(None, "seq", "head")),
        check_vma=False,
    )
```

```python
import functools
import math

import jax
import jax.numpy as jnp
from jax import lax
from jax.experimental import pallas as pl
from jax.experimental.pallas import tpu as pltpu
from jax.sharding import PartitionSpec as P

DH = 128
L = 512
TILE = 128
SPAN = 4
F32 = jnp.float32
BF16 = jnp.bfloat16
INV_ROOT = 1.0 / math.sqrt(DH)
KERNEL_LIMIT = 32 * 1024 * 1024
SMALL_LIMIT = 8 * 1024 * 1024


def dot(a, b, contract):
    return lax.dot_general(a, b, ((contract[:1], contract[1:]), ((), ())), preferred_element_type=F32)


def held(caps_ref, d, captions):
    first, second = caps_ref[0, d], caps_ref[1, d]
    single = jnp.logical_or(first == captions, second == captions)
    return single, jnp.where(first == captions, second, first)


def main_slot(caps_ref, d, captions):
    single, _ = held(caps_ref, d, captions)
    _, other = held(caps_ref, jnp.bitwise_xor(d, 1), captions)
    first = caps_ref[0, d]
    return jnp.where(single, jnp.where(first == captions, 1, 0), jnp.where(first == other, 1, 0))


def backward(key, value, query, grad):
    scores = dot(key, query, (1, 1))
    top = jnp.max(scores, axis=0, keepdims=True)
    exps = jnp.exp((scores - top) * INV_ROOT)
    attention = exps * (1.0 / jnp.sum(exps, axis=0, keepdims=True))
    attention_lo = attention.astype(BF16)
    attention_grad = dot(value, grad, (1, 1))
    row_dot = jnp.sum(attention_lo.astype(F32) * attention_grad, axis=0, keepdims=True)
    score_lo = (attention * (attention_grad - row_dot)).astype(BF16)
    return attention_lo, score_lo


def fetch(pairs, sems):
    copies = [pltpu.make_async_copy(a, b, sems.at[i]) for i, (a, b) in enumerate(pairs)]
    for c in copies:
        c.start()
    return copies


def stage_kernel(captions, tiles, mask_hbm, caps_hbm, q_hbm, g_hbm, *refs):
    *sent, mask_ref, caps_ref, q_buf, g_buf, sems = refs
    me = lax.axis_index("seq")
    first = 1 - jnp.bitwise_and(me, 1)
    rows = pl.ds(pl.multiple_of(first * TILE, TILE), (tiles - 1) * TILE)
    copies = fetch(
        [(mask_hbm, mask_ref), (caps_hbm, caps_ref), (q_hbm.at[rows], q_buf), (g_hbm.at[rows], g_buf)], sems
    )
    for c in copies:
        c.wait()
    mine = main_slot(caps_ref, me, captions)
    for i, out in enumerate(sent):
        keep = (mask_ref[mine, first + i] == 0).astype(F32).astype(BF16)
        at = slice(i * TILE, (i + 1) * TILE)
        out[0] = q_buf[at, :] * keep
        out[1] = g_buf[at, :] * keep


def own_kernel(
    captions, tiles, heads, mask_hbm, caps_hbm, q_hbm, g_hbm, cache_hbm, wk_hbm, wv_hbm,
    dq_hbm, part_ref, main_ref, weight_ref, mains_ref, mask_ref, caps_ref, q_buf, g_buf, cache_buf, dq_buf, sems, out_sems,
):
    me = lax.axis_index("seq")
    pairs = [(mask_hbm, mask_ref), (caps_hbm, caps_ref), (q_hbm, q_buf), (g_hbm, g_buf)]
    pairs += [(cache_hbm.at[:, :, :, pl.ds(h * DH, DH)], cache_buf.at[h]) for h in range(heads)]
    width = heads * DH
    pairs += [(wk_hbm, weight_ref.at[:, pl.ds(0, width)]), (wv_hbm, weight_ref.at[:, pl.ds(width, width)])]
    copies = fetch(pairs, sems)
    for c in copies[:4]:
        c.wait()
    mine = main_slot(caps_ref, me, captions)
    slots = [jnp.where(mask_ref[1, t] == 1, 1, 0) for t in range(tiles)]
    keeps = [(slot == mine).astype(F32).astype(BF16) for slot in slots]
    stores = []
    for h in range(heads):
        cols = slice(h * DH, (h + 1) * DH)
        copies[4 + h].wait()
        probs, grads, queries, outs = [], [], [], []
        for t in range(tiles):
            rows = slice(t * TILE, (t + 1) * TILE)
            query, grad = q_buf[rows, cols], g_buf[rows, cols]
            key, value = cache_buf[h, 0, slots[t]], cache_buf[h, 1, slots[t]]
            attention_lo, score_lo = backward(key, value, query, grad)
            probs.append(attention_lo)
            grads.append(score_lo)
            queries.append(query * keeps[t])
            outs.append(grad * keeps[t])
        score_grads = jnp.concatenate(grads, axis=1)
        dq_main = dot(cache_buf[h, 0, mine].T, score_grads, (1, 0)) * INV_ROOT
        dq_other = dot(cache_buf[h, 0, 1 - mine].T, score_grads, (1, 0)) * INV_ROOT
        for t in range(tiles):
            rows = slice(t * TILE, (t + 1) * TILE)
            dq_t = jnp.where(slots[t] == mine, dq_main[:, rows], dq_other[:, rows])
            dq_buf[h, rows, :] = dq_t.astype(BF16).T
        store = pltpu.make_async_copy(dq_buf.at[h], dq_hbm.at[:, pl.ds(h * DH, DH)], out_sems.at[h])
        store.start()
        stores.append(store)
        part_ref[0, :, cols] = dot(score_grads, jnp.concatenate(queries, axis=0), (1, 0))
        part_ref[1, :, cols] = dot(jnp.concatenate(probs, axis=1), jnp.concatenate(outs, axis=0), (1, 0))
        main_ref[0, :, cols] = cache_buf[h, 0, mine]
        main_ref[1, :, cols] = cache_buf[h, 1, mine]
    for k in range(mains_ref.shape[0]):
        source = jnp.bitwise_xor(me, k)
        main = caps_ref[main_slot(caps_ref, source, captions), source]
        mains_ref[k : k + 1, :] = jnp.full((1, mains_ref.shape[1]), main, jnp.int32)
    for copy in stores + copies[4 + heads :]:
        copy.wait()


def shipped(heads, recv_ref, main_ref, h):
    cols = slice(h * DH, (h + 1) * DH)
    query, grad = recv_ref[0, :, cols], recv_ref[1, :, cols]
    attention_lo, score_lo = backward(main_ref[0, :, cols], main_ref[1, :, cols], query, grad)
    return dot(score_lo, query, (1, 0)), dot(attention_lo, grad, (1, 0))


def shipped_kernel(heads, recv_ref, main_ref, part_ref, out_ref):
    for h in range(heads):
        cols = slice(h * DH, (h + 1) * DH)
        dk, dv = shipped(heads, recv_ref, main_ref, h)
        out_ref[0, :, cols] = part_ref[0, :, cols] + dk
        out_ref[1, :, cols] = part_ref[1, :, cols] + dv


def project(both_ref, weight_ref, rel, kept_ref, sent_ref):
    features = kept_ref.shape[2]
    chip = jnp.right_shift(lax.axis_index("head"), 1)
    rows = pl.ds(pl.multiple_of(jnp.bitwise_xor(chip, rel) * features, features), features)
    text = dot(both_ref[...], weight_ref[rows, :], (1, 1)).astype(BF16)
    half = text.shape[0] // 2
    kept_ref[...] = text[:half].reshape(kept_ref.shape)
    sent_ref[...] = text[half:].reshape(sent_ref.shape)


def first_text_kernel(heads, blocks, recv_ref, main_ref, part_ref, weight_ref, both_ref, kept_ref, sent_ref):
    me, core = lax.axis_index("seq"), jnp.bitwise_and(lax.axis_index("head"), 1)
    width = heads * DH
    block_rows = L // blocks
    places = []
    for s in range(blocks):
        rel = jnp.bitwise_xor(jnp.bitwise_xor(me, s), core)
        pair, quarter = jnp.right_shift(rel, 1), blocks // 4
        place = jnp.where(pair >= quarter, pair - quarter, 2 * quarter - 1 - pair)
        place += jnp.bitwise_and(rel, 1) * (blocks // 2)
        places.append(pl.ds(pl.multiple_of(place * block_rows, block_rows), block_rows))
    for h in range(heads):
        cols = slice(h * DH, (h + 1) * DH)
        dk, dv = shipped(heads, recv_ref, main_ref, h)
        dk = ((part_ref[0, :, cols] + dk) * INV_ROOT).astype(BF16)
        dv = (part_ref[1, :, cols] + dv).astype(BF16)
        for s, rows in enumerate(places):
            both_ref[rows, h * DH : (h + 1) * DH] = dk[s * block_rows : (s + 1) * block_rows]
            both_ref[rows, width + h * DH : width + (h + 1) * DH] = dv[s * block_rows : (s + 1) * block_rows]
    project(both_ref, weight_ref, 1, kept_ref, sent_ref)


def second_text_kernel(both_ref, weight_ref, kept_ref, sent_ref):
    project(both_ref, weight_ref, 0, kept_ref, sent_ref)


def pair_kernel(kept_ref, came_ref, *outs):
    for i, out in enumerate(outs):
        out[...] = (kept_ref[i].astype(F32) + came_ref[i].astype(F32)).astype(BF16)


def cross_kernel(i, kept_ref, came_ref, crossed_ref, out_ref):
    pair = (kept_ref[i].astype(F32) + came_ref[i].astype(F32)).astype(BF16)
    out_ref[...] = (pair.astype(F32) + crossed_ref[...].astype(F32)).astype(BF16)


def caption_kernel(bases, *refs):
    *blocks, own_ref, mains_ref, kept_ref, sent_ref = refs
    captions, _, width = kept_ref.shape
    core = jnp.bitwise_and(lax.axis_index("head"), 1)
    totals = [0.0] * captions
    for base, block in zip(bases, blocks, strict=True):
        value = block[...].astype(F32)
        if base == 0:
            value = jnp.where(core == 0, own_ref[...].astype(F32), value)
        main = mains_ref[pl.ds(base + core, 1), :]
        main = jnp.tile(main, (1, value.shape[1] // main.shape[1]))
        for c in range(captions):
            totals[c] += jnp.where(main == c, value, 0.0)
    for c in range(captions):
        low, high = totals[c][:, :width], totals[c][:, width:]
        kept_ref[c] = jnp.where(core == 0, low, high)
        sent_ref[c] = jnp.where(core == 0, high, low).astype(BF16)


def final_kernel(kept_ref, came_ref, out_ref):
    out_ref[...] = (kept_ref[...] + came_ref[...].astype(F32)).astype(BF16)


def swap(array, axis, bit):
    n = lax.axis_size(axis)
    return lax.ppermute(array, axis, [(i, i ^ bit) for i in range(n)])


def send(block, base):
    seq_count, head_devices = lax.axis_size("seq"), lax.axis_size("head")
    pairs = []
    for s in range(seq_count):
        for h in range(head_devices):
            target = s ^ base ^ (h & 1)
            if target != s:
                pairs.append((s * head_devices + h, target * head_devices + h))
    return lax.ppermute(block, ("seq", "head"), pairs)


def call(kernel, name, out_shape, operands, specs, scratch=(), limit=SMALL_LIMIT, hint_us=1.0, out_specs=None):
    vmem = pl.BlockSpec(memory_space=pltpu.VMEM)
    return pl.pallas_call(
        kernel,
        out_shape=out_shape,
        in_specs=specs,
        out_specs=out_specs or jax.tree.map(lambda _: vmem, out_shape),
        scratch_shapes=scratch,
        compiler_params=pltpu.CompilerParams(vmem_limit_bytes=limit),
        cost_estimate=pl.CostEstimate(flops=0, bytes_accessed=int(hint_us * 3_600_000), transcendentals=0),
        name=name,
    )(*operands)


def shards_pairs(queries, out_grad, tile_mask, slot_caption, caption_cache, key_weight, value_weight):
    rows_here, width = queries.shape
    heads = width // DH
    tiles = rows_here // TILE
    slots = tile_mask.shape[1]
    seq_count, head_devices = lax.axis_size("seq"), lax.axis_size("head")
    captions = seq_count // SPAN
    block_rows = L // seq_count
    held_back = [
        pltpu.with_memory_space_constraint(x, pltpu.HBM)
        for x in (tile_mask.T, slot_caption.T, queries, out_grad, caption_cache, key_weight, value_weight)
    ]
    mask_t, caps_t = held_back[:2]
    vmem = pl.BlockSpec(memory_space=pltpu.VMEM)
    hbm = pl.BlockSpec(memory_space=pltpu.HBM)
    scalars = [pltpu.SMEM(mask_t.shape, jnp.int32), pltpu.SMEM(caps_t.shape, jnp.int32)]

    def like(*shape, dtype=BF16):
        return jax.ShapeDtypeStruct(shape, dtype)

    sent = call(
        functools.partial(stage_kernel, captions, tiles),
        "stage",
        (like(2, TILE, width),) * (tiles - 1),
        held_back[:4],
        [hbm] * 4,
        scalars + [pltpu.VMEM(((tiles - 1) * TILE, width), BF16)] * 2 + [pltpu.SemaphoreType.DMA((4,))],
    )
    received = [swap(x, "seq", 1) for x in sent]

    query_grad, part, main, weight, mains = call(
        functools.partial(own_kernel, captions, tiles, heads),
        "own_tiles",
        (
            like(rows_here, width),
            like(2, L, width, dtype=F32),
            like(2, L, width),
            like(key_weight.shape[0], 2 * width),
            like(seq_count, 128, dtype=jnp.int32),
        ),
        held_back,
        [hbm] * 7,
        scalars
        + [pltpu.VMEM((rows_here, width), BF16)] * 2
        + [
            pltpu.VMEM((heads, 2, slots, L, DH), BF16),
            pltpu.VMEM((heads, rows_here, DH), BF16),
            pltpu.SemaphoreType.DMA((6 + heads,)),
            pltpu.SemaphoreType.DMA((heads,)),
        ],
        limit=KERNEL_LIMIT,
        hint_us=5.0,
        out_specs=(hbm, vmem, vmem, vmem, vmem),
    )
    for tile in received[:-1]:
        part = call(
            functools.partial(shipped_kernel, heads),
            "shipped_tile",
            like(2, L, width, dtype=F32),
            (tile, main, part),
            [vmem] * 3,
            limit=KERNEL_LIMIT,
            hint_us=2.0,
        )
    half = like(seq_count // 2, block_rows, 2 * width)
    both, kept, sent = call(
        functools.partial(first_text_kernel, heads, seq_count),
        "first_text",
        (like(L, 2 * width), half, half),
        (received[-1], main, part, weight),
        [vmem] * 4,
        limit=KERNEL_LIMIT,
        hint_us=3.0,
    )
    kept_own, sent_own = call(
        second_text_kernel,
        "second_text",
        (half, half),
        (both, weight),
        [vmem] * 2,
        limit=KERNEL_LIMIT,
        hint_us=1.0,
    )
    block = like(block_rows, 2 * width)
    far = call(pair_kernel, "pair", (block,) * (seq_count // 2), (kept, swap(sent, "head", 1)), [vmem] * 2)
    came_own = swap(sent_own, "head", 1)
    quarter = seq_count // 4
    bases = [2 * (quarter + i) for i in range(quarter)] + [2 * (quarter - 1 - i) for i in range(quarter)]
    arrived, own = [], None
    for i, base in enumerate(bases):
        mine = call(
            functools.partial(cross_kernel, i),
            "cross",
            block,
            (kept_own, came_own, swap(far[i], "head", 2)),
            [vmem] * 3,
        )
        if base == 0:
            own = mine
        arrived.append(send(mine, base))
    kept, sent = call(
        functools.partial(caption_kernel, bases),
        "captions",
        (like(captions, block_rows, width, dtype=F32), like(captions, block_rows, width)),
        (*arrived, own, mains),
        [vmem] * (2 + len(bases)),
    )
    text_grad = call(
        final_kernel, "final", like(captions, block_rows, width), (kept, swap(sent, "head", 1)), [vmem] * 2
    )
    return query_grad, text_grad


def shards_general(queries, out_grad, tile_mask, slot_caption, caption_cache, key_weight, value_weight):
    highest = lax.Precision.HIGHEST
    rows_here, width = queries.shape
    head_count = width // DH
    tile_count = rows_here // TILE
    slot_count = tile_mask.shape[1]
    inv_root = 1.0 / math.sqrt(DH)
    query_tiles = queries.reshape(tile_count, TILE, head_count, DH)
    grad_tiles = out_grad.reshape(tile_count, TILE, head_count, DH)
    slot_onehot = tile_mask.astype(jnp.float32)
    slot_lo = tile_mask.astype(jnp.bfloat16)
    key_rows = jnp.einsum(
        "ts,sjc->tjc", slot_lo, caption_cache[0], preferred_element_type=jnp.float32
    )
    key_rows = key_rows.astype(jnp.bfloat16).reshape(tile_count, L, head_count, DH)
    value_rows = jnp.einsum(
        "ts,sjc->tjc", slot_lo, caption_cache[1], preferred_element_type=jnp.float32
    )
    value_rows = value_rows.astype(jnp.bfloat16).reshape(tile_count, L, head_count, DH)
    scores = (
        jnp.einsum("tqhe,tjhe->thqj", query_tiles, key_rows, preferred_element_type=jnp.float32)
        * inv_root
    )
    row_max = jnp.max(scores, axis=-1, keepdims=True)
    exp_scores = jnp.exp(scores - row_max)
    attention = exp_scores / jnp.sum(exp_scores, axis=-1, keepdims=True)
    attention_lo = attention.astype(jnp.bfloat16)
    context = jnp.einsum(
        "thqj,tjhe->tqhe", attention_lo, value_rows, preferred_element_type=jnp.float32
    )
    row_dot = jnp.transpose(jnp.sum(grad_tiles.astype(jnp.float32) * context, axis=-1), (0, 2, 1))
    attention_grad = jnp.einsum(
        "tqhe,tjhe->thqj", grad_tiles, value_rows, preferred_element_type=jnp.float32
    )
    score_grad = attention * (attention_grad - row_dot[..., None])
    score_lo = score_grad.astype(jnp.bfloat16)
    query_grad = (
        jnp.einsum("thqj,tjhe->tqhe", score_lo, key_rows, preferred_element_type=jnp.float32)
        * inv_root
    )
    query_grad = query_grad.astype(jnp.bfloat16).reshape(rows_here, width)
    key_pieces = (
        jnp.einsum("thqj,tqhe->tjhe", score_lo, query_tiles, preferred_element_type=jnp.float32)
        * inv_root
    )
    value_pieces = jnp.einsum(
        "thqj,tqhe->tjhe", attention_lo, grad_tiles, preferred_element_type=jnp.float32
    )
    key_part = jnp.einsum("ts,tjhe->sjhe", slot_onehot, key_pieces, precision=highest)
    key_part = key_part.astype(jnp.bfloat16).reshape(slot_count, L, width)
    value_part = jnp.einsum("ts,tjhe->sjhe", slot_onehot, value_pieces, precision=highest)
    value_part = value_part.astype(jnp.bfloat16).reshape(slot_count, L, width)
    seq_count = lax.axis_size("seq")
    caption_count = seq_count // SPAN
    block_rows = L // seq_count
    features = key_weight.shape[0]
    flat_table = slot_caption.T.reshape(1, slot_count * seq_count)
    selector = (flat_table == jnp.arange(caption_count, dtype=jnp.int32)[:, None]).astype(
        jnp.float32
    )
    payload = jnp.stack([key_part, value_part]).reshape(2, slot_count, seq_count, block_rows, width)
    received = lax.all_to_all(payload, "seq", split_axis=2, concat_axis=2, tiled=True)
    received = received.reshape(2, slot_count * seq_count, block_rows * width).astype(jnp.float32)
    merged = jnp.einsum("cm,kmx->kcx", selector, received, precision=highest)
    merged = merged.reshape(2, caption_count * block_rows, width)
    summed = jnp.dot(merged[0], key_weight.astype(jnp.float32).T, precision=highest)
    summed = summed + jnp.dot(merged[1], value_weight.astype(jnp.float32).T, precision=highest)
    summed = summed.reshape(caption_count, block_rows, features)
    text_grad = lax.psum_scatter(summed, "head", scatter_dimension=2, tiled=True).astype(
        jnp.bfloat16
    )
    return (query_grad, text_grad)


def solution(mesh):
    seq_count, head_devices = mesh.shape["seq"], mesh.shape["head"]
    pairs = seq_count // SPAN <= 2 and seq_count & (seq_count - 1) == 0 and head_devices == 4
    placed = (
        P("seq", "head"),
        P("seq", "head"),
        P("seq", None),
        P(),
        P(None, "seq", None, "head"),
        P(None, "head"),
        P(None, "head"),
    )
    return jax.shard_map(
        shards_pairs if pairs else shards_general,
        mesh=mesh,
        in_specs=placed,
        out_specs=(P("seq", "head"), P(None, "seq", "head")),
        check_vma=False,
    )
```

```python
import functools
import math

import jax
import jax.numpy as jnp
from jax import lax
from jax.experimental import pallas as pl
from jax.experimental.pallas import tpu as pltpu
from jax.sharding import PartitionSpec as P

DH = 128
L = 512
TILE = 128
SPAN = 4
F32 = jnp.float32
BF16 = jnp.bfloat16
INV_ROOT = 1.0 / math.sqrt(DH)
KERNEL_LIMIT = 32 * 1024 * 1024
SMALL_LIMIT = 8 * 1024 * 1024


def dot(a, b, contract):
    return lax.dot_general(a, b, ((contract[:1], contract[1:]), ((), ())), preferred_element_type=F32)


def shipping(mask_ref, caps_ref, me, seq_count, tiles):
    odd = jnp.bitwise_and(me, 1)
    ones = mask_ref[1, 0]
    for t in range(1, tiles):
        ones += mask_ref[1, t]
    most = jnp.where(2 * ones > tiles, 1, 0)
    outer = jnp.where(odd == 0, 0, tiles - 1)
    at_end = jnp.where(odd == 0, me == 0, me == seq_count - 1)
    alone = jnp.logical_and(at_end, mask_ref[1 - most, outer] == 1)
    main = jnp.where(alone, 1 - most, most)
    return main, tiles - 1 - outer, jnp.where(alone, tiles // 2, outer)


def backward(key, value, query, grad):
    scores = dot(key, query, (1, 1))
    top = jnp.max(scores, axis=0, keepdims=True)
    exps = jnp.exp((scores - top) * INV_ROOT)
    attention = exps * (1.0 / jnp.sum(exps, axis=0, keepdims=True))
    attention_lo = attention.astype(BF16)
    attention_grad = dot(value, grad, (1, 1))
    row_dot = jnp.sum(attention_lo.astype(F32) * attention_grad, axis=0, keepdims=True)
    score_lo = (attention * (attention_grad - row_dot)).astype(BF16)
    return attention_lo, score_lo


def fetch(pairs, sems):
    copies = [pltpu.make_async_copy(a, b, sems.at[i]) for i, (a, b) in enumerate(pairs)]
    for c in copies:
        c.start()
    return copies


def stage_kernel(seq_count, tiles, mask_hbm, caps_hbm, q_hbm, g_hbm, cache_hbm, *refs):
    y_ref, z_ref, q_ref, g_ref, cache_ref, flags_ref, caption_ref, mask_ref, caps_ref, sems = refs
    me = lax.axis_index("seq")
    copies = fetch(
        [
            (mask_hbm, mask_ref),
            (caps_hbm, caps_ref),
            (q_hbm, q_ref),
            (g_hbm, g_ref),
            (cache_hbm.at[:, :, :, pl.ds(0, DH)], cache_ref),
        ],
        sems,
    )
    for c in copies[:4]:
        c.wait()
    mine, *picked = shipping(mask_ref, caps_ref, me, seq_count, tiles)
    for tile, out in zip(picked, (y_ref, z_ref), strict=True):
        keep = (mask_ref[mine, tile] == 0).astype(F32).astype(BF16)
        at = pl.ds(pl.multiple_of(tile * TILE, TILE), TILE)
        out[0] = q_ref[at, :] * keep
        out[1] = g_ref[at, :] * keep
    lanes = (1, flags_ref.shape[1])
    for t in range(tiles):
        flags_ref[t : t + 1, :] = jnp.full(lanes, mask_ref[1, t].astype(F32), F32)
        flags_ref[tiles + t : tiles + t + 1, :] = jnp.full(lanes, mask_ref[mine, t].astype(F32), F32)
    flags_ref[2 * tiles : 2 * tiles + 1, :] = jnp.full(lanes, mine.astype(F32), F32)
    caption_ref[...] = jnp.full(caption_ref.shape, caps_ref[mine, me].astype(F32), F32).astype(BF16)
    copies[4].wait()


def pick(flag, pair):
    return pair[0] * (1.0 - flag).astype(BF16) + pair[1] * flag.astype(BF16)


def own_kernel(
    tiles, heads, flags_ref, q_ref, g_ref, first_ref, cache_hbm, wk_hbm, wv_hbm,
    dq_hbm, part_ref, main_ref, weight_ref, cache_buf, dq_buf, sems, out_sems,
):
    pairs = [(cache_hbm.at[:, :, :, pl.ds(h * DH, DH)], cache_buf.at[h - 1]) for h in range(1, heads)]
    width = heads * DH
    pairs += [(wk_hbm, weight_ref.at[:, pl.ds(0, width)]), (wv_hbm, weight_ref.at[:, pl.ds(width, width)])]
    copies = fetch(pairs, sems)
    slots = [flags_ref[t : t + 1, :] for t in range(tiles)]
    keeps = [flags_ref[tiles + t : tiles + t + 1, :] for t in range(tiles)]
    mine = flags_ref[2 * tiles : 2 * tiles + 1, :]
    stores = []
    for h in range(heads):
        cols = slice(h * DH, (h + 1) * DH)
        if h:
            copies[h - 1].wait()
        cache = first_ref if h == 0 else cache_buf.at[h - 1]
        keys, values = (cache[0, 0], cache[0, 1]), (cache[1, 0], cache[1, 1])
        probs, grads, queries, outs = [], [], [], []
        for t in range(tiles):
            rows = slice(t * TILE, (t + 1) * TILE)
            query, grad = q_ref[rows, cols], g_ref[rows, cols]
            attention_lo, score_lo = backward(pick(slots[t], keys), pick(slots[t], values), query, grad)
            probs.append(attention_lo)
            grads.append(score_lo)
            queries.append(query * keeps[t].astype(BF16))
            outs.append(grad * keeps[t].astype(BF16))
        score_grads = jnp.concatenate(grads, axis=1)
        dq = [dot(key.T, score_grads, (1, 0)) * INV_ROOT for key in keys]
        for t in range(tiles):
            rows = slice(t * TILE, (t + 1) * TILE)
            dq_t = jnp.where(slots[t] == 1.0, dq[1][:, rows], dq[0][:, rows])
            dq_buf[h, rows, :] = dq_t.astype(BF16).T
        store = pltpu.make_async_copy(dq_buf.at[h], dq_hbm.at[:, pl.ds(h * DH, DH)], out_sems.at[h])
        store.start()
        stores.append(store)
        part_ref[0, :, cols] = dot(score_grads, jnp.concatenate(queries, axis=0), (1, 0))
        part_ref[1, :, cols] = dot(jnp.concatenate(probs, axis=1), jnp.concatenate(outs, axis=0), (1, 0))
        main_ref[0, :, cols] = pick(mine, keys)
        main_ref[1, :, cols] = pick(mine, values)
    for copy in stores + copies[heads - 1 :]:
        copy.wait()


def gather_parts(heads, blocks, y_ref, z_ref, main_ref, part_ref, both_ref):
    me, core = lax.axis_index("seq"), jnp.bitwise_and(lax.axis_index("head"), 1)
    block_rows, width = L // blocks, heads * DH
    places = []
    for s in range(blocks):
        rel = jnp.bitwise_xor(jnp.bitwise_xor(me, s), core)
        pair, quarter = jnp.right_shift(rel, 1), blocks // 4
        place = jnp.where(pair >= quarter, pair - quarter, 2 * quarter - 1 - pair)
        place += jnp.bitwise_and(rel, 1) * (blocks // 2)
        places.append(pl.ds(pl.multiple_of(place * block_rows, block_rows), block_rows))
    for h in range(heads):
        cols = slice(h * DH, (h + 1) * DH)
        query, grad = y_ref[0, :, cols] + z_ref[0, :, cols], y_ref[1, :, cols] + z_ref[1, :, cols]
        attention_lo, score_lo = backward(main_ref[0, :, cols], main_ref[1, :, cols], query, grad)
        dk = ((part_ref[0, :, cols] + dot(score_lo, query, (1, 0))) * INV_ROOT).astype(BF16)
        dv = (part_ref[1, :, cols] + dot(attention_lo, grad, (1, 0))).astype(BF16)
        for s, rows in enumerate(places):
            both_ref[rows, h * DH : (h + 1) * DH] = dk[s * block_rows : (s + 1) * block_rows]
            both_ref[rows, width + h * DH : width + (h + 1) * DH] = dv[s * block_rows : (s + 1) * block_rows]


def project(both_ref, weight_ref, rel, kept_ref, sent_ref):
    features = kept_ref.shape[2]
    chip = jnp.right_shift(lax.axis_index("head"), 1)
    rows = pl.ds(pl.multiple_of(jnp.bitwise_xor(chip, rel) * features, features), features)
    text = dot(both_ref[...], weight_ref[rows, :], (1, 1)).astype(BF16)
    half = text.shape[0] // 2
    kept_ref[...] = text[:half].reshape(kept_ref.shape)
    sent_ref[...] = text[half:].reshape(sent_ref.shape)


def first_text_kernel(heads, blocks, y_ref, z_ref, main_ref, part_ref, weight_ref, both_ref, kept_ref, sent_ref):
    gather_parts(heads, blocks, y_ref, z_ref, main_ref, part_ref, both_ref)
    project(both_ref, weight_ref, 1, kept_ref, sent_ref)


def second_text_kernel(both_ref, weight_ref, kept_ref, sent_ref):
    project(both_ref, weight_ref, 0, kept_ref, sent_ref)


def pair_kernel(kept_ref, came_ref, *outs):
    for i, out in enumerate(outs):
        out[...] = (kept_ref[i].astype(F32) + came_ref[i].astype(F32)).astype(BF16)


def cross_kernel(i, kept_ref, came_ref, crossed_ref, caption_ref, out_ref):
    pair = (kept_ref[i].astype(F32) + came_ref[i].astype(F32)).astype(BF16)
    total = (pair.astype(F32) + crossed_ref[...].astype(F32)).astype(BF16)
    height, lanes = out_ref.shape[1:]
    across = total.shape[1] // lanes
    for n in range(out_ref.shape[0] - 1):
        r, c = n // across * height, n % across * lanes
        out_ref[n] = total[r : r + height, c : c + lanes]
    out_ref[out_ref.shape[0] - 1] = caption_ref[...]


def caption_kernel(bases, *refs):
    *blocks, own_ref, kept_ref, sent_ref = refs
    captions, block_rows, width = kept_ref.shape
    _, height, lanes = own_ref.shape
    half = width // lanes
    across = 2 * half
    core = jnp.bitwise_and(lax.axis_index("head"), 1)
    for r in range(block_rows // height):
        totals = [[0.0] * across for _ in range(captions)]
        for base, block in zip(bases, blocks, strict=True):
            caption = block[block.shape[0] - 1].astype(F32)
            if base == 0:
                caption = jnp.where(core == 0, own_ref[own_ref.shape[0] - 1].astype(F32), caption)
            for n in range(across):
                value = block[r * across + n].astype(F32)
                if base == 0:
                    value = jnp.where(core == 0, own_ref[r * across + n].astype(F32), value)
                for c in range(captions):
                    totals[c][n] += jnp.where(caption == c, value, 0.0)
        rows = slice(r * height, (r + 1) * height)
        for c in range(captions):
            for n in range(half):
                cols = slice(n * lanes, (n + 1) * lanes)
                low, high = totals[c][n], totals[c][half + n]
                kept_ref[c, rows, cols] = jnp.where(core == 0, low, high)
                sent_ref[c, rows, cols] = jnp.where(core == 0, high, low).astype(BF16)


def final_kernel(kept_ref, came_ref, out_ref):
    out_ref[...] = (kept_ref[...] + came_ref[...].astype(F32)).astype(BF16)


def swap(array, axis, bit):
    n = lax.axis_size(axis)
    return lax.ppermute(array, axis, [(i, i ^ bit) for i in range(n)])


def send(block, base):
    seq_count, head_devices = lax.axis_size("seq"), lax.axis_size("head")
    pairs = []
    for s in range(seq_count):
        for h in range(head_devices):
            target = s ^ base ^ (h & 1)
            if target != s:
                pairs.append((s * head_devices + h, target * head_devices + h))
    return lax.ppermute(block, ("seq", "head"), pairs)


def call(kernel, name, out_shape, operands, specs, scratch=(), limit=SMALL_LIMIT, hint_us=1.0, out_specs=None):
    vmem = pl.BlockSpec(memory_space=pltpu.VMEM)
    return pl.pallas_call(
        kernel,
        out_shape=out_shape,
        in_specs=specs,
        out_specs=out_specs or jax.tree.map(lambda _: vmem, out_shape),
        scratch_shapes=scratch,
        compiler_params=pltpu.CompilerParams(vmem_limit_bytes=limit),
        cost_estimate=pl.CostEstimate(flops=0, bytes_accessed=int(hint_us * 3_600_000), transcendentals=0),
        name=name,
    )(*operands)


def shards_pairs(queries, out_grad, tile_mask, slot_caption, caption_cache, key_weight, value_weight):
    rows_here, width = queries.shape
    heads = width // DH
    tiles = rows_here // TILE
    slots = tile_mask.shape[1]
    seq_count, head_devices = lax.axis_size("seq"), lax.axis_size("head")
    captions = seq_count // SPAN
    block_rows = L // seq_count
    held_back = [
        pltpu.with_memory_space_constraint(x, pltpu.HBM)
        for x in (tile_mask.T, slot_caption.T, queries, out_grad, caption_cache, key_weight, value_weight)
    ]
    mask_t, caps_t = held_back[:2]
    vmem = pl.BlockSpec(memory_space=pltpu.VMEM)
    hbm = pl.BlockSpec(memory_space=pltpu.HBM)

    def like(*shape, dtype=BF16):
        return jax.ShapeDtypeStruct(shape, dtype)

    to_y, to_z, q_here, g_here, cache_first, flags, caption = call(
        functools.partial(stage_kernel, seq_count, tiles),
        "stage",
        (
            like(2, TILE, width),
            like(2, TILE, width),
            like(rows_here, width),
            like(rows_here, width),
            like(2, slots, L, DH),
            like(8 * (-(-(2 * tiles + 1) // 8)), 128, dtype=F32),
            like(16, 128),
        ),
        held_back[:5],
        [hbm] * 5,
        [
            pltpu.SMEM(mask_t.shape, jnp.int32),
            pltpu.SMEM(caps_t.shape, jnp.int32),
            pltpu.SemaphoreType.DMA((5,)),
        ],
        limit=KERNEL_LIMIT,
    )
    from_y = swap(to_y, "seq", 1)
    from_z = lax.ppermute(to_z, "seq", [(s, (s + (2 if s & 1 else -2)) % seq_count) for s in range(seq_count)])

    query_grad, part, main, weight = call(
        functools.partial(own_kernel, tiles, heads),
        "own_tiles",
        (
            like(rows_here, width),
            like(2, L, width, dtype=F32),
            like(2, L, width),
            like(key_weight.shape[0], 2 * width),
        ),
        (flags, q_here, g_here, cache_first, *held_back[4:]),
        [vmem] * 4 + [hbm] * 3,
        [
            pltpu.VMEM((heads - 1, 2, slots, L, DH), BF16),
            pltpu.VMEM((heads, rows_here, DH), BF16),
            pltpu.SemaphoreType.DMA((heads + 1,)),
            pltpu.SemaphoreType.DMA((heads,)),
        ],
        limit=KERNEL_LIMIT,
        hint_us=5.0,
        out_specs=(hbm, vmem, vmem, vmem),
    )
    half = like(seq_count // 2, block_rows, 2 * width)
    both, kept, sent = call(
        functools.partial(first_text_kernel, heads, seq_count),
        "first_text",
        (like(L, 2 * width), half, half),
        (from_y, from_z, main, part, weight),
        [vmem] * 5,
        limit=KERNEL_LIMIT,
        hint_us=2.0,
    )
    kept_own, sent_own = call(
        second_text_kernel,
        "second_text",
        (half, half),
        (both, weight),
        [vmem] * 2,
        limit=KERNEL_LIMIT,
        hint_us=1.0,
    )
    block = like(block_rows, 2 * width)
    far = call(pair_kernel, "pair", (block,) * (seq_count // 2), (kept, swap(sent, "head", 1)), [vmem] * 2)
    came_own = swap(sent_own, "head", 1)
    quarter = seq_count // 4
    bases = [2 * (quarter + i) for i in range(quarter)] + [2 * (quarter - 1 - i) for i in range(quarter)]
    arrived, own = [], None
    for i, base in enumerate(bases):
        mine = call(
            functools.partial(cross_kernel, i),
            "cross",
            like(block_rows // 16 * (2 * width // 128) + 1, 16, 128),
            (kept_own, came_own, swap(far[i], "head", 2), caption),
            [vmem] * 4,
        )
        if base == 0:
            own = mine
        arrived.append(send(mine, base))
    kept, sent = call(
        functools.partial(caption_kernel, bases[::-1]),
        "captions",
        (like(captions, block_rows, width, dtype=F32), like(captions, block_rows, width)),
        (*reversed(arrived), own),
        [vmem] * (1 + len(bases)),
    )
    text_grad = call(
        final_kernel, "final", like(captions, block_rows, width), (kept, swap(sent, "head", 1)), [vmem] * 2
    )
    return query_grad, text_grad


def shards_general(queries, out_grad, tile_mask, slot_caption, caption_cache, key_weight, value_weight):
    highest = lax.Precision.HIGHEST
    rows_here, width = queries.shape
    head_count = width // DH
    tile_count = rows_here // TILE
    slot_count = tile_mask.shape[1]
    inv_root = 1.0 / math.sqrt(DH)
    query_tiles = queries.reshape(tile_count, TILE, head_count, DH)
    grad_tiles = out_grad.reshape(tile_count, TILE, head_count, DH)
    slot_onehot = tile_mask.astype(jnp.float32)
    slot_lo = tile_mask.astype(jnp.bfloat16)
    key_rows = jnp.einsum(
        "ts,sjc->tjc", slot_lo, caption_cache[0], preferred_element_type=jnp.float32
    )
    key_rows = key_rows.astype(jnp.bfloat16).reshape(tile_count, L, head_count, DH)
    value_rows = jnp.einsum(
        "ts,sjc->tjc", slot_lo, caption_cache[1], preferred_element_type=jnp.float32
    )
    value_rows = value_rows.astype(jnp.bfloat16).reshape(tile_count, L, head_count, DH)
    scores = (
        jnp.einsum("tqhe,tjhe->thqj", query_tiles, key_rows, preferred_element_type=jnp.float32)
        * inv_root
    )
    row_max = jnp.max(scores, axis=-1, keepdims=True)
    exp_scores = jnp.exp(scores - row_max)
    attention = exp_scores / jnp.sum(exp_scores, axis=-1, keepdims=True)
    attention_lo = attention.astype(jnp.bfloat16)
    context = jnp.einsum(
        "thqj,tjhe->tqhe", attention_lo, value_rows, preferred_element_type=jnp.float32
    )
    row_dot = jnp.transpose(jnp.sum(grad_tiles.astype(jnp.float32) * context, axis=-1), (0, 2, 1))
    attention_grad = jnp.einsum(
        "tqhe,tjhe->thqj", grad_tiles, value_rows, preferred_element_type=jnp.float32
    )
    score_grad = attention * (attention_grad - row_dot[..., None])
    score_lo = score_grad.astype(jnp.bfloat16)
    query_grad = (
        jnp.einsum("thqj,tjhe->tqhe", score_lo, key_rows, preferred_element_type=jnp.float32)
        * inv_root
    )
    query_grad = query_grad.astype(jnp.bfloat16).reshape(rows_here, width)
    key_pieces = (
        jnp.einsum("thqj,tqhe->tjhe", score_lo, query_tiles, preferred_element_type=jnp.float32)
        * inv_root
    )
    value_pieces = jnp.einsum(
        "thqj,tqhe->tjhe", attention_lo, grad_tiles, preferred_element_type=jnp.float32
    )
    key_part = jnp.einsum("ts,tjhe->sjhe", slot_onehot, key_pieces, precision=highest)
    key_part = key_part.astype(jnp.bfloat16).reshape(slot_count, L, width)
    value_part = jnp.einsum("ts,tjhe->sjhe", slot_onehot, value_pieces, precision=highest)
    value_part = value_part.astype(jnp.bfloat16).reshape(slot_count, L, width)
    seq_count = lax.axis_size("seq")
    caption_count = seq_count // SPAN
    block_rows = L // seq_count
    features = key_weight.shape[0]
    flat_table = slot_caption.T.reshape(1, slot_count * seq_count)
    selector = (flat_table == jnp.arange(caption_count, dtype=jnp.int32)[:, None]).astype(
        jnp.float32
    )
    payload = jnp.stack([key_part, value_part]).reshape(2, slot_count, seq_count, block_rows, width)
    received = lax.all_to_all(payload, "seq", split_axis=2, concat_axis=2, tiled=True)
    received = received.reshape(2, slot_count * seq_count, block_rows * width).astype(jnp.float32)
    merged = jnp.einsum("cm,kmx->kcx", selector, received, precision=highest)
    merged = merged.reshape(2, caption_count * block_rows, width)
    summed = jnp.dot(merged[0], key_weight.astype(jnp.float32).T, precision=highest)
    summed = summed + jnp.dot(merged[1], value_weight.astype(jnp.float32).T, precision=highest)
    summed = summed.reshape(caption_count, block_rows, features)
    text_grad = lax.psum_scatter(summed, "head", scatter_dimension=2, tiled=True).astype(
        jnp.bfloat16
    )
    return (query_grad, text_grad)


def solution(mesh):
    seq_count, head_devices = mesh.shape["seq"], mesh.shape["head"]
    pairs = seq_count // SPAN <= 2 and seq_count in (4, 8, 16, 32) and head_devices == 4
    placed = (
        P("seq", "head"),
        P("seq", "head"),
        P("seq", None),
        P(),
        P(None, "seq", None, "head"),
        P(None, "head"),
        P(None, "head"),
    )
    return jax.shard_map(
        shards_pairs if pairs else shards_general,
        mesh=mesh,
        in_specs=placed,
        out_specs=(P("seq", "head"), P(None, "seq", "head")),
        check_vma=False,
    )
```

```python
import functools
import math

import jax
import jax.numpy as jnp
from jax import lax
from jax.experimental import pallas as pl
from jax.experimental.pallas import tpu as pltpu
from jax.sharding import PartitionSpec as P

DH = 128
L = 512
TILE = 128
SPAN = 4
F32 = jnp.float32
BF16 = jnp.bfloat16
INV_ROOT = 1.0 / math.sqrt(DH)
KERNEL_LIMIT = 32 * 1024 * 1024
SMALL_LIMIT = 8 * 1024 * 1024


def dot(a, b, contract):
    return lax.dot_general(a, b, ((contract[:1], contract[1:]), ((), ())), preferred_element_type=F32)


def shipping(mask_ref, me, seq_count, tiles):
    odd = jnp.bitwise_and(me, 1)
    ones = mask_ref[1, 0]
    for t in range(1, tiles):
        ones += mask_ref[1, t]
    most = jnp.where(2 * ones > tiles, 1, 0)
    outer = jnp.where(odd == 0, 0, tiles - 1)
    at_end = jnp.where(odd == 0, me == 0, me == seq_count - 1)
    alone = jnp.logical_and(at_end, mask_ref[1 - most, outer] == 1)
    main = jnp.where(alone, 1 - most, most)
    return main, tiles - 1 - outer, jnp.where(alone, tiles // 2, outer)


def backward(key, value, query, grad):
    scores = dot(key, query, (1, 1))
    top = jnp.max(scores, axis=0, keepdims=True)
    exps = jnp.exp((scores - top) * INV_ROOT)
    attention = exps * (1.0 / jnp.sum(exps, axis=0, keepdims=True))
    attention_lo = attention.astype(BF16)
    attention_grad = dot(value, grad, (1, 1))
    row_dot = jnp.sum(attention_lo.astype(F32) * attention_grad, axis=0, keepdims=True)
    score_lo = (attention * (attention_grad - row_dot)).astype(BF16)
    return attention_lo, score_lo


def fetch(pairs, sems):
    copies = [pltpu.make_async_copy(a, b, sems.at[i]) for i, (a, b) in enumerate(pairs)]
    for c in copies:
        c.start()
    return copies


def stage_kernel(seq_count, captions, tiles, mask_hbm, caps_hbm, q_hbm, g_hbm, cache_hbm, *refs):
    y_ref, z_ref, q_ref, g_ref, cache_ref, flags_ref, caption_ref, mask_ref, caps_ref, sems = refs
    me = lax.axis_index("seq")
    copies = fetch(
        [
            (mask_hbm, mask_ref),
            (caps_hbm, caps_ref),
            (q_hbm, q_ref),
            (g_hbm, g_ref),
            (cache_hbm.at[:, :, :, pl.ds(0, DH)], cache_ref),
        ],
        sems,
    )
    for c in copies[:4]:
        c.wait()
    mine, *picked = shipping(mask_ref, me, seq_count, tiles)
    for tile, out in zip(picked, (y_ref, z_ref), strict=True):
        keep = (mask_ref[mine, tile] == 0).astype(F32).astype(BF16)
        at = pl.ds(pl.multiple_of(tile * TILE, TILE), TILE)
        out[0] = q_ref[at, :] * keep
        out[1] = g_ref[at, :] * keep
    lanes = (1, flags_ref.shape[1])
    for t in range(tiles):
        flags_ref[t : t + 1, :] = jnp.full(lanes, mask_ref[1, t].astype(F32), F32)
        flags_ref[tiles + t : tiles + t + 1, :] = jnp.full(lanes, mask_ref[mine, t].astype(F32), F32)
    flags_ref[2 * tiles : 2 * tiles + 1, :] = jnp.full(lanes, mine.astype(F32), F32)
    along = lax.rem(me + jnp.where(jnp.bitwise_and(me, 1) == 0, 2, seq_count - 2), seq_count)
    expects = jnp.int32(0)
    for d in (jnp.bitwise_xor(me, 1), along):
        expects += jnp.where(jnp.logical_and(caps_ref[0, d] < captions, caps_ref[1, d] < captions), 1, 0)
    last = flags_ref.shape[0] - 1
    flags_ref[last : last + 1, :] = jnp.full(lanes, expects.astype(F32), F32)
    caption_ref[...] = jnp.full(caption_ref.shape, caps_ref[mine, me].astype(F32), F32).astype(BF16)
    copies[4].wait()


def pick(flag, pair):
    return pair[0] * (1.0 - flag).astype(BF16) + pair[1] * flag.astype(BF16)


def own_kernel(
    tiles, heads, flags_ref, q_ref, g_ref, first_ref, cache_hbm, wk_hbm, wv_hbm,
    dq_hbm, part_ref, main_ref, weight_ref, cache_buf, dq_buf, sems, out_sems,
):
    pairs = [(cache_hbm.at[:, :, :, pl.ds(h * DH, DH)], cache_buf.at[h - 1]) for h in range(1, heads)]
    width = heads * DH
    pairs += [(wk_hbm, weight_ref.at[:, pl.ds(0, width)]), (wv_hbm, weight_ref.at[:, pl.ds(width, width)])]
    copies = fetch(pairs, sems)
    slots = [flags_ref[t : t + 1, :] for t in range(tiles)]
    keeps = [flags_ref[tiles + t : tiles + t + 1, :] for t in range(tiles)]
    mine = flags_ref[2 * tiles : 2 * tiles + 1, :]
    stores = []
    for h in range(heads):
        cols = slice(h * DH, (h + 1) * DH)
        if h:
            copies[h - 1].wait()
        cache = first_ref if h == 0 else cache_buf.at[h - 1]
        keys, values = (cache[0, 0], cache[0, 1]), (cache[1, 0], cache[1, 1])
        probs, grads, queries, outs = [], [], [], []
        for t in range(tiles):
            rows = slice(t * TILE, (t + 1) * TILE)
            query, grad = q_ref[rows, cols], g_ref[rows, cols]
            attention_lo, score_lo = backward(pick(slots[t], keys), pick(slots[t], values), query, grad)
            probs.append(attention_lo)
            grads.append(score_lo)
            queries.append(query * keeps[t].astype(BF16))
            outs.append(grad * keeps[t].astype(BF16))
        score_grads = jnp.concatenate(grads, axis=1)
        dq = [dot(key.T, score_grads, (1, 0)) * INV_ROOT for key in keys]
        for t in range(tiles):
            rows = slice(t * TILE, (t + 1) * TILE)
            dq_t = jnp.where(slots[t] == 1.0, dq[1][:, rows], dq[0][:, rows])
            dq_buf[h, rows, :] = dq_t.astype(BF16).T
        store = pltpu.make_async_copy(dq_buf.at[h], dq_hbm.at[:, pl.ds(h * DH, DH)], out_sems.at[h])
        store.start()
        stores.append(store)
        part_ref[0, :, cols] = dot(score_grads, jnp.concatenate(queries, axis=0), (1, 0))
        part_ref[1, :, cols] = dot(jnp.concatenate(probs, axis=1), jnp.concatenate(outs, axis=0), (1, 0))
        main_ref[0, :, cols] = pick(mine, keys)
        main_ref[1, :, cols] = pick(mine, values)
    for copy in stores + copies[heads - 1 :]:
        copy.wait()


def gather_parts(heads, blocks, main_ref, part_ref, both_ref, received=None):
    me, core = lax.axis_index("seq"), jnp.bitwise_and(lax.axis_index("head"), 1)
    block_rows, width = L // blocks, heads * DH
    places = []
    for s in range(blocks):
        rel = jnp.bitwise_xor(jnp.bitwise_xor(me, s), core)
        pair, quarter = jnp.right_shift(rel, 1), blocks // 4
        place = jnp.where(pair >= quarter, 2 * (pair - quarter), 2 * (quarter - 1 - pair) + 1)
        place += jnp.bitwise_and(rel, 1) * (blocks // 2)
        places.append(pl.ds(pl.multiple_of(place * block_rows, block_rows), block_rows))
    for h in range(heads):
        cols = slice(h * DH, (h + 1) * DH)
        dk, dv = part_ref[0, :, cols], part_ref[1, :, cols]
        if received is not None:
            y_ref, z_ref = received
            query, grad = y_ref[0, :, cols] + z_ref[0, :, cols], y_ref[1, :, cols] + z_ref[1, :, cols]
            attention_lo, score_lo = backward(main_ref[0, :, cols], main_ref[1, :, cols], query, grad)
            dk, dv = dk + dot(score_lo, query, (1, 0)), dv + dot(attention_lo, grad, (1, 0))
        dk, dv = (dk * INV_ROOT).astype(BF16), dv.astype(BF16)
        for s, rows in enumerate(places):
            both_ref[rows, h * DH : (h + 1) * DH] = dk[s * block_rows : (s + 1) * block_rows]
            both_ref[rows, width + h * DH : width + (h + 1) * DH] = dv[s * block_rows : (s + 1) * block_rows]


def project(both_ref, weight_ref, rel, kept_ref, sent_ref):
    features = kept_ref.shape[2]
    chip = jnp.right_shift(lax.axis_index("head"), 1)
    rows = pl.ds(pl.multiple_of(jnp.bitwise_xor(chip, rel) * features, features), features)
    text = dot(both_ref[...], weight_ref[rows, :], (1, 1)).astype(BF16)
    half = text.shape[0] // 2
    kept_ref[...] = text[:half].reshape(kept_ref.shape)
    sent_ref[...] = text[half:].reshape(sent_ref.shape)


def expects(flags_ref):
    last = flags_ref.shape[0] - 1
    return jnp.max(flags_ref[last : last + 1, :]) > 0.0


def early_text_kernel(heads, blocks, flags_ref, part_ref, weight_ref, both_ref, kept_ref, sent_ref):
    @pl.when(jnp.logical_not(expects(flags_ref)))
    def _():
        gather_parts(heads, blocks, None, part_ref, both_ref)
        project(both_ref, weight_ref, 1, kept_ref, sent_ref)


def first_text_kernel(heads, blocks, flags_ref, z_ref, y_ref, main_ref, part_ref, weight_ref, *refs):
    early, outs = refs[:3], refs[3:]
    come = expects(flags_ref)

    @pl.when(come)
    def _():
        both_ref, kept_ref, sent_ref = outs
        gather_parts(heads, blocks, main_ref, part_ref, both_ref, (y_ref, z_ref))
        project(both_ref, weight_ref, 1, kept_ref, sent_ref)

    @pl.when(jnp.logical_not(come))
    def _():
        for a, b in zip(early, outs, strict=True):
            b[...] = a[...]


def second_text_kernel(both_ref, weight_ref, kept_ref, sent_ref):
    project(both_ref, weight_ref, 0, kept_ref, sent_ref)


def pair_kernel(kept_ref, came_ref, *outs):
    for i, out in enumerate(outs):
        out[...] = (kept_ref[i].astype(F32) + came_ref[i].astype(F32)).astype(BF16)


def cross_kernel(i, kept_ref, came_ref, crossed_ref, caption_ref, out_ref):
    pair = (kept_ref[i].astype(F32) + came_ref[i].astype(F32)).astype(BF16)
    total = (pair.astype(F32) + crossed_ref[...].astype(F32)).astype(BF16)
    height, lanes = out_ref.shape[1:]
    across = total.shape[1] // lanes
    for n in range(out_ref.shape[0] - 1):
        r, c = n // across * height, n % across * lanes
        out_ref[n] = total[r : r + height, c : c + lanes]
    out_ref[out_ref.shape[0] - 1] = caption_ref[...]


def caption_kernel(bases, *refs):
    *blocks, own_ref, kept_ref, sent_ref = refs
    captions, block_rows, width = kept_ref.shape
    _, height, lanes = own_ref.shape
    half = width // lanes
    across = 2 * half
    core = jnp.bitwise_and(lax.axis_index("head"), 1)
    for r in range(block_rows // height):
        totals = [[0.0] * across for _ in range(captions)]
        for base, block in zip(bases, blocks, strict=True):
            caption = block[block.shape[0] - 1].astype(F32)
            if base == 0:
                caption = jnp.where(core == 0, own_ref[own_ref.shape[0] - 1].astype(F32), caption)
            for n in range(across):
                value = block[r * across + n].astype(F32)
                if base == 0:
                    value = jnp.where(core == 0, own_ref[r * across + n].astype(F32), value)
                for c in range(captions):
                    totals[c][n] += jnp.where(caption == c, value, 0.0)
        rows = slice(r * height, (r + 1) * height)
        for c in range(captions):
            for n in range(half):
                cols = slice(n * lanes, (n + 1) * lanes)
                low, high = totals[c][n], totals[c][half + n]
                kept_ref[c, rows, cols] = jnp.where(core == 0, low, high)
                sent_ref[c, rows, cols] = jnp.where(core == 0, high, low).astype(BF16)


def final_kernel(kept_ref, came_ref, out_ref):
    out_ref[...] = (kept_ref[...] + came_ref[...].astype(F32)).astype(BF16)


def swap(array, axis, bit):
    n = lax.axis_size(axis)
    return lax.ppermute(array, axis, [(i, i ^ bit) for i in range(n)])


def send(block, base):
    seq_count, head_devices = lax.axis_size("seq"), lax.axis_size("head")
    pairs = []
    for s in range(seq_count):
        for h in range(head_devices):
            target = s ^ base ^ (h & 1)
            if target != s:
                pairs.append((s * head_devices + h, target * head_devices + h))
    return lax.ppermute(block, ("seq", "head"), pairs)


def call(kernel, name, out_shape, operands, specs, scratch=(), limit=SMALL_LIMIT, hint_us=1.0, out_specs=None):
    vmem = pl.BlockSpec(memory_space=pltpu.VMEM)
    return pl.pallas_call(
        kernel,
        out_shape=out_shape,
        in_specs=specs,
        out_specs=out_specs or jax.tree.map(lambda _: vmem, out_shape),
        scratch_shapes=scratch,
        compiler_params=pltpu.CompilerParams(vmem_limit_bytes=limit),
        cost_estimate=pl.CostEstimate(flops=0, bytes_accessed=int(hint_us * 3_600_000), transcendentals=0),
        name=name,
    )(*operands)


def shards_pairs(queries, out_grad, tile_mask, slot_caption, caption_cache, key_weight, value_weight):
    rows_here, width = queries.shape
    heads = width // DH
    tiles = rows_here // TILE
    slots = tile_mask.shape[1]
    seq_count, head_devices = lax.axis_size("seq"), lax.axis_size("head")
    captions = seq_count // SPAN
    block_rows = L // seq_count
    held_back = [
        pltpu.with_memory_space_constraint(x, pltpu.HBM)
        for x in (tile_mask.T, slot_caption.T, queries, out_grad, caption_cache, key_weight, value_weight)
    ]
    mask_t, caps_t = held_back[:2]
    vmem = pl.BlockSpec(memory_space=pltpu.VMEM)
    hbm = pl.BlockSpec(memory_space=pltpu.HBM)

    def like(*shape, dtype=BF16):
        return jax.ShapeDtypeStruct(shape, dtype)

    to_y, to_z, q_here, g_here, cache_first, flags, caption = call(
        functools.partial(stage_kernel, seq_count, captions, tiles),
        "stage",
        (
            like(2, TILE, width),
            like(2, TILE, width),
            like(rows_here, width),
            like(rows_here, width),
            like(2, slots, L, DH),
            like(8 * (-(-(2 * tiles + 2) // 8)), 128, dtype=F32),
            like(16, 128),
        ),
        held_back[:5],
        [hbm] * 5,
        [
            pltpu.SMEM(mask_t.shape, jnp.int32),
            pltpu.SMEM(caps_t.shape, jnp.int32),
            pltpu.SemaphoreType.DMA((5,)),
        ],
        limit=KERNEL_LIMIT,
    )
    from_y = swap(to_y, "seq", 1)
    from_z = lax.ppermute(to_z, "seq", [(s, (s + (2 if s & 1 else -2)) % seq_count) for s in range(seq_count)])

    query_grad, part, main, weight = call(
        functools.partial(own_kernel, tiles, heads),
        "own_tiles",
        (
            like(rows_here, width),
            like(2, L, width, dtype=F32),
            like(2, L, width),
            like(key_weight.shape[0], 2 * width),
        ),
        (flags, q_here, g_here, cache_first, *held_back[4:]),
        [vmem] * 4 + [hbm] * 3,
        [
            pltpu.VMEM((heads - 1, 2, slots, L, DH), BF16),
            pltpu.VMEM((heads, rows_here, DH), BF16),
            pltpu.SemaphoreType.DMA((heads + 1,)),
            pltpu.SemaphoreType.DMA((heads,)),
        ],
        limit=KERNEL_LIMIT,
        hint_us=5.0,
        out_specs=(hbm, vmem, vmem, vmem),
    )
    half = like(seq_count // 2, block_rows, 2 * width)
    texts = (like(L, 2 * width), half, half)
    early = call(
        functools.partial(early_text_kernel, heads, seq_count),
        "early_text",
        texts,
        (flags, part, weight),
        [vmem] * 3,
        limit=KERNEL_LIMIT,
        hint_us=1.0,
    )
    both, kept, sent = call(
        functools.partial(first_text_kernel, heads, seq_count),
        "first_text",
        texts,
        (flags, from_z, from_y, main, part, weight, *early),
        [vmem] * 9,
        limit=KERNEL_LIMIT,
        hint_us=2.0,
    )
    kept_own, sent_own = call(
        second_text_kernel,
        "second_text",
        (half, half),
        (both, weight),
        [vmem] * 2,
        limit=KERNEL_LIMIT,
        hint_us=1.0,
    )
    block = like(block_rows, 2 * width)
    far = call(pair_kernel, "pair", (block,) * (seq_count // 2), (kept, swap(sent, "head", 1)), [vmem] * 2)
    came_own = swap(sent_own, "head", 1)
    quarter = seq_count // 4
    bases = [2 * b for i in range(quarter) for b in (quarter + i, quarter - 1 - i)]
    arrived, own = [], None
    for i, base in enumerate(bases):
        mine = call(
            functools.partial(cross_kernel, i),
            "cross",
            like(block_rows // 16 * (2 * width // 128) + 1, 16, 128),
            (kept_own, came_own, swap(far[i], "head", 2), caption),
            [vmem] * 4,
        )
        if base == 0:
            own = mine
        arrived.append(send(mine, base))
    kept, sent = call(
        functools.partial(caption_kernel, bases[::-1]),
        "captions",
        (like(captions, block_rows, width, dtype=F32), like(captions, block_rows, width)),
        (*reversed(arrived), own),
        [vmem] * (1 + len(bases)),
    )
    text_grad = call(
        final_kernel, "final", like(captions, block_rows, width), (kept, swap(sent, "head", 1)), [vmem] * 2
    )
    return query_grad, text_grad


def shards_general(queries, out_grad, tile_mask, slot_caption, caption_cache, key_weight, value_weight):
    highest = lax.Precision.HIGHEST
    rows_here, width = queries.shape
    head_count = width // DH
    tile_count = rows_here // TILE
    slot_count = tile_mask.shape[1]
    inv_root = 1.0 / math.sqrt(DH)
    query_tiles = queries.reshape(tile_count, TILE, head_count, DH)
    grad_tiles = out_grad.reshape(tile_count, TILE, head_count, DH)
    slot_onehot = tile_mask.astype(jnp.float32)
    slot_lo = tile_mask.astype(jnp.bfloat16)
    key_rows = jnp.einsum(
        "ts,sjc->tjc", slot_lo, caption_cache[0], preferred_element_type=jnp.float32
    )
    key_rows = key_rows.astype(jnp.bfloat16).reshape(tile_count, L, head_count, DH)
    value_rows = jnp.einsum(
        "ts,sjc->tjc", slot_lo, caption_cache[1], preferred_element_type=jnp.float32
    )
    value_rows = value_rows.astype(jnp.bfloat16).reshape(tile_count, L, head_count, DH)
    scores = (
        jnp.einsum("tqhe,tjhe->thqj", query_tiles, key_rows, preferred_element_type=jnp.float32)
        * inv_root
    )
    row_max = jnp.max(scores, axis=-1, keepdims=True)
    exp_scores = jnp.exp(scores - row_max)
    attention = exp_scores / jnp.sum(exp_scores, axis=-1, keepdims=True)
    attention_lo = attention.astype(jnp.bfloat16)
    context = jnp.einsum(
        "thqj,tjhe->tqhe", attention_lo, value_rows, preferred_element_type=jnp.float32
    )
    row_dot = jnp.transpose(jnp.sum(grad_tiles.astype(jnp.float32) * context, axis=-1), (0, 2, 1))
    attention_grad = jnp.einsum(
        "tqhe,tjhe->thqj", grad_tiles, value_rows, preferred_element_type=jnp.float32
    )
    score_grad = attention * (attention_grad - row_dot[..., None])
    score_lo = score_grad.astype(jnp.bfloat16)
    query_grad = (
        jnp.einsum("thqj,tjhe->tqhe", score_lo, key_rows, preferred_element_type=jnp.float32)
        * inv_root
    )
    query_grad = query_grad.astype(jnp.bfloat16).reshape(rows_here, width)
    key_pieces = (
        jnp.einsum("thqj,tqhe->tjhe", score_lo, query_tiles, preferred_element_type=jnp.float32)
        * inv_root
    )
    value_pieces = jnp.einsum(
        "thqj,tqhe->tjhe", attention_lo, grad_tiles, preferred_element_type=jnp.float32
    )
    key_part = jnp.einsum("ts,tjhe->sjhe", slot_onehot, key_pieces, precision=highest)
    key_part = key_part.astype(jnp.bfloat16).reshape(slot_count, L, width)
    value_part = jnp.einsum("ts,tjhe->sjhe", slot_onehot, value_pieces, precision=highest)
    value_part = value_part.astype(jnp.bfloat16).reshape(slot_count, L, width)
    seq_count = lax.axis_size("seq")
    caption_count = seq_count // SPAN
    block_rows = L // seq_count
    features = key_weight.shape[0]
    flat_table = slot_caption.T.reshape(1, slot_count * seq_count)
    selector = (flat_table == jnp.arange(caption_count, dtype=jnp.int32)[:, None]).astype(
        jnp.float32
    )
    payload = jnp.stack([key_part, value_part]).reshape(2, slot_count, seq_count, block_rows, width)
    received = lax.all_to_all(payload, "seq", split_axis=2, concat_axis=2, tiled=True)
    received = received.reshape(2, slot_count * seq_count, block_rows * width).astype(jnp.float32)
    merged = jnp.einsum("cm,kmx->kcx", selector, received, precision=highest)
    merged = merged.reshape(2, caption_count * block_rows, width)
    summed = jnp.dot(merged[0], key_weight.astype(jnp.float32).T, precision=highest)
    summed = summed + jnp.dot(merged[1], value_weight.astype(jnp.float32).T, precision=highest)
    summed = summed.reshape(caption_count, block_rows, features)
    text_grad = lax.psum_scatter(summed, "head", scatter_dimension=2, tiled=True).astype(
        jnp.bfloat16
    )
    return (query_grad, text_grad)


def solution(mesh):
    seq_count, head_devices = mesh.shape["seq"], mesh.shape["head"]
    pairs = seq_count // SPAN <= 2 and seq_count in (4, 8, 16, 32) and head_devices == 4
    placed = (
        P("seq", "head"),
        P("seq", "head"),
        P("seq", None),
        P(),
        P(None, "seq", None, "head"),
        P(None, "head"),
        P(None, "head"),
    )
    return jax.shard_map(
        shards_pairs if pairs else shards_general,
        mesh=mesh,
        in_specs=placed,
        out_specs=(P("seq", "head"), P(None, "seq", "head")),
        check_vma=False,
    )
```

```python
import functools
import math

import jax
import jax.numpy as jnp
from jax import lax
from jax.experimental import pallas as pl
from jax.experimental.pallas import tpu as pltpu
from jax.sharding import PartitionSpec as P

DH = 128
L = 512
TILE = 128
SPAN = 4
F32 = jnp.float32
BF16 = jnp.bfloat16
INV_ROOT = 1.0 / math.sqrt(DH)
KERNEL_LIMIT = 32 * 1024 * 1024
SMALL_LIMIT = 8 * 1024 * 1024


def dot(a, b, contract):
    return lax.dot_general(a, b, ((contract[:1], contract[1:]), ((), ())), preferred_element_type=F32)


def shipping(mask_ref, me, seq_count, tiles):
    odd = jnp.bitwise_and(me, 1)
    ones = mask_ref[1, 0]
    for t in range(1, tiles):
        ones += mask_ref[1, t]
    most = jnp.where(2 * ones > tiles, 1, 0)
    outer = jnp.where(odd == 0, 0, tiles - 1)
    at_end = jnp.where(odd == 0, me == 0, me == seq_count - 1)
    alone = jnp.logical_and(at_end, mask_ref[1 - most, outer] == 1)
    main = jnp.where(alone, 1 - most, most)
    return main, tiles - 1 - outer, jnp.where(alone, tiles // 2, outer)


def backward(key, value, query, grad):
    scores = dot(key, query, (1, 1))
    top = jnp.max(scores, axis=0, keepdims=True)
    exps = jnp.exp((scores - top) * INV_ROOT)
    attention = exps * (1.0 / jnp.sum(exps, axis=0, keepdims=True))
    attention_lo = attention.astype(BF16)
    attention_grad = dot(value, grad, (1, 1))
    row_dot = jnp.sum(attention_lo.astype(F32) * attention_grad, axis=0, keepdims=True)
    score_lo = (attention * (attention_grad - row_dot)).astype(BF16)
    return attention_lo, score_lo


def fetch(pairs, sems):
    copies = [pltpu.make_async_copy(a, b, sems.at[i]) for i, (a, b) in enumerate(pairs)]
    for c in copies:
        c.start()
    return copies


def stage_kernel(seq_count, captions, tiles, mask_hbm, caps_hbm, q_hbm, g_hbm, cache_hbm, *refs):
    y_ref, z_ref, q_ref, g_ref, cache_ref, flags_ref, caption_ref, mask_ref, caps_ref, sems = refs
    me = lax.axis_index("seq")
    copies = fetch(
        [
            (mask_hbm, mask_ref),
            (caps_hbm, caps_ref),
            (q_hbm, q_ref),
            (g_hbm, g_ref),
            (cache_hbm.at[:, :, :, pl.ds(0, DH)], cache_ref),
        ],
        sems,
    )
    for c in copies[:4]:
        c.wait()
    mine, *picked = shipping(mask_ref, me, seq_count, tiles)
    for tile, out in zip(picked, (y_ref, z_ref), strict=True):
        keep = (mask_ref[mine, tile] == 0).astype(F32).astype(BF16)
        at = pl.ds(pl.multiple_of(tile * TILE, TILE), TILE)
        out[0] = q_ref[at, :] * keep
        out[1] = g_ref[at, :] * keep
    lanes = (1, flags_ref.shape[1])
    for t in range(tiles):
        flags_ref[t : t + 1, :] = jnp.full(lanes, mask_ref[1, t].astype(F32), F32)
        flags_ref[tiles + t : tiles + t + 1, :] = jnp.full(lanes, mask_ref[mine, t].astype(F32), F32)
    flags_ref[2 * tiles : 2 * tiles + 1, :] = jnp.full(lanes, mine.astype(F32), F32)
    along = lax.rem(me + jnp.where(jnp.bitwise_and(me, 1) == 0, 2, seq_count - 2), seq_count)
    expects = jnp.int32(0)
    for d in (jnp.bitwise_xor(me, 1), along):
        expects += jnp.where(jnp.logical_and(caps_ref[0, d] < captions, caps_ref[1, d] < captions), 1, 0)
    last = flags_ref.shape[0] - 1
    flags_ref[last : last + 1, :] = jnp.full(lanes, expects.astype(F32), F32)
    caption_ref[...] = jnp.full(caption_ref.shape, caps_ref[mine, me].astype(F32), F32).astype(BF16)
    copies[4].wait()


def pick(flag, pair):
    return pair[0] * (1.0 - flag).astype(BF16) + pair[1] * flag.astype(BF16)


def own_kernel(
    tiles, heads, flags_ref, q_ref, g_ref, first_ref, cache_hbm, wk_hbm, wv_hbm,
    dq_hbm, part_ref, main_ref, weight_ref, cache_buf, dq_buf, sems, out_sems,
):
    pairs = [(cache_hbm.at[:, :, :, pl.ds(h * DH, DH)], cache_buf.at[h - 1]) for h in range(1, heads)]
    width = heads * DH
    pairs += [(wk_hbm, weight_ref.at[:, pl.ds(0, width)]), (wv_hbm, weight_ref.at[:, pl.ds(width, width)])]
    copies = fetch(pairs, sems)
    mine = flags_ref[2 * tiles : 2 * tiles + 1, :]
    slot = (jnp.max(mine) > 0.0).astype(jnp.int32)
    one_caption = jnp.min(flags_ref[tiles : 2 * tiles, :]) > 0.0
    stores = [
        pltpu.make_async_copy(dq_buf.at[h], dq_hbm.at[:, pl.ds(h * DH, DH)], out_sems.at[h]) for h in range(heads)
    ]

    @pl.when(one_caption)
    def _():
        for h in range(heads):
            cols = slice(h * DH, (h + 1) * DH)
            if h:
                copies[h - 1].wait()
            cache = first_ref if h == 0 else cache_buf.at[h - 1]
            key, value = cache[0, slot], cache[1, slot]
            query, grad = q_ref[:, cols], g_ref[:, cols]
            attention_lo, score_lo = backward(key, value, query, grad)
            dq_buf[h] = (dot(key.T, score_lo, (1, 0)) * INV_ROOT).astype(BF16).T
            stores[h].start()
            part_ref[0, :, cols] = dot(score_lo, query, (1, 0))
            part_ref[1, :, cols] = dot(attention_lo, grad, (1, 0))
            main_ref[0, :, cols] = key
            main_ref[1, :, cols] = value

    @pl.when(jnp.logical_not(one_caption))
    def _():
        slots = [flags_ref[t : t + 1, :] for t in range(tiles)]
        keeps = [flags_ref[tiles + t : tiles + t + 1, :] for t in range(tiles)]
        for h in range(heads):
            cols = slice(h * DH, (h + 1) * DH)
            if h:
                copies[h - 1].wait()
            cache = first_ref if h == 0 else cache_buf.at[h - 1]
            keys, values = (cache[0, 0], cache[0, 1]), (cache[1, 0], cache[1, 1])
            probs, grads, queries, outs = [], [], [], []
            for t in range(tiles):
                rows = slice(t * TILE, (t + 1) * TILE)
                query, grad = q_ref[rows, cols], g_ref[rows, cols]
                attention_lo, score_lo = backward(pick(slots[t], keys), pick(slots[t], values), query, grad)
                probs.append(attention_lo)
                grads.append(score_lo)
                queries.append(query * keeps[t].astype(BF16))
                outs.append(grad * keeps[t].astype(BF16))
            score_grads = jnp.concatenate(grads, axis=1)
            dq = [dot(key.T, score_grads, (1, 0)) * INV_ROOT for key in keys]
            for t in range(tiles):
                rows = slice(t * TILE, (t + 1) * TILE)
                dq_t = jnp.where(slots[t] == 1.0, dq[1][:, rows], dq[0][:, rows])
                dq_buf[h, rows, :] = dq_t.astype(BF16).T
            stores[h].start()
            part_ref[0, :, cols] = dot(score_grads, jnp.concatenate(queries, axis=0), (1, 0))
            part_ref[1, :, cols] = dot(jnp.concatenate(probs, axis=1), jnp.concatenate(outs, axis=0), (1, 0))
            main_ref[0, :, cols] = pick(mine, keys)
            main_ref[1, :, cols] = pick(mine, values)

    for copy in stores + copies[heads - 1 :]:
        copy.wait()


def gather_parts(heads, blocks, main_ref, part_ref, both_ref, received=None):
    me, core = lax.axis_index("seq"), jnp.bitwise_and(lax.axis_index("head"), 1)
    block_rows, width = L // blocks, heads * DH
    places = []
    for s in range(blocks):
        rel = jnp.bitwise_xor(jnp.bitwise_xor(me, s), core)
        place = blocks // 2 - 1 - jnp.right_shift(rel, 1)
        place += jnp.bitwise_and(rel, 1) * (blocks // 2)
        places.append(pl.ds(pl.multiple_of(place * block_rows, block_rows), block_rows))
    for h in range(heads):
        cols = slice(h * DH, (h + 1) * DH)
        dk, dv = part_ref[0, :, cols], part_ref[1, :, cols]
        if received is not None:
            y_ref, z_ref = received
            query, grad = y_ref[0, :, cols] + z_ref[0, :, cols], y_ref[1, :, cols] + z_ref[1, :, cols]
            attention_lo, score_lo = backward(main_ref[0, :, cols], main_ref[1, :, cols], query, grad)
            dk, dv = dk + dot(score_lo, query, (1, 0)), dv + dot(attention_lo, grad, (1, 0))
        dk, dv = (dk * INV_ROOT).astype(BF16), dv.astype(BF16)
        for s, rows in enumerate(places):
            both_ref[rows, h * DH : (h + 1) * DH] = dk[s * block_rows : (s + 1) * block_rows]
            both_ref[rows, width + h * DH : width + (h + 1) * DH] = dv[s * block_rows : (s + 1) * block_rows]


def project(both_ref, weight_ref, rel, kept_ref, sent_ref):
    features = kept_ref.shape[2]
    chip = jnp.right_shift(lax.axis_index("head"), 1)
    rows = pl.ds(pl.multiple_of(jnp.bitwise_xor(chip, rel) * features, features), features)
    text = dot(both_ref[...], weight_ref[rows, :], (1, 1)).astype(BF16)
    half = text.shape[0] // 2
    kept_ref[...] = text[:half].reshape(kept_ref.shape)
    sent_ref[...] = text[half:].reshape(sent_ref.shape)


def expects(flags_ref):
    last = flags_ref.shape[0] - 1
    return jnp.max(flags_ref[last : last + 1, :]) > 0.0


def early_text_kernel(heads, blocks, flags_ref, part_ref, weight_ref, both_ref, kept_ref, sent_ref):
    @pl.when(jnp.logical_not(expects(flags_ref)))
    def _():
        gather_parts(heads, blocks, None, part_ref, both_ref)
        project(both_ref, weight_ref, 1, kept_ref, sent_ref)


def first_text_kernel(heads, blocks, flags_ref, z_ref, y_ref, main_ref, part_ref, weight_ref, *refs):
    early, outs = refs[:3], refs[3:]
    come = expects(flags_ref)

    @pl.when(come)
    def _():
        both_ref, kept_ref, sent_ref = outs
        gather_parts(heads, blocks, main_ref, part_ref, both_ref, (y_ref, z_ref))
        project(both_ref, weight_ref, 1, kept_ref, sent_ref)

    @pl.when(jnp.logical_not(come))
    def _():
        for a, b in zip(early, outs, strict=True):
            b[...] = a[...]


def second_text_kernel(both_ref, weight_ref, kept_ref, sent_ref):
    project(both_ref, weight_ref, 0, kept_ref, sent_ref)


def pair_kernel(kept_ref, came_ref, *outs):
    for i, out in enumerate(outs):
        out[...] = (kept_ref[i].astype(F32) + came_ref[i].astype(F32)).astype(BF16)


def cross_kernel(i, kept_ref, came_ref, crossed_ref, caption_ref, out_ref):
    pair = (kept_ref[i].astype(F32) + came_ref[i].astype(F32)).astype(BF16)
    total = (pair.astype(F32) + crossed_ref[...].astype(F32)).astype(BF16)
    height, lanes = out_ref.shape[1:]
    across = total.shape[1] // lanes
    for n in range(out_ref.shape[0] - 1):
        r, c = n // across * height, n % across * lanes
        out_ref[n] = total[r : r + height, c : c + lanes]
    out_ref[out_ref.shape[0] - 1] = caption_ref[...]


def caption_kernel(bases, *refs):
    *blocks, own_ref, kept_ref, sent_ref = refs
    captions, block_rows, width = kept_ref.shape
    _, height, lanes = own_ref.shape
    half = width // lanes
    across = 2 * half
    core = jnp.bitwise_and(lax.axis_index("head"), 1)
    for r in range(block_rows // height):
        totals = [[0.0] * across for _ in range(captions)]
        for base, block in zip(bases, blocks, strict=True):
            caption = block[block.shape[0] - 1].astype(F32)
            if base == 0:
                caption = jnp.where(core == 0, own_ref[own_ref.shape[0] - 1].astype(F32), caption)
            for n in range(across):
                value = block[r * across + n].astype(F32)
                if base == 0:
                    value = jnp.where(core == 0, own_ref[r * across + n].astype(F32), value)
                for c in range(captions):
                    totals[c][n] += jnp.where(caption == c, value, 0.0)
        rows = slice(r * height, (r + 1) * height)
        for c in range(captions):
            for n in range(half):
                cols = slice(n * lanes, (n + 1) * lanes)
                low, high = totals[c][n], totals[c][half + n]
                kept_ref[c, rows, cols] = jnp.where(core == 0, low, high)
                sent_ref[c, rows, cols] = jnp.where(core == 0, high, low).astype(BF16)


def final_kernel(kept_ref, came_ref, out_ref):
    out_ref[...] = (kept_ref[...] + came_ref[...].astype(F32)).astype(BF16)


def swap(array, axis, bit):
    n = lax.axis_size(axis)
    return lax.ppermute(array, axis, [(i, i ^ bit) for i in range(n)])


def send(block, base):
    seq_count, head_devices = lax.axis_size("seq"), lax.axis_size("head")
    pairs = []
    for s in range(seq_count):
        for h in range(head_devices):
            target = s ^ base ^ (h & 1)
            if target != s:
                pairs.append((s * head_devices + h, target * head_devices + h))
    return lax.ppermute(block, ("seq", "head"), pairs)


def call(kernel, name, out_shape, operands, specs, scratch=(), limit=SMALL_LIMIT, hint_us=1.0, out_specs=None):
    vmem = pl.BlockSpec(memory_space=pltpu.VMEM)
    return pl.pallas_call(
        kernel,
        out_shape=out_shape,
        in_specs=specs,
        out_specs=out_specs or jax.tree.map(lambda _: vmem, out_shape),
        scratch_shapes=scratch,
        compiler_params=pltpu.CompilerParams(vmem_limit_bytes=limit),
        cost_estimate=pl.CostEstimate(flops=0, bytes_accessed=int(hint_us * 3_600_000), transcendentals=0),
        name=name,
    )(*operands)


def shards_pairs(queries, out_grad, tile_mask, slot_caption, caption_cache, key_weight, value_weight):
    rows_here, width = queries.shape
    heads = width // DH
    tiles = rows_here // TILE
    slots = tile_mask.shape[1]
    seq_count, head_devices = lax.axis_size("seq"), lax.axis_size("head")
    captions = seq_count // SPAN
    block_rows = L // seq_count
    held_back = [
        pltpu.with_memory_space_constraint(x, pltpu.HBM)
        for x in (tile_mask.T, slot_caption.T, queries, out_grad, caption_cache, key_weight, value_weight)
    ]
    mask_t, caps_t = held_back[:2]
    vmem = pl.BlockSpec(memory_space=pltpu.VMEM)
    hbm = pl.BlockSpec(memory_space=pltpu.HBM)

    def like(*shape, dtype=BF16):
        return jax.ShapeDtypeStruct(shape, dtype)

    to_y, to_z, q_here, g_here, cache_first, flags, caption = call(
        functools.partial(stage_kernel, seq_count, captions, tiles),
        "stage",
        (
            like(2, TILE, width),
            like(2, TILE, width),
            like(rows_here, width),
            like(rows_here, width),
            like(2, slots, L, DH),
            like(8 * (-(-(2 * tiles + 2) // 8)), 128, dtype=F32),
            like(16, 128),
        ),
        held_back[:5],
        [hbm] * 5,
        [
            pltpu.SMEM(mask_t.shape, jnp.int32),
            pltpu.SMEM(caps_t.shape, jnp.int32),
            pltpu.SemaphoreType.DMA((5,)),
        ],
        limit=KERNEL_LIMIT,
    )
    from_y = swap(to_y, "seq", 1)
    from_z = lax.ppermute(to_z, "seq", [(s, (s + (2 if s & 1 else -2)) % seq_count) for s in range(seq_count)])

    query_grad, part, main, weight = call(
        functools.partial(own_kernel, tiles, heads),
        "own_tiles",
        (
            like(rows_here, width),
            like(2, L, width, dtype=F32),
            like(2, L, width),
            like(key_weight.shape[0], 2 * width),
        ),
        (flags, q_here, g_here, cache_first, *held_back[4:]),
        [vmem] * 4 + [hbm] * 3,
        [
            pltpu.VMEM((heads - 1, 2, slots, L, DH), BF16),
            pltpu.VMEM((heads, rows_here, DH), BF16),
            pltpu.SemaphoreType.DMA((heads + 1,)),
            pltpu.SemaphoreType.DMA((heads,)),
        ],
        limit=KERNEL_LIMIT,
        hint_us=5.0,
        out_specs=(hbm, vmem, vmem, vmem),
    )
    half = like(seq_count // 2, block_rows, 2 * width)
    texts = (like(L, 2 * width), half, half)
    early = call(
        functools.partial(early_text_kernel, heads, seq_count),
        "early_text",
        texts,
        (flags, part, weight),
        [vmem] * 3,
        limit=KERNEL_LIMIT,
        hint_us=1.0,
    )
    both, kept, sent = call(
        functools.partial(first_text_kernel, heads, seq_count),
        "first_text",
        texts,
        (flags, from_z, from_y, main, part, weight, *early),
        [vmem] * 9,
        limit=KERNEL_LIMIT,
        hint_us=2.0,
    )
    kept_own, sent_own = call(
        second_text_kernel,
        "second_text",
        (half, half),
        (both, weight),
        [vmem] * 2,
        limit=KERNEL_LIMIT,
        hint_us=1.0,
    )
    block = like(block_rows, 2 * width)
    far = call(pair_kernel, "pair", (block,) * (seq_count // 2), (kept, swap(sent, "head", 1)), [vmem] * 2)
    came_own = swap(sent_own, "head", 1)
    bases = [2 * (seq_count // 2 - 1 - i) for i in range(seq_count // 2)]
    arrived, own = [], None
    for i, base in enumerate(bases):
        mine = call(
            functools.partial(cross_kernel, i),
            "cross",
            like(block_rows // 16 * (2 * width // 128) + 1, 16, 128),
            (kept_own, came_own, swap(far[i], "head", 2), caption),
            [vmem] * 4,
        )
        if base == 0:
            own = mine
        arrived.append(send(mine, base))
    kept, sent = call(
        functools.partial(caption_kernel, bases[::-1]),
        "captions",
        (like(captions, block_rows, width, dtype=F32), like(captions, block_rows, width)),
        (*reversed(arrived), own),
        [vmem] * (1 + len(bases)),
    )
    text_grad = call(
        final_kernel, "final", like(captions, block_rows, width), (kept, swap(sent, "head", 1)), [vmem] * 2
    )
    return query_grad, text_grad


def shards_general(queries, out_grad, tile_mask, slot_caption, caption_cache, key_weight, value_weight):
    highest = lax.Precision.HIGHEST
    rows_here, width = queries.shape
    head_count = width // DH
    tile_count = rows_here // TILE
    slot_count = tile_mask.shape[1]
    inv_root = 1.0 / math.sqrt(DH)
    query_tiles = queries.reshape(tile_count, TILE, head_count, DH)
    grad_tiles = out_grad.reshape(tile_count, TILE, head_count, DH)
    slot_onehot = tile_mask.astype(jnp.float32)
    slot_lo = tile_mask.astype(jnp.bfloat16)
    key_rows = jnp.einsum(
        "ts,sjc->tjc", slot_lo, caption_cache[0], preferred_element_type=jnp.float32
    )
    key_rows = key_rows.astype(jnp.bfloat16).reshape(tile_count, L, head_count, DH)
    value_rows = jnp.einsum(
        "ts,sjc->tjc", slot_lo, caption_cache[1], preferred_element_type=jnp.float32
    )
    value_rows = value_rows.astype(jnp.bfloat16).reshape(tile_count, L, head_count, DH)
    scores = (
        jnp.einsum("tqhe,tjhe->thqj", query_tiles, key_rows, preferred_element_type=jnp.float32)
        * inv_root
    )
    row_max = jnp.max(scores, axis=-1, keepdims=True)
    exp_scores = jnp.exp(scores - row_max)
    attention = exp_scores / jnp.sum(exp_scores, axis=-1, keepdims=True)
    attention_lo = attention.astype(jnp.bfloat16)
    context = jnp.einsum(
        "thqj,tjhe->tqhe", attention_lo, value_rows, preferred_element_type=jnp.float32
    )
    row_dot = jnp.transpose(jnp.sum(grad_tiles.astype(jnp.float32) * context, axis=-1), (0, 2, 1))
    attention_grad = jnp.einsum(
        "tqhe,tjhe->thqj", grad_tiles, value_rows, preferred_element_type=jnp.float32
    )
    score_grad = attention * (attention_grad - row_dot[..., None])
    score_lo = score_grad.astype(jnp.bfloat16)
    query_grad = (
        jnp.einsum("thqj,tjhe->tqhe", score_lo, key_rows, preferred_element_type=jnp.float32)
        * inv_root
    )
    query_grad = query_grad.astype(jnp.bfloat16).reshape(rows_here, width)
    key_pieces = (
        jnp.einsum("thqj,tqhe->tjhe", score_lo, query_tiles, preferred_element_type=jnp.float32)
        * inv_root
    )
    value_pieces = jnp.einsum(
        "thqj,tqhe->tjhe", attention_lo, grad_tiles, preferred_element_type=jnp.float32
    )
    key_part = jnp.einsum("ts,tjhe->sjhe", slot_onehot, key_pieces, precision=highest)
    key_part = key_part.astype(jnp.bfloat16).reshape(slot_count, L, width)
    value_part = jnp.einsum("ts,tjhe->sjhe", slot_onehot, value_pieces, precision=highest)
    value_part = value_part.astype(jnp.bfloat16).reshape(slot_count, L, width)
    seq_count = lax.axis_size("seq")
    caption_count = seq_count // SPAN
    block_rows = L // seq_count
    features = key_weight.shape[0]
    flat_table = slot_caption.T.reshape(1, slot_count * seq_count)
    selector = (flat_table == jnp.arange(caption_count, dtype=jnp.int32)[:, None]).astype(
        jnp.float32
    )
    payload = jnp.stack([key_part, value_part]).reshape(2, slot_count, seq_count, block_rows, width)
    received = lax.all_to_all(payload, "seq", split_axis=2, concat_axis=2, tiled=True)
    received = received.reshape(2, slot_count * seq_count, block_rows * width).astype(jnp.float32)
    merged = jnp.einsum("cm,kmx->kcx", selector, received, precision=highest)
    merged = merged.reshape(2, caption_count * block_rows, width)
    summed = jnp.dot(merged[0], key_weight.astype(jnp.float32).T, precision=highest)
    summed = summed + jnp.dot(merged[1], value_weight.astype(jnp.float32).T, precision=highest)
    summed = summed.reshape(caption_count, block_rows, features)
    text_grad = lax.psum_scatter(summed, "head", scatter_dimension=2, tiled=True).astype(
        jnp.bfloat16
    )
    return (query_grad, text_grad)


def solution(mesh):
    seq_count, head_devices = mesh.shape["seq"], mesh.shape["head"]
    pairs = seq_count // SPAN <= 2 and seq_count in (4, 8, 16, 32) and head_devices == 4
    placed = (
        P("seq", "head"),
        P("seq", "head"),
        P("seq", None),
        P(),
        P(None, "seq", None, "head"),
        P(None, "head"),
        P(None, "head"),
    )
    return jax.shard_map(
        shards_pairs if pairs else shards_general,
        mesh=mesh,
        in_specs=placed,
        out_specs=(P("seq", "head"), P(None, "seq", "head")),
        check_vma=False,
    )
```

```python
import functools
import math

import jax
import jax.numpy as jnp
from jax import lax
from jax.experimental import pallas as pl
from jax.experimental.pallas import tpu as pltpu
from jax.sharding import PartitionSpec as P

DH = 128
L = 512
TILE = 128
SPAN = 4
F32 = jnp.float32
BF16 = jnp.bfloat16
INV_ROOT = 1.0 / math.sqrt(DH)
KERNEL_LIMIT = 32 * 1024 * 1024
SMALL_LIMIT = 8 * 1024 * 1024


def dot(a, b, contract):
    return lax.dot_general(a, b, ((contract[:1], contract[1:]), ((), ())), preferred_element_type=F32)


def shipping(mask_ref, me, seq_count, tiles):
    odd = jnp.bitwise_and(me, 1)
    ones = mask_ref[1, 0]
    for t in range(1, tiles):
        ones += mask_ref[1, t]
    most = jnp.where(2 * ones > tiles, 1, 0)
    outer = jnp.where(odd == 0, 0, tiles - 1)
    at_end = jnp.where(odd == 0, me == 0, me == seq_count - 1)
    alone = jnp.logical_and(at_end, mask_ref[1 - most, outer] == 1)
    main = jnp.where(alone, 1 - most, most)
    return main, tiles - 1 - outer, jnp.where(alone, tiles // 2, outer)


def backward(key, value, query, grad):
    scores = dot(key, query, (1, 1))
    top = jnp.max(scores, axis=0, keepdims=True)
    exps = jnp.exp((scores - top) * INV_ROOT)
    attention = exps * (1.0 / jnp.sum(exps, axis=0, keepdims=True))
    attention_lo = attention.astype(BF16)
    attention_grad = dot(value, grad, (1, 1))
    row_dot = jnp.sum(attention_lo.astype(F32) * attention_grad, axis=0, keepdims=True)
    score_lo = (attention * (attention_grad - row_dot)).astype(BF16)
    return attention_lo, score_lo


def fetch(pairs, sems):
    copies = [pltpu.make_async_copy(a, b, sems.at[i]) for i, (a, b) in enumerate(pairs)]
    for c in copies:
        c.start()
    return copies


def stage_kernel(seq_count, captions, tiles, mask_hbm, caps_hbm, q_hbm, g_hbm, cache_hbm, *refs):
    y_ref, z_ref, q_ref, g_ref, cache_ref, flags_ref, caption_ref, mask_ref, caps_ref, sems = refs
    me = lax.axis_index("seq")
    copies = fetch(
        [
            (mask_hbm, mask_ref),
            (caps_hbm, caps_ref),
            (q_hbm, q_ref),
            (g_hbm, g_ref),
            (cache_hbm.at[:, :, :, pl.ds(0, DH)], cache_ref),
        ],
        sems,
    )
    for c in copies[:4]:
        c.wait()
    mine, *picked = shipping(mask_ref, me, seq_count, tiles)
    for tile, out in zip(picked, (y_ref, z_ref), strict=True):
        keep = (mask_ref[mine, tile] == 0).astype(F32).astype(BF16)
        at = pl.ds(pl.multiple_of(tile * TILE, TILE), TILE)
        out[0] = q_ref[at, :] * keep
        out[1] = g_ref[at, :] * keep
    lanes = (1, flags_ref.shape[1])
    for t in range(tiles):
        flags_ref[t : t + 1, :] = jnp.full(lanes, mask_ref[1, t].astype(F32), F32)
        flags_ref[tiles + t : tiles + t + 1, :] = jnp.full(lanes, mask_ref[mine, t].astype(F32), F32)
    flags_ref[2 * tiles : 2 * tiles + 1, :] = jnp.full(lanes, mine.astype(F32), F32)
    along = lax.rem(me + jnp.where(jnp.bitwise_and(me, 1) == 0, 2, seq_count - 2), seq_count)
    expects = jnp.int32(0)
    for d in (jnp.bitwise_xor(me, 1), along):
        expects += jnp.where(jnp.logical_and(caps_ref[0, d] < captions, caps_ref[1, d] < captions), 1, 0)
    last = flags_ref.shape[0] - 1
    flags_ref[last : last + 1, :] = jnp.full(lanes, expects.astype(F32), F32)
    caption_ref[...] = jnp.full(caption_ref.shape, caps_ref[mine, me].astype(F32), F32).astype(BF16)
    copies[4].wait()


def pick(flag, pair):
    return pair[0] * (1.0 - flag).astype(BF16) + pair[1] * flag.astype(BF16)


def own_kernel(
    tiles, heads, flags_ref, q_ref, g_ref, first_ref, cache_hbm, wk_hbm, wv_hbm,
    dq_hbm, part_ref, main_ref, weight_ref, cache_buf, dq_buf, sems, out_sems,
):
    pairs = [(cache_hbm.at[:, :, :, pl.ds(h * DH, DH)], cache_buf.at[h - 1]) for h in range(1, heads)]
    width = heads * DH
    pairs += [(wk_hbm, weight_ref.at[:, pl.ds(0, width)]), (wv_hbm, weight_ref.at[:, pl.ds(width, width)])]
    copies = fetch(pairs, sems)
    mine = flags_ref[2 * tiles : 2 * tiles + 1, :]
    slot = (jnp.max(mine) > 0.0).astype(jnp.int32)
    one_caption = jnp.min(flags_ref[tiles : 2 * tiles, :]) > 0.0
    stores = [
        pltpu.make_async_copy(dq_buf.at[h], dq_hbm.at[:, pl.ds(h * DH, DH)], out_sems.at[h]) for h in range(heads)
    ]

    @pl.when(one_caption)
    def _():
        for h in range(heads):
            cols = slice(h * DH, (h + 1) * DH)
            if h:
                copies[h - 1].wait()
            cache = first_ref if h == 0 else cache_buf.at[h - 1]
            key, value = cache[0, slot], cache[1, slot]
            query, grad = q_ref[:, cols], g_ref[:, cols]
            attention_lo, score_lo = backward(key, value, query, grad)
            dq_buf[h] = (dot(key.T, score_lo, (1, 0)) * INV_ROOT).astype(BF16).T
            stores[h].start()
            part_ref[0, :, cols] = dot(score_lo, query, (1, 0))
            part_ref[1, :, cols] = dot(attention_lo, grad, (1, 0))
            main_ref[0, :, cols] = key
            main_ref[1, :, cols] = value

    @pl.when(jnp.logical_not(one_caption))
    def _():
        slots = [flags_ref[t : t + 1, :] for t in range(tiles)]
        keeps = [flags_ref[tiles + t : tiles + t + 1, :] for t in range(tiles)]
        for h in range(heads):
            cols = slice(h * DH, (h + 1) * DH)
            if h:
                copies[h - 1].wait()
            cache = first_ref if h == 0 else cache_buf.at[h - 1]
            keys, values = (cache[0, 0], cache[0, 1]), (cache[1, 0], cache[1, 1])
            probs, grads, queries, outs = [], [], [], []
            for t in range(tiles):
                rows = slice(t * TILE, (t + 1) * TILE)
                query, grad = q_ref[rows, cols], g_ref[rows, cols]
                attention_lo, score_lo = backward(pick(slots[t], keys), pick(slots[t], values), query, grad)
                probs.append(attention_lo)
                grads.append(score_lo)
                queries.append(query * keeps[t].astype(BF16))
                outs.append(grad * keeps[t].astype(BF16))
            score_grads = jnp.concatenate(grads, axis=1)
            dq = [dot(key.T, score_grads, (1, 0)) * INV_ROOT for key in keys]
            for t in range(tiles):
                rows = slice(t * TILE, (t + 1) * TILE)
                dq_t = jnp.where(slots[t] == 1.0, dq[1][:, rows], dq[0][:, rows])
                dq_buf[h, rows, :] = dq_t.astype(BF16).T
            stores[h].start()
            part_ref[0, :, cols] = dot(score_grads, jnp.concatenate(queries, axis=0), (1, 0))
            part_ref[1, :, cols] = dot(jnp.concatenate(probs, axis=1), jnp.concatenate(outs, axis=0), (1, 0))
            main_ref[0, :, cols] = pick(mine, keys)
            main_ref[1, :, cols] = pick(mine, values)

    for copy in stores + copies[heads - 1 :]:
        copy.wait()


def gather_parts(heads, blocks, main_ref, part_ref, both_ref, received=None):
    me, core = lax.axis_index("seq"), jnp.bitwise_and(lax.axis_index("head"), 1)
    block_rows, width = L // blocks, heads * DH
    places = []
    for s in range(blocks):
        rel = jnp.bitwise_xor(jnp.bitwise_xor(me, s), core)
        place = blocks // 2 - 1 - jnp.right_shift(rel, 1)
        place += jnp.bitwise_and(rel, 1) * (blocks // 2)
        places.append(pl.ds(pl.multiple_of(place * block_rows, block_rows), block_rows))
    for h in range(heads):
        cols = slice(h * DH, (h + 1) * DH)
        dk, dv = part_ref[0, :, cols], part_ref[1, :, cols]
        if received is not None:
            y_ref, z_ref = received
            query, grad = y_ref[0, :, cols] + z_ref[0, :, cols], y_ref[1, :, cols] + z_ref[1, :, cols]
            attention_lo, score_lo = backward(main_ref[0, :, cols], main_ref[1, :, cols], query, grad)
            dk, dv = dk + dot(score_lo, query, (1, 0)), dv + dot(attention_lo, grad, (1, 0))
        dk, dv = (dk * INV_ROOT).astype(BF16), dv.astype(BF16)
        for s, rows in enumerate(places):
            both_ref[rows, h * DH : (h + 1) * DH] = dk[s * block_rows : (s + 1) * block_rows]
            both_ref[rows, width + h * DH : width + (h + 1) * DH] = dv[s * block_rows : (s + 1) * block_rows]


def project(both, weight_ref, rel, out_ref):
    features = out_ref.shape[2]
    chip = jnp.right_shift(lax.axis_index("head"), 1)
    rows = pl.ds(pl.multiple_of(jnp.bitwise_xor(chip, rel) * features, features), features)
    out_ref[...] = dot(both, weight_ref[rows, :], (1, 1)).astype(BF16).reshape(out_ref.shape)


def expects(flags_ref):
    last = flags_ref.shape[0] - 1
    return jnp.max(flags_ref[last : last + 1, :]) > 0.0


def early_text_kernel(heads, blocks, flags_ref, part_ref, weight_ref, both_ref, sent_ref):
    @pl.when(jnp.logical_not(expects(flags_ref)))
    def _():
        gather_parts(heads, blocks, None, part_ref, both_ref)
        project(both_ref[L // 2 :, :], weight_ref, 1, sent_ref)


def first_text_kernel(heads, blocks, flags_ref, z_ref, y_ref, main_ref, part_ref, weight_ref, *refs):
    early, outs = refs[:2], refs[2:]
    come = expects(flags_ref)

    @pl.when(come)
    def _():
        both_ref, sent_ref = outs
        gather_parts(heads, blocks, main_ref, part_ref, both_ref, (y_ref, z_ref))
        project(both_ref[L // 2 :, :], weight_ref, 1, sent_ref)

    @pl.when(jnp.logical_not(come))
    def _():
        for a, b in zip(early, outs, strict=True):
            b[...] = a[...]


def second_text_kernel(both_ref, weight_ref, sent_own_ref, kept_ref, kept_own_ref):
    project(both_ref[L // 2 :, :], weight_ref, 0, sent_own_ref)
    project(both_ref[: L // 2, :], weight_ref, 1, kept_ref)
    project(both_ref[: L // 2, :], weight_ref, 0, kept_own_ref)


def pair_kernel(kept_ref, came_ref, *outs):
    for i, out in enumerate(outs):
        out[...] = (kept_ref[i].astype(F32) + came_ref[i].astype(F32)).astype(BF16)


def cross_kernel(i, kept_ref, came_ref, crossed_ref, caption_ref, out_ref):
    pair = (kept_ref[i].astype(F32) + came_ref[i].astype(F32)).astype(BF16)
    total = (pair.astype(F32) + crossed_ref[...].astype(F32)).astype(BF16)
    height, lanes = out_ref.shape[1:]
    across = total.shape[1] // lanes
    for n in range(out_ref.shape[0] - 1):
        r, c = n // across * height, n % across * lanes
        out_ref[n] = total[r : r + height, c : c + lanes]
    out_ref[out_ref.shape[0] - 1] = caption_ref[...]


def caption_kernel(bases, *refs):
    *blocks, own_ref, kept_ref, sent_ref = refs
    captions, block_rows, width = kept_ref.shape
    _, height, lanes = own_ref.shape
    half = width // lanes
    across = 2 * half
    core = jnp.bitwise_and(lax.axis_index("head"), 1)
    for r in range(block_rows // height):
        totals = [[0.0] * across for _ in range(captions)]
        for base, block in zip(bases, blocks, strict=True):
            caption = block[block.shape[0] - 1].astype(F32)
            if base == 0:
                caption = jnp.where(core == 0, own_ref[own_ref.shape[0] - 1].astype(F32), caption)
            for n in range(across):
                value = block[r * across + n].astype(F32)
                if base == 0:
                    value = jnp.where(core == 0, own_ref[r * across + n].astype(F32), value)
                for c in range(captions):
                    totals[c][n] += jnp.where(caption == c, value, 0.0)
        rows = slice(r * height, (r + 1) * height)
        for c in range(captions):
            for n in range(half):
                cols = slice(n * lanes, (n + 1) * lanes)
                low, high = totals[c][n], totals[c][half + n]
                kept_ref[c, rows, cols] = jnp.where(core == 0, low, high)
                sent_ref[c, rows, cols] = jnp.where(core == 0, high, low).astype(BF16)


def final_kernel(kept_ref, came_ref, out_ref):
    out_ref[...] = (kept_ref[...] + came_ref[...].astype(F32)).astype(BF16)


def swap(array, axis, bit):
    n = lax.axis_size(axis)
    return lax.ppermute(array, axis, [(i, i ^ bit) for i in range(n)])


def send(block, base):
    seq_count, head_devices = lax.axis_size("seq"), lax.axis_size("head")
    pairs = []
    for s in range(seq_count):
        for h in range(head_devices):
            target = s ^ base ^ (h & 1)
            if target != s:
                pairs.append((s * head_devices + h, target * head_devices + h))
    return lax.ppermute(block, ("seq", "head"), pairs)


def call(kernel, name, out_shape, operands, specs, scratch=(), limit=SMALL_LIMIT, hint_us=1.0, out_specs=None):
    vmem = pl.BlockSpec(memory_space=pltpu.VMEM)
    return pl.pallas_call(
        kernel,
        out_shape=out_shape,
        in_specs=specs,
        out_specs=out_specs or jax.tree.map(lambda _: vmem, out_shape),
        scratch_shapes=scratch,
        compiler_params=pltpu.CompilerParams(vmem_limit_bytes=limit),
        cost_estimate=pl.CostEstimate(flops=0, bytes_accessed=int(hint_us * 3_600_000), transcendentals=0),
        name=name,
    )(*operands)


def shards_pairs(queries, out_grad, tile_mask, slot_caption, caption_cache, key_weight, value_weight):
    rows_here, width = queries.shape
    heads = width // DH
    tiles = rows_here // TILE
    slots = tile_mask.shape[1]
    seq_count, head_devices = lax.axis_size("seq"), lax.axis_size("head")
    captions = seq_count // SPAN
    block_rows = L // seq_count
    held_back = [
        pltpu.with_memory_space_constraint(x, pltpu.HBM)
        for x in (tile_mask.T, slot_caption.T, queries, out_grad, caption_cache, key_weight, value_weight)
    ]
    mask_t, caps_t = held_back[:2]
    vmem = pl.BlockSpec(memory_space=pltpu.VMEM)
    hbm = pl.BlockSpec(memory_space=pltpu.HBM)

    def like(*shape, dtype=BF16):
        return jax.ShapeDtypeStruct(shape, dtype)

    to_y, to_z, q_here, g_here, cache_first, flags, caption = call(
        functools.partial(stage_kernel, seq_count, captions, tiles),
        "stage",
        (
            like(2, TILE, width),
            like(2, TILE, width),
            like(rows_here, width),
            like(rows_here, width),
            like(2, slots, L, DH),
            like(8 * (-(-(2 * tiles + 2) // 8)), 128, dtype=F32),
            like(16, 128),
        ),
        held_back[:5],
        [hbm] * 5,
        [
            pltpu.SMEM(mask_t.shape, jnp.int32),
            pltpu.SMEM(caps_t.shape, jnp.int32),
            pltpu.SemaphoreType.DMA((5,)),
        ],
        limit=KERNEL_LIMIT,
    )
    from_y = swap(to_y, "seq", 1)
    from_z = lax.ppermute(to_z, "seq", [(s, (s + (2 if s & 1 else -2)) % seq_count) for s in range(seq_count)])

    query_grad, part, main, weight = call(
        functools.partial(own_kernel, tiles, heads),
        "own_tiles",
        (
            like(rows_here, width),
            like(2, L, width, dtype=F32),
            like(2, L, width),
            like(key_weight.shape[0], 2 * width),
        ),
        (flags, q_here, g_here, cache_first, *held_back[4:]),
        [vmem] * 4 + [hbm] * 3,
        [
            pltpu.VMEM((heads - 1, 2, slots, L, DH), BF16),
            pltpu.VMEM((heads, rows_here, DH), BF16),
            pltpu.SemaphoreType.DMA((heads + 1,)),
            pltpu.SemaphoreType.DMA((heads,)),
        ],
        limit=KERNEL_LIMIT,
        hint_us=5.0,
        out_specs=(hbm, vmem, vmem, vmem),
    )
    half = like(seq_count // 2, block_rows, 2 * width)
    texts = (like(L, 2 * width), half)
    early = call(
        functools.partial(early_text_kernel, heads, seq_count),
        "early_text",
        texts,
        (flags, part, weight),
        [vmem] * 3,
        limit=KERNEL_LIMIT,
        hint_us=1.0,
    )
    both, sent = call(
        functools.partial(first_text_kernel, heads, seq_count),
        "first_text",
        texts,
        (flags, from_z, from_y, main, part, weight, *early),
        [vmem] * 8,
        limit=KERNEL_LIMIT,
        hint_us=2.0,
    )
    sent_own, kept, kept_own = call(
        second_text_kernel,
        "second_text",
        (half, half, half),
        (both, weight),
        [vmem] * 2,
        limit=KERNEL_LIMIT,
        hint_us=1.0,
    )
    block = like(block_rows, 2 * width)
    far = call(pair_kernel, "pair", (block,) * (seq_count // 2), (kept, swap(sent, "head", 1)), [vmem] * 2)
    came_own = swap(sent_own, "head", 1)
    bases = [2 * (seq_count // 2 - 1 - i) for i in range(seq_count // 2)]
    arrived, own = [], None
    for i, base in enumerate(bases):
        mine = call(
            functools.partial(cross_kernel, i),
            "cross",
            like(block_rows // 16 * (2 * width // 128) + 1, 16, 128),
            (kept_own, came_own, swap(far[i], "head", 2), caption),
            [vmem] * 4,
        )
        if base == 0:
            own = mine
        arrived.append(send(mine, base))
    kept, sent = call(
        functools.partial(caption_kernel, bases[::-1]),
        "captions",
        (like(captions, block_rows, width, dtype=F32), like(captions, block_rows, width)),
        (*reversed(arrived), own),
        [vmem] * (1 + len(bases)),
    )
    text_grad = call(
        final_kernel, "final", like(captions, block_rows, width), (kept, swap(sent, "head", 1)), [vmem] * 2
    )
    return query_grad, text_grad


def shards_general(queries, out_grad, tile_mask, slot_caption, caption_cache, key_weight, value_weight):
    highest = lax.Precision.HIGHEST
    rows_here, width = queries.shape
    head_count = width // DH
    tile_count = rows_here // TILE
    slot_count = tile_mask.shape[1]
    inv_root = 1.0 / math.sqrt(DH)
    query_tiles = queries.reshape(tile_count, TILE, head_count, DH)
    grad_tiles = out_grad.reshape(tile_count, TILE, head_count, DH)
    slot_onehot = tile_mask.astype(jnp.float32)
    slot_lo = tile_mask.astype(jnp.bfloat16)
    key_rows = jnp.einsum(
        "ts,sjc->tjc", slot_lo, caption_cache[0], preferred_element_type=jnp.float32
    )
    key_rows = key_rows.astype(jnp.bfloat16).reshape(tile_count, L, head_count, DH)
    value_rows = jnp.einsum(
        "ts,sjc->tjc", slot_lo, caption_cache[1], preferred_element_type=jnp.float32
    )
    value_rows = value_rows.astype(jnp.bfloat16).reshape(tile_count, L, head_count, DH)
    scores = (
        jnp.einsum("tqhe,tjhe->thqj", query_tiles, key_rows, preferred_element_type=jnp.float32)
        * inv_root
    )
    row_max = jnp.max(scores, axis=-1, keepdims=True)
    exp_scores = jnp.exp(scores - row_max)
    attention = exp_scores / jnp.sum(exp_scores, axis=-1, keepdims=True)
    attention_lo = attention.astype(jnp.bfloat16)
    context = jnp.einsum(
        "thqj,tjhe->tqhe", attention_lo, value_rows, preferred_element_type=jnp.float32
    )
    row_dot = jnp.transpose(jnp.sum(grad_tiles.astype(jnp.float32) * context, axis=-1), (0, 2, 1))
    attention_grad = jnp.einsum(
        "tqhe,tjhe->thqj", grad_tiles, value_rows, preferred_element_type=jnp.float32
    )
    score_grad = attention * (attention_grad - row_dot[..., None])
    score_lo = score_grad.astype(jnp.bfloat16)
    query_grad = (
        jnp.einsum("thqj,tjhe->tqhe", score_lo, key_rows, preferred_element_type=jnp.float32)
        * inv_root
    )
    query_grad = query_grad.astype(jnp.bfloat16).reshape(rows_here, width)
    key_pieces = (
        jnp.einsum("thqj,tqhe->tjhe", score_lo, query_tiles, preferred_element_type=jnp.float32)
        * inv_root
    )
    value_pieces = jnp.einsum(
        "thqj,tqhe->tjhe", attention_lo, grad_tiles, preferred_element_type=jnp.float32
    )
    key_part = jnp.einsum("ts,tjhe->sjhe", slot_onehot, key_pieces, precision=highest)
    key_part = key_part.astype(jnp.bfloat16).reshape(slot_count, L, width)
    value_part = jnp.einsum("ts,tjhe->sjhe", slot_onehot, value_pieces, precision=highest)
    value_part = value_part.astype(jnp.bfloat16).reshape(slot_count, L, width)
    seq_count = lax.axis_size("seq")
    caption_count = seq_count // SPAN
    block_rows = L // seq_count
    features = key_weight.shape[0]
    flat_table = slot_caption.T.reshape(1, slot_count * seq_count)
    selector = (flat_table == jnp.arange(caption_count, dtype=jnp.int32)[:, None]).astype(
        jnp.float32
    )
    payload = jnp.stack([key_part, value_part]).reshape(2, slot_count, seq_count, block_rows, width)
    received = lax.all_to_all(payload, "seq", split_axis=2, concat_axis=2, tiled=True)
    received = received.reshape(2, slot_count * seq_count, block_rows * width).astype(jnp.float32)
    merged = jnp.einsum("cm,kmx->kcx", selector, received, precision=highest)
    merged = merged.reshape(2, caption_count * block_rows, width)
    summed = jnp.dot(merged[0], key_weight.astype(jnp.float32).T, precision=highest)
    summed = summed + jnp.dot(merged[1], value_weight.astype(jnp.float32).T, precision=highest)
    summed = summed.reshape(caption_count, block_rows, features)
    text_grad = lax.psum_scatter(summed, "head", scatter_dimension=2, tiled=True).astype(
        jnp.bfloat16
    )
    return (query_grad, text_grad)


def solution(mesh):
    seq_count, head_devices = mesh.shape["seq"], mesh.shape["head"]
    pairs = seq_count // SPAN <= 2 and seq_count in (4, 8, 16, 32) and head_devices == 4
    placed = (
        P("seq", "head"),
        P("seq", "head"),
        P("seq", None),
        P(),
        P(None, "seq", None, "head"),
        P(None, "head"),
        P(None, "head"),
    )
    return jax.shard_map(
        shards_pairs if pairs else shards_general,
        mesh=mesh,
        in_specs=placed,
        out_specs=(P("seq", "head"), P(None, "seq", "head")),
        check_vma=False,
    )
```

```python
import functools
import math

import jax
import jax.numpy as jnp
from jax import lax
from jax.experimental import pallas as pl
from jax.experimental.pallas import tpu as pltpu
from jax.sharding import PartitionSpec as P

DH = 128
L = 512
TILE = 128
SPAN = 4
F32 = jnp.float32
BF16 = jnp.bfloat16
INV_ROOT = 1.0 / math.sqrt(DH)
KERNEL_LIMIT = 32 * 1024 * 1024
SMALL_LIMIT = 8 * 1024 * 1024


def dot(a, b, contract):
    return lax.dot_general(a, b, ((contract[:1], contract[1:]), ((), ())), preferred_element_type=F32)


def shipping(mask_ref, me, seq_count, tiles):
    odd = jnp.bitwise_and(me, 1)
    ones = mask_ref[1, 0]
    for t in range(1, tiles):
        ones += mask_ref[1, t]
    most = jnp.where(2 * ones > tiles, 1, 0)
    outer = jnp.where(odd == 0, 0, tiles - 1)
    at_end = jnp.where(odd == 0, me == 0, me == seq_count - 1)
    alone = jnp.logical_and(at_end, mask_ref[1 - most, outer] == 1)
    main = jnp.where(alone, 1 - most, most)
    return main, tiles - 1 - outer, jnp.where(alone, tiles // 2, outer)


def backward(key, value, query, grad):
    scores = dot(key, query, (1, 1))
    top = jnp.max(scores, axis=0, keepdims=True)
    exps = jnp.exp((scores - top) * INV_ROOT)
    attention = exps * (1.0 / jnp.sum(exps, axis=0, keepdims=True))
    attention_lo = attention.astype(BF16)
    attention_grad = dot(value, grad, (1, 1))
    row_dot = jnp.sum(attention_lo.astype(F32) * attention_grad, axis=0, keepdims=True)
    score_lo = (attention * (attention_grad - row_dot)).astype(BF16)
    return attention_lo, score_lo


def fetch(pairs, sems):
    copies = [pltpu.make_async_copy(a, b, sems.at[i]) for i, (a, b) in enumerate(pairs)]
    for c in copies:
        c.start()
    return copies


def stage_kernel(seq_count, captions, tiles, mask_hbm, caps_hbm, q_hbm, g_hbm, cache_hbm, *refs):
    y_ref, z_ref, q_ref, g_ref, cache_ref, flags_ref, caption_ref, mask_ref, caps_ref, sems = refs
    me = lax.axis_index("seq")
    copies = fetch(
        [
            (mask_hbm, mask_ref),
            (caps_hbm, caps_ref),
            (q_hbm, q_ref),
            (g_hbm, g_ref),
            (cache_hbm.at[:, :, :, pl.ds(0, DH)], cache_ref),
        ],
        sems,
    )
    for c in copies[:2]:
        c.wait()
    mine, *picked = shipping(mask_ref, me, seq_count, tiles)
    lanes = (1, flags_ref.shape[1])
    for t in range(tiles):
        flags_ref[t : t + 1, :] = jnp.full(lanes, mask_ref[1, t].astype(F32), F32)
        flags_ref[tiles + t : tiles + t + 1, :] = jnp.full(lanes, mask_ref[mine, t].astype(F32), F32)
    flags_ref[2 * tiles : 2 * tiles + 1, :] = jnp.full(lanes, mine.astype(F32), F32)
    along = lax.rem(me + jnp.where(jnp.bitwise_and(me, 1) == 0, 2, seq_count - 2), seq_count)
    expects = jnp.int32(0)
    for d in (jnp.bitwise_xor(me, 1), along):
        expects += jnp.where(jnp.logical_and(caps_ref[0, d] < captions, caps_ref[1, d] < captions), 1, 0)
    last = flags_ref.shape[0] - 1
    flags_ref[last : last + 1, :] = jnp.full(lanes, expects.astype(F32), F32)
    caption_ref[...] = jnp.full(caption_ref.shape, caps_ref[mine, me].astype(F32), F32).astype(BF16)
    for c in copies[2:4]:
        c.wait()
    for tile, out in zip(picked, (y_ref, z_ref), strict=True):
        keep = (mask_ref[mine, tile] == 0).astype(F32).astype(BF16)
        at = pl.ds(pl.multiple_of(tile * TILE, TILE), TILE)
        out[0] = q_ref[at, :] * keep
        out[1] = g_ref[at, :] * keep
    copies[4].wait()


def pick(flag, pair):
    return pair[0] * (1.0 - flag).astype(BF16) + pair[1] * flag.astype(BF16)


def own_kernel(
    tiles, heads, flags_ref, q_ref, g_ref, first_ref, cache_hbm, wk_hbm, wv_hbm,
    dq_hbm, part_ref, main_ref, weight_ref, cache_buf, dq_buf, sems, out_sems,
):
    pairs = [(cache_hbm.at[:, :, :, pl.ds(h * DH, DH)], cache_buf.at[h - 1]) for h in range(1, heads)]
    width = heads * DH
    pairs += [(wk_hbm, weight_ref.at[:, pl.ds(0, width)]), (wv_hbm, weight_ref.at[:, pl.ds(width, width)])]
    copies = fetch(pairs, sems)
    mine = flags_ref[2 * tiles : 2 * tiles + 1, :]
    slot = (jnp.max(mine) > 0.0).astype(jnp.int32)
    one_caption = jnp.min(flags_ref[tiles : 2 * tiles, :]) > 0.0
    stores = [
        pltpu.make_async_copy(dq_buf.at[h], dq_hbm.at[:, pl.ds(h * DH, DH)], out_sems.at[h]) for h in range(heads)
    ]

    @pl.when(one_caption)
    def _():
        for h in range(heads):
            cols = slice(h * DH, (h + 1) * DH)
            if h:
                copies[h - 1].wait()
            cache = first_ref if h == 0 else cache_buf.at[h - 1]
            key, value = cache[0, slot], cache[1, slot]
            query, grad = q_ref[:, cols], g_ref[:, cols]
            attention_lo, score_lo = backward(key, value, query, grad)
            dq_buf[h] = (dot(key.T, score_lo, (1, 0)) * INV_ROOT).astype(BF16).T
            stores[h].start()
            part_ref[0, :, cols] = dot(score_lo, query, (1, 0))
            part_ref[1, :, cols] = dot(attention_lo, grad, (1, 0))
            main_ref[0, :, cols] = key
            main_ref[1, :, cols] = value

    @pl.when(jnp.logical_not(one_caption))
    def _():
        slots = [flags_ref[t : t + 1, :] for t in range(tiles)]
        keeps = [flags_ref[tiles + t : tiles + t + 1, :] for t in range(tiles)]
        for h in range(heads):
            cols = slice(h * DH, (h + 1) * DH)
            if h:
                copies[h - 1].wait()
            cache = first_ref if h == 0 else cache_buf.at[h - 1]
            keys, values = (cache[0, 0], cache[0, 1]), (cache[1, 0], cache[1, 1])
            probs, grads, queries, outs = [], [], [], []
            for t in range(tiles):
                rows = slice(t * TILE, (t + 1) * TILE)
                query, grad = q_ref[rows, cols], g_ref[rows, cols]
                attention_lo, score_lo = backward(pick(slots[t], keys), pick(slots[t], values), query, grad)
                probs.append(attention_lo)
                grads.append(score_lo)
                queries.append(query * keeps[t].astype(BF16))
                outs.append(grad * keeps[t].astype(BF16))
            score_grads = jnp.concatenate(grads, axis=1)
            dq = [dot(key.T, score_grads, (1, 0)) * INV_ROOT for key in keys]
            for t in range(tiles):
                rows = slice(t * TILE, (t + 1) * TILE)
                dq_t = jnp.where(slots[t] == 1.0, dq[1][:, rows], dq[0][:, rows])
                dq_buf[h, rows, :] = dq_t.astype(BF16).T
            stores[h].start()
            part_ref[0, :, cols] = dot(score_grads, jnp.concatenate(queries, axis=0), (1, 0))
            part_ref[1, :, cols] = dot(jnp.concatenate(probs, axis=1), jnp.concatenate(outs, axis=0), (1, 0))
            main_ref[0, :, cols] = pick(mine, keys)
            main_ref[1, :, cols] = pick(mine, values)

    for copy in stores + copies[heads - 1 :]:
        copy.wait()


def gather_parts(heads, blocks, main_ref, part_ref, both_ref, received=None):
    me, core = lax.axis_index("seq"), jnp.bitwise_and(lax.axis_index("head"), 1)
    block_rows, width = L // blocks, heads * DH
    places = []
    for s in range(blocks):
        rel = jnp.bitwise_xor(jnp.bitwise_xor(me, s), core)
        place = blocks // 2 - 1 - jnp.right_shift(rel, 1)
        place += jnp.bitwise_and(rel, 1) * (blocks // 2)
        places.append(pl.ds(pl.multiple_of(place * block_rows, block_rows), block_rows))
    for h in range(heads):
        cols = slice(h * DH, (h + 1) * DH)
        dk, dv = part_ref[0, :, cols], part_ref[1, :, cols]
        if received is not None:
            y_ref, z_ref = received
            query, grad = y_ref[0, :, cols] + z_ref[0, :, cols], y_ref[1, :, cols] + z_ref[1, :, cols]
            attention_lo, score_lo = backward(main_ref[0, :, cols], main_ref[1, :, cols], query, grad)
            dk, dv = dk + dot(score_lo, query, (1, 0)), dv + dot(attention_lo, grad, (1, 0))
        dk, dv = (dk * INV_ROOT).astype(BF16), dv.astype(BF16)
        for s, rows in enumerate(places):
            both_ref[rows, h * DH : (h + 1) * DH] = dk[s * block_rows : (s + 1) * block_rows]
            both_ref[rows, width + h * DH : width + (h + 1) * DH] = dv[s * block_rows : (s + 1) * block_rows]


def project(both, weight_ref, rel, out_ref):
    features = out_ref.shape[2]
    chip = jnp.right_shift(lax.axis_index("head"), 1)
    rows = pl.ds(pl.multiple_of(jnp.bitwise_xor(chip, rel) * features, features), features)
    out_ref[...] = dot(both, weight_ref[rows, :], (1, 1)).astype(BF16).reshape(out_ref.shape)


def expects(flags_ref):
    last = flags_ref.shape[0] - 1
    return jnp.max(flags_ref[last : last + 1, :]) > 0.0


def early_text_kernel(heads, blocks, flags_ref, part_ref, weight_ref, both_ref, sent_ref):
    @pl.when(jnp.logical_not(expects(flags_ref)))
    def _():
        gather_parts(heads, blocks, None, part_ref, both_ref)
        project(both_ref[L // 2 :, :], weight_ref, 1, sent_ref)


def first_text_kernel(heads, blocks, flags_ref, z_ref, y_ref, main_ref, part_ref, weight_ref, *refs):
    early, outs = refs[:2], refs[2:]
    come = expects(flags_ref)

    @pl.when(come)
    def _():
        both_ref, sent_ref = outs
        gather_parts(heads, blocks, main_ref, part_ref, both_ref, (y_ref, z_ref))
        project(both_ref[L // 2 :, :], weight_ref, 1, sent_ref)

    @pl.when(jnp.logical_not(come))
    def _():
        for a, b in zip(early, outs, strict=True):
            b[...] = a[...]


def second_text_kernel(both_ref, weight_ref, sent_own_ref, kept_ref, kept_own_ref):
    project(both_ref[L // 2 :, :], weight_ref, 0, sent_own_ref)
    project(both_ref[: L // 2, :], weight_ref, 1, kept_ref)
    project(both_ref[: L // 2, :], weight_ref, 0, kept_own_ref)


def pair_kernel(kept_ref, came_ref, *outs):
    for i, out in enumerate(outs):
        out[...] = (kept_ref[i].astype(F32) + came_ref[i].astype(F32)).astype(BF16)


def cross_kernel(i, kept_ref, came_ref, crossed_ref, caption_ref, out_ref):
    pair = (kept_ref[i].astype(F32) + came_ref[i].astype(F32)).astype(BF16)
    total = (pair.astype(F32) + crossed_ref[...].astype(F32)).astype(BF16)
    height, lanes = out_ref.shape[1:]
    across = total.shape[1] // lanes
    for n in range(out_ref.shape[0] - 1):
        r, c = n // across * height, n % across * lanes
        out_ref[n] = total[r : r + height, c : c + lanes]
    out_ref[out_ref.shape[0] - 1] = caption_ref[...]


def caption_kernel(bases, *refs):
    *blocks, own_ref, kept_ref, sent_ref = refs
    captions, block_rows, width = kept_ref.shape
    _, height, lanes = own_ref.shape
    half = width // lanes
    across = 2 * half
    core = jnp.bitwise_and(lax.axis_index("head"), 1)
    for r in range(block_rows // height):
        totals = [[0.0] * across for _ in range(captions)]
        for base, block in zip(bases, blocks, strict=True):
            caption = block[block.shape[0] - 1].astype(F32)
            if base == 0:
                caption = jnp.where(core == 0, own_ref[own_ref.shape[0] - 1].astype(F32), caption)
            for n in range(across):
                value = block[r * across + n].astype(F32)
                if base == 0:
                    value = jnp.where(core == 0, own_ref[r * across + n].astype(F32), value)
                for c in range(captions):
                    totals[c][n] += jnp.where(caption == c, value, 0.0)
        rows = slice(r * height, (r + 1) * height)
        for c in range(captions):
            for n in range(half):
                cols = slice(n * lanes, (n + 1) * lanes)
                low, high = totals[c][n], totals[c][half + n]
                kept_ref[c, rows, cols] = jnp.where(core == 0, low, high)
                sent_ref[c, rows, cols] = jnp.where(core == 0, high, low).astype(BF16)


def final_kernel(kept_ref, came_ref, out_ref):
    out_ref[...] = (kept_ref[...] + came_ref[...].astype(F32)).astype(BF16)


def swap(array, axis, bit):
    n = lax.axis_size(axis)
    return lax.ppermute(array, axis, [(i, i ^ bit) for i in range(n)])


def send(block, base):
    seq_count, head_devices = lax.axis_size("seq"), lax.axis_size("head")
    pairs = []
    for s in range(seq_count):
        for h in range(head_devices):
            target = s ^ base ^ (h & 1)
            if target != s:
                pairs.append((s * head_devices + h, target * head_devices + h))
    return lax.ppermute(block, ("seq", "head"), pairs)


def call(kernel, name, out_shape, operands, specs, scratch=(), limit=SMALL_LIMIT, hint_us=1.0, out_specs=None):
    vmem = pl.BlockSpec(memory_space=pltpu.VMEM)
    return pl.pallas_call(
        kernel,
        out_shape=out_shape,
        in_specs=specs,
        out_specs=out_specs or jax.tree.map(lambda _: vmem, out_shape),
        scratch_shapes=scratch,
        compiler_params=pltpu.CompilerParams(vmem_limit_bytes=limit),
        cost_estimate=pl.CostEstimate(flops=0, bytes_accessed=int(hint_us * 3_600_000), transcendentals=0),
        name=name,
    )(*operands)


def shards_pairs(queries, out_grad, tile_mask, slot_caption, caption_cache, key_weight, value_weight):
    rows_here, width = queries.shape
    heads = width // DH
    tiles = rows_here // TILE
    slots = tile_mask.shape[1]
    seq_count, head_devices = lax.axis_size("seq"), lax.axis_size("head")
    captions = seq_count // SPAN
    block_rows = L // seq_count
    held_back = [
        pltpu.with_memory_space_constraint(x, pltpu.HBM)
        for x in (tile_mask.T, slot_caption.T, queries, out_grad, caption_cache, key_weight, value_weight)
    ]
    mask_t, caps_t = held_back[:2]
    vmem = pl.BlockSpec(memory_space=pltpu.VMEM)
    hbm = pl.BlockSpec(memory_space=pltpu.HBM)

    def like(*shape, dtype=BF16):
        return jax.ShapeDtypeStruct(shape, dtype)

    to_y, to_z, q_here, g_here, cache_first, flags, caption = call(
        functools.partial(stage_kernel, seq_count, captions, tiles),
        "stage",
        (
            like(2, TILE, width),
            like(2, TILE, width),
            like(rows_here, width),
            like(rows_here, width),
            like(2, slots, L, DH),
            like(8 * (-(-(2 * tiles + 2) // 8)), 128, dtype=F32),
            like(16, 128),
        ),
        held_back[:5],
        [hbm] * 5,
        [
            pltpu.SMEM(mask_t.shape, jnp.int32),
            pltpu.SMEM(caps_t.shape, jnp.int32),
            pltpu.SemaphoreType.DMA((5,)),
        ],
        limit=KERNEL_LIMIT,
    )
    from_y = swap(to_y, "seq", 1)
    from_z = lax.ppermute(to_z, "seq", [(s, (s + (2 if s & 1 else -2)) % seq_count) for s in range(seq_count)])

    query_grad, part, main, weight = call(
        functools.partial(own_kernel, tiles, heads),
        "own_tiles",
        (
            like(rows_here, width),
            like(2, L, width, dtype=F32),
            like(2, L, width),
            like(key_weight.shape[0], 2 * width),
        ),
        (flags, q_here, g_here, cache_first, *held_back[4:]),
        [vmem] * 4 + [hbm] * 3,
        [
            pltpu.VMEM((heads - 1, 2, slots, L, DH), BF16),
            pltpu.VMEM((heads, rows_here, DH), BF16),
            pltpu.SemaphoreType.DMA((heads + 1,)),
            pltpu.SemaphoreType.DMA((heads,)),
        ],
        limit=KERNEL_LIMIT,
        hint_us=5.0,
        out_specs=(hbm, vmem, vmem, vmem),
    )
    half = like(seq_count // 2, block_rows, 2 * width)
    texts = (like(L, 2 * width), half)
    early = call(
        functools.partial(early_text_kernel, heads, seq_count),
        "early_text",
        texts,
        (flags, part, weight),
        [vmem] * 3,
        limit=KERNEL_LIMIT,
        hint_us=1.0,
    )
    both, sent = call(
        functools.partial(first_text_kernel, heads, seq_count),
        "first_text",
        texts,
        (flags, from_z, from_y, main, part, weight, *early),
        [vmem] * 8,
        limit=KERNEL_LIMIT,
        hint_us=2.0,
    )
    sent_own, kept, kept_own = call(
        second_text_kernel,
        "second_text",
        (half, half, half),
        (both, weight),
        [vmem] * 2,
        limit=KERNEL_LIMIT,
        hint_us=1.0,
    )
    block = like(block_rows, 2 * width)
    far = call(pair_kernel, "pair", (block,) * (seq_count // 2), (kept, swap(sent, "head", 1)), [vmem] * 2)
    came_own = swap(sent_own, "head", 1)
    bases = [2 * (seq_count // 2 - 1 - i) for i in range(seq_count // 2)]
    arrived, own = [], None
    for i, base in enumerate(bases):
        mine = call(
            functools.partial(cross_kernel, i),
            "cross",
            like(block_rows // 16 * (2 * width // 128) + 1, 16, 128),
            (kept_own, came_own, swap(far[i], "head", 2), caption),
            [vmem] * 4,
        )
        if base == 0:
            own = mine
        arrived.append(send(mine, base))
    kept, sent = call(
        functools.partial(caption_kernel, bases[::-1]),
        "captions",
        (like(captions, block_rows, width, dtype=F32), like(captions, block_rows, width)),
        (*reversed(arrived), own),
        [vmem] * (1 + len(bases)),
    )
    text_grad = call(
        final_kernel, "final", like(captions, block_rows, width), (kept, swap(sent, "head", 1)), [vmem] * 2
    )
    return query_grad, text_grad


def shards_general(queries, out_grad, tile_mask, slot_caption, caption_cache, key_weight, value_weight):
    highest = lax.Precision.HIGHEST
    rows_here, width = queries.shape
    head_count = width // DH
    tile_count = rows_here // TILE
    slot_count = tile_mask.shape[1]
    inv_root = 1.0 / math.sqrt(DH)
    query_tiles = queries.reshape(tile_count, TILE, head_count, DH)
    grad_tiles = out_grad.reshape(tile_count, TILE, head_count, DH)
    slot_onehot = tile_mask.astype(jnp.float32)
    slot_lo = tile_mask.astype(jnp.bfloat16)
    key_rows = jnp.einsum(
        "ts,sjc->tjc", slot_lo, caption_cache[0], preferred_element_type=jnp.float32
    )
    key_rows = key_rows.astype(jnp.bfloat16).reshape(tile_count, L, head_count, DH)
    value_rows = jnp.einsum(
        "ts,sjc->tjc", slot_lo, caption_cache[1], preferred_element_type=jnp.float32
    )
    value_rows = value_rows.astype(jnp.bfloat16).reshape(tile_count, L, head_count, DH)
    scores = (
        jnp.einsum("tqhe,tjhe->thqj", query_tiles, key_rows, preferred_element_type=jnp.float32)
        * inv_root
    )
    row_max = jnp.max(scores, axis=-1, keepdims=True)
    exp_scores = jnp.exp(scores - row_max)
    attention = exp_scores / jnp.sum(exp_scores, axis=-1, keepdims=True)
    attention_lo = attention.astype(jnp.bfloat16)
    context = jnp.einsum(
        "thqj,tjhe->tqhe", attention_lo, value_rows, preferred_element_type=jnp.float32
    )
    row_dot = jnp.transpose(jnp.sum(grad_tiles.astype(jnp.float32) * context, axis=-1), (0, 2, 1))
    attention_grad = jnp.einsum(
        "tqhe,tjhe->thqj", grad_tiles, value_rows, preferred_element_type=jnp.float32
    )
    score_grad = attention * (attention_grad - row_dot[..., None])
    score_lo = score_grad.astype(jnp.bfloat16)
    query_grad = (
        jnp.einsum("thqj,tjhe->tqhe", score_lo, key_rows, preferred_element_type=jnp.float32)
        * inv_root
    )
    query_grad = query_grad.astype(jnp.bfloat16).reshape(rows_here, width)
    key_pieces = (
        jnp.einsum("thqj,tqhe->tjhe", score_lo, query_tiles, preferred_element_type=jnp.float32)
        * inv_root
    )
    value_pieces = jnp.einsum(
        "thqj,tqhe->tjhe", attention_lo, grad_tiles, preferred_element_type=jnp.float32
    )
    key_part = jnp.einsum("ts,tjhe->sjhe", slot_onehot, key_pieces, precision=highest)
    key_part = key_part.astype(jnp.bfloat16).reshape(slot_count, L, width)
    value_part = jnp.einsum("ts,tjhe->sjhe", slot_onehot, value_pieces, precision=highest)
    value_part = value_part.astype(jnp.bfloat16).reshape(slot_count, L, width)
    seq_count = lax.axis_size("seq")
    caption_count = seq_count // SPAN
    block_rows = L // seq_count
    features = key_weight.shape[0]
    flat_table = slot_caption.T.reshape(1, slot_count * seq_count)
    selector = (flat_table == jnp.arange(caption_count, dtype=jnp.int32)[:, None]).astype(
        jnp.float32
    )
    payload = jnp.stack([key_part, value_part]).reshape(2, slot_count, seq_count, block_rows, width)
    received = lax.all_to_all(payload, "seq", split_axis=2, concat_axis=2, tiled=True)
    received = received.reshape(2, slot_count * seq_count, block_rows * width).astype(jnp.float32)
    merged = jnp.einsum("cm,kmx->kcx", selector, received, precision=highest)
    merged = merged.reshape(2, caption_count * block_rows, width)
    summed = jnp.dot(merged[0], key_weight.astype(jnp.float32).T, precision=highest)
    summed = summed + jnp.dot(merged[1], value_weight.astype(jnp.float32).T, precision=highest)
    summed = summed.reshape(caption_count, block_rows, features)
    text_grad = lax.psum_scatter(summed, "head", scatter_dimension=2, tiled=True).astype(
        jnp.bfloat16
    )
    return (query_grad, text_grad)


def solution(mesh):
    seq_count, head_devices = mesh.shape["seq"], mesh.shape["head"]
    pairs = seq_count // SPAN <= 2 and seq_count in (4, 8, 16, 32) and head_devices == 4
    placed = (
        P("seq", "head"),
        P("seq", "head"),
        P("seq", None),
        P(),
        P(None, "seq", None, "head"),
        P(None, "head"),
        P(None, "head"),
    )
    return jax.shard_map(
        shards_pairs if pairs else shards_general,
        mesh=mesh,
        in_specs=placed,
        out_specs=(P("seq", "head"), P(None, "seq", "head")),
        check_vma=False,
    )
```

```python
import functools
import math

import jax
import jax.numpy as jnp
from jax import lax
from jax.experimental import pallas as pl
from jax.experimental.pallas import tpu as pltpu
from jax.sharding import PartitionSpec as P

DH = 128
L = 512
TILE = 128
SPAN = 4
F32 = jnp.float32
BF16 = jnp.bfloat16
INV_ROOT = 1.0 / math.sqrt(DH)
KERNEL_LIMIT = 32 * 1024 * 1024
SMALL_LIMIT = 8 * 1024 * 1024


def dot(a, b, contract):
    return lax.dot_general(a, b, ((contract[:1], contract[1:]), ((), ())), preferred_element_type=F32)


def shipping(mask_ref, me, seq_count, tiles):
    odd = jnp.bitwise_and(me, 1)
    ones = mask_ref[1, 0]
    for t in range(1, tiles):
        ones += mask_ref[1, t]
    most = jnp.where(2 * ones > tiles, 1, 0)
    outer = jnp.where(odd == 0, 0, tiles - 1)
    at_end = jnp.where(odd == 0, me == 0, me == seq_count - 1)
    alone = jnp.logical_and(at_end, mask_ref[1 - most, outer] == 1)
    main = jnp.where(alone, 1 - most, most)
    return main, tiles - 1 - outer, jnp.where(alone, tiles // 2, outer)


def backward(key, value, query, grad):
    scores = dot(key, query, (1, 1))
    top = jnp.max(scores, axis=0, keepdims=True)
    exps = jnp.exp((scores - top) * INV_ROOT)
    attention = exps * (1.0 / jnp.sum(exps, axis=0, keepdims=True))
    attention_lo = attention.astype(BF16)
    attention_grad = dot(value, grad, (1, 1))
    row_dot = jnp.sum(attention_lo.astype(F32) * attention_grad, axis=0, keepdims=True)
    score_lo = (attention * (attention_grad - row_dot)).astype(BF16)
    return attention_lo, score_lo


def fetch(pairs, sems):
    copies = [pltpu.make_async_copy(a, b, sems.at[i]) for i, (a, b) in enumerate(pairs)]
    for c in copies:
        c.start()
    return copies


def stage_kernel(seq_count, captions, tiles, mask_hbm, caps_hbm, q_hbm, g_hbm, cache_hbm, *refs):
    y_ref, z_ref, q_ref, g_ref, cache_ref, flags_ref, caption_ref, mask_ref, caps_ref, sems = refs
    me = lax.axis_index("seq")
    copies = fetch(
        [
            (mask_hbm, mask_ref),
            (caps_hbm, caps_ref),
            (q_hbm, q_ref),
            (g_hbm, g_ref),
            (cache_hbm.at[:, :, :, pl.ds(0, DH)], cache_ref),
        ],
        sems,
    )
    for c in copies[:4]:
        c.wait()
    mine, *picked = shipping(mask_ref, me, seq_count, tiles)
    for tile, out in zip(picked, (y_ref, z_ref), strict=True):
        keep = (mask_ref[mine, tile] == 0).astype(F32).astype(BF16)
        at = pl.ds(pl.multiple_of(tile * TILE, TILE), TILE)
        out[0] = q_ref[at, :] * keep
        out[1] = g_ref[at, :] * keep
    lanes = (1, flags_ref.shape[1])
    for t in range(tiles):
        flags_ref[t : t + 1, :] = jnp.full(lanes, mask_ref[1, t].astype(F32), F32)
        flags_ref[tiles + t : tiles + t + 1, :] = jnp.full(lanes, mask_ref[mine, t].astype(F32), F32)
    flags_ref[2 * tiles : 2 * tiles + 1, :] = jnp.full(lanes, mine.astype(F32), F32)
    along = lax.rem(me + jnp.where(jnp.bitwise_and(me, 1) == 0, 2, seq_count - 2), seq_count)
    expects = jnp.int32(0)
    for d in (jnp.bitwise_xor(me, 1), along):
        expects += jnp.where(jnp.logical_and(caps_ref[0, d] < captions, caps_ref[1, d] < captions), 1, 0)
    last = flags_ref.shape[0] - 1
    flags_ref[last : last + 1, :] = jnp.full(lanes, expects.astype(F32), F32)
    caption_ref[...] = jnp.full(caption_ref.shape, caps_ref[mine, me].astype(F32), F32).astype(BF16)
    copies[4].wait()


def pick(flag, pair):
    return pair[0] * (1.0 - flag).astype(BF16) + pair[1] * flag.astype(BF16)


def own_kernel(
    tiles, heads, flags_ref, q_ref, g_ref, first_ref, cache_hbm, wk_hbm, wv_hbm,
    dq_hbm, part_ref, main_ref, weight_ref, cache_buf, dq_buf, sems, out_sems,
):
    pairs = [(cache_hbm.at[:, :, :, pl.ds(h * DH, DH)], cache_buf.at[h - 1]) for h in range(1, heads)]
    width = heads * DH
    pairs += [(wk_hbm, weight_ref.at[:, pl.ds(0, width)]), (wv_hbm, weight_ref.at[:, pl.ds(width, width)])]
    copies = fetch(pairs, sems)
    mine = flags_ref[2 * tiles : 2 * tiles + 1, :]
    slot = (jnp.max(mine) > 0.0).astype(jnp.int32)
    one_caption = jnp.min(flags_ref[tiles : 2 * tiles, :]) > 0.0
    stores = [
        pltpu.make_async_copy(dq_buf.at[h], dq_hbm.at[:, pl.ds(h * DH, DH)], out_sems.at[h]) for h in range(heads)
    ]

    @pl.when(one_caption)
    def _():
        for h in range(heads):
            cols = slice(h * DH, (h + 1) * DH)
            if h:
                copies[h - 1].wait()
            cache = first_ref if h == 0 else cache_buf.at[h - 1]
            key, value = cache[0, slot], cache[1, slot]
            query, grad = q_ref[:, cols], g_ref[:, cols]
            attention_lo, score_lo = backward(key, value, query, grad)
            dq_buf[h] = (dot(key.T, score_lo, (1, 0)) * INV_ROOT).astype(BF16).T
            stores[h].start()
            part_ref[0, :, cols] = dot(score_lo, query, (1, 0))
            part_ref[1, :, cols] = dot(attention_lo, grad, (1, 0))
            main_ref[0, :, cols] = key
            main_ref[1, :, cols] = value

    @pl.when(jnp.logical_not(one_caption))
    def _():
        slots = [flags_ref[t : t + 1, :] for t in range(tiles)]
        keeps = [flags_ref[tiles + t : tiles + t + 1, :] for t in range(tiles)]
        for h in range(heads):
            cols = slice(h * DH, (h + 1) * DH)
            if h:
                copies[h - 1].wait()
            cache = first_ref if h == 0 else cache_buf.at[h - 1]
            keys, values = (cache[0, 0], cache[0, 1]), (cache[1, 0], cache[1, 1])
            probs, grads, queries, outs = [], [], [], []
            for t in range(tiles):
                rows = slice(t * TILE, (t + 1) * TILE)
                query, grad = q_ref[rows, cols], g_ref[rows, cols]
                attention_lo, score_lo = backward(pick(slots[t], keys), pick(slots[t], values), query, grad)
                probs.append(attention_lo)
                grads.append(score_lo)
                queries.append(query * keeps[t].astype(BF16))
                outs.append(grad * keeps[t].astype(BF16))
            score_grads = jnp.concatenate(grads, axis=1)
            dq = [dot(key.T, score_grads, (1, 0)) * INV_ROOT for key in keys]
            for t in range(tiles):
                rows = slice(t * TILE, (t + 1) * TILE)
                dq_t = jnp.where(slots[t] == 1.0, dq[1][:, rows], dq[0][:, rows])
                dq_buf[h, rows, :] = dq_t.astype(BF16).T
            stores[h].start()
            part_ref[0, :, cols] = dot(score_grads, jnp.concatenate(queries, axis=0), (1, 0))
            part_ref[1, :, cols] = dot(jnp.concatenate(probs, axis=1), jnp.concatenate(outs, axis=0), (1, 0))
            main_ref[0, :, cols] = pick(mine, keys)
            main_ref[1, :, cols] = pick(mine, values)

    for copy in stores + copies[heads - 1 :]:
        copy.wait()


def gather_parts(heads, blocks, main_ref, part_ref, both_ref, received=None):
    me, core = lax.axis_index("seq"), jnp.bitwise_and(lax.axis_index("head"), 1)
    block_rows, width = L // blocks, heads * DH
    places = []
    for s in range(blocks):
        rel = jnp.bitwise_xor(jnp.bitwise_xor(me, s), core)
        place = blocks // 2 - 1 - jnp.right_shift(rel, 1)
        place += jnp.bitwise_and(rel, 1) * (blocks // 2)
        places.append(pl.ds(pl.multiple_of(place * block_rows, block_rows), block_rows))
    for h in range(heads):
        cols = slice(h * DH, (h + 1) * DH)
        dk, dv = part_ref[0, :, cols], part_ref[1, :, cols]
        if received is not None:
            y_ref, z_ref = received
            query, grad = y_ref[0, :, cols] + z_ref[0, :, cols], y_ref[1, :, cols] + z_ref[1, :, cols]
            attention_lo, score_lo = backward(main_ref[0, :, cols], main_ref[1, :, cols], query, grad)
            dk, dv = dk + dot(score_lo, query, (1, 0)), dv + dot(attention_lo, grad, (1, 0))
        dk, dv = (dk * INV_ROOT).astype(BF16), dv.astype(BF16)
        for s, rows in enumerate(places):
            both_ref[rows, h * DH : (h + 1) * DH] = dk[s * block_rows : (s + 1) * block_rows]
            both_ref[rows, width + h * DH : width + (h + 1) * DH] = dv[s * block_rows : (s + 1) * block_rows]


def project(both, weight_ref, rel, out_ref):
    features = out_ref.shape[2]
    chip = jnp.right_shift(lax.axis_index("head"), 1)
    rows = pl.ds(pl.multiple_of(jnp.bitwise_xor(chip, rel) * features, features), features)
    out_ref[...] = dot(both, weight_ref[rows, :], (1, 1)).astype(BF16).reshape(out_ref.shape)


def expects(flags_ref):
    last = flags_ref.shape[0] - 1
    return jnp.max(flags_ref[last : last + 1, :]) > 0.0


def early_text_kernel(heads, blocks, flags_ref, part_ref, weight_ref, both_ref, sent_ref):
    @pl.when(jnp.logical_not(expects(flags_ref)))
    def _():
        gather_parts(heads, blocks, None, part_ref, both_ref)
        project(both_ref[L // 2 :, :], weight_ref, 1, sent_ref)


def first_text_kernel(heads, blocks, flags_ref, z_ref, y_ref, main_ref, part_ref, weight_ref, *refs):
    early, outs = refs[:2], refs[2:]
    come = expects(flags_ref)

    @pl.when(come)
    def _():
        both_ref, sent_ref = outs
        gather_parts(heads, blocks, main_ref, part_ref, both_ref, (y_ref, z_ref))
        project(both_ref[L // 2 :, :], weight_ref, 1, sent_ref)

    @pl.when(jnp.logical_not(come))
    def _():
        for a, b in zip(early, outs, strict=True):
            b[...] = a[...]


def second_text_kernel(both_ref, weight_ref, sent_own_ref, kept_ref):
    project(both_ref[L // 2 :, :], weight_ref, 0, sent_own_ref)
    project(both_ref[: L // 2, :], weight_ref, 1, kept_ref)


def third_text_kernel(both_ref, weight_ref, kept_own_ref):
    project(both_ref[: L // 2, :], weight_ref, 0, kept_own_ref)


def pair_kernel(kept_ref, came_ref, *outs):
    for i, out in enumerate(outs):
        out[...] = (kept_ref[i].astype(F32) + came_ref[i].astype(F32)).astype(BF16)


def cross_kernel(i, kept_ref, came_ref, crossed_ref, caption_ref, out_ref):
    pair = (kept_ref[i].astype(F32) + came_ref[i].astype(F32)).astype(BF16)
    total = (pair.astype(F32) + crossed_ref[...].astype(F32)).astype(BF16)
    height, lanes = out_ref.shape[1:]
    across = total.shape[1] // lanes
    for n in range(out_ref.shape[0] - 1):
        r, c = n // across * height, n % across * lanes
        out_ref[n] = total[r : r + height, c : c + lanes]
    out_ref[out_ref.shape[0] - 1] = caption_ref[...]


def caption_kernel(bases, *refs):
    *blocks, own_ref, kept_ref, sent_ref = refs
    captions, block_rows, width = kept_ref.shape
    _, height, lanes = own_ref.shape
    half = width // lanes
    across = 2 * half
    core = jnp.bitwise_and(lax.axis_index("head"), 1)
    for r in range(block_rows // height):
        totals = [[0.0] * across for _ in range(captions)]
        for base, block in zip(bases, blocks, strict=True):
            caption = block[block.shape[0] - 1].astype(F32)
            if base == 0:
                caption = jnp.where(core == 0, own_ref[own_ref.shape[0] - 1].astype(F32), caption)
            for n in range(across):
                value = block[r * across + n].astype(F32)
                if base == 0:
                    value = jnp.where(core == 0, own_ref[r * across + n].astype(F32), value)
                for c in range(captions):
                    totals[c][n] += jnp.where(caption == c, value, 0.0)
        rows = slice(r * height, (r + 1) * height)
        for c in range(captions):
            for n in range(half):
                cols = slice(n * lanes, (n + 1) * lanes)
                low, high = totals[c][n], totals[c][half + n]
                kept_ref[c, rows, cols] = jnp.where(core == 0, low, high)
                sent_ref[c, rows, cols] = jnp.where(core == 0, high, low).astype(BF16)


def final_kernel(kept_ref, came_ref, out_ref):
    out_ref[...] = (kept_ref[...] + came_ref[...].astype(F32)).astype(BF16)


def swap(array, axis, bit):
    n = lax.axis_size(axis)
    return lax.ppermute(array, axis, [(i, i ^ bit) for i in range(n)])


def send(block, base):
    seq_count, head_devices = lax.axis_size("seq"), lax.axis_size("head")
    pairs = []
    for s in range(seq_count):
        for h in range(head_devices):
            target = s ^ base ^ (h & 1)
            if target != s:
                pairs.append((s * head_devices + h, target * head_devices + h))
    return lax.ppermute(block, ("seq", "head"), pairs)


def call(kernel, name, out_shape, operands, specs, scratch=(), limit=SMALL_LIMIT, hint_us=1.0, out_specs=None):
    vmem = pl.BlockSpec(memory_space=pltpu.VMEM)
    return pl.pallas_call(
        kernel,
        out_shape=out_shape,
        in_specs=specs,
        out_specs=out_specs or jax.tree.map(lambda _: vmem, out_shape),
        scratch_shapes=scratch,
        compiler_params=pltpu.CompilerParams(vmem_limit_bytes=limit),
        cost_estimate=pl.CostEstimate(flops=0, bytes_accessed=int(hint_us * 3_600_000), transcendentals=0),
        name=name,
    )(*operands)


def shards_pairs(queries, out_grad, tile_mask, slot_caption, caption_cache, key_weight, value_weight):
    rows_here, width = queries.shape
    heads = width // DH
    tiles = rows_here // TILE
    slots = tile_mask.shape[1]
    seq_count, head_devices = lax.axis_size("seq"), lax.axis_size("head")
    captions = seq_count // SPAN
    block_rows = L // seq_count
    held_back = [
        pltpu.with_memory_space_constraint(x, pltpu.HBM)
        for x in (tile_mask.T, slot_caption.T, queries, out_grad, caption_cache, key_weight, value_weight)
    ]
    mask_t, caps_t = held_back[:2]
    vmem = pl.BlockSpec(memory_space=pltpu.VMEM)
    hbm = pl.BlockSpec(memory_space=pltpu.HBM)

    def like(*shape, dtype=BF16):
        return jax.ShapeDtypeStruct(shape, dtype)

    to_y, to_z, q_here, g_here, cache_first, flags, caption = call(
        functools.partial(stage_kernel, seq_count, captions, tiles),
        "stage",
        (
            like(2, TILE, width),
            like(2, TILE, width),
            like(rows_here, width),
            like(rows_here, width),
            like(2, slots, L, DH),
            like(8 * (-(-(2 * tiles + 2) // 8)), 128, dtype=F32),
            like(16, 128),
        ),
        held_back[:5],
        [hbm] * 5,
        [
            pltpu.SMEM(mask_t.shape, jnp.int32),
            pltpu.SMEM(caps_t.shape, jnp.int32),
            pltpu.SemaphoreType.DMA((5,)),
        ],
        limit=KERNEL_LIMIT,
    )
    from_y = swap(to_y, "seq", 1)
    from_z = lax.ppermute(to_z, "seq", [(s, (s + (2 if s & 1 else -2)) % seq_count) for s in range(seq_count)])

    query_grad, part, main, weight = call(
        functools.partial(own_kernel, tiles, heads),
        "own_tiles",
        (
            like(rows_here, width),
            like(2, L, width, dtype=F32),
            like(2, L, width),
            like(key_weight.shape[0], 2 * width),
        ),
        (flags, q_here, g_here, cache_first, *held_back[4:]),
        [vmem] * 4 + [hbm] * 3,
        [
            pltpu.VMEM((heads - 1, 2, slots, L, DH), BF16),
            pltpu.VMEM((heads, rows_here, DH), BF16),
            pltpu.SemaphoreType.DMA((heads + 1,)),
            pltpu.SemaphoreType.DMA((heads,)),
        ],
        limit=KERNEL_LIMIT,
        hint_us=5.0,
        out_specs=(hbm, vmem, vmem, vmem),
    )
    half = like(seq_count // 2, block_rows, 2 * width)
    texts = (like(L, 2 * width), half)
    early = call(
        functools.partial(early_text_kernel, heads, seq_count),
        "early_text",
        texts,
        (flags, part, weight),
        [vmem] * 3,
        limit=KERNEL_LIMIT,
        hint_us=1.0,
    )
    both, sent = call(
        functools.partial(first_text_kernel, heads, seq_count),
        "first_text",
        texts,
        (flags, from_z, from_y, main, part, weight, *early),
        [vmem] * 8,
        limit=KERNEL_LIMIT,
        hint_us=2.0,
    )
    sent_own, kept = call(
        second_text_kernel,
        "second_text",
        (half, half),
        (both, weight),
        [vmem] * 2,
        limit=KERNEL_LIMIT,
        hint_us=1.0,
    )
    kept_own = call(
        third_text_kernel, "third_text", half, (both, weight), [vmem] * 2, limit=KERNEL_LIMIT, hint_us=1.0
    )
    block = like(block_rows, 2 * width)
    far = call(pair_kernel, "pair", (block,) * (seq_count // 2), (kept, swap(sent, "head", 1)), [vmem] * 2)
    came_own = swap(sent_own, "head", 1)
    bases = [2 * (seq_count // 2 - 1 - i) for i in range(seq_count // 2)]
    arrived, own = [], None
    for i, base in enumerate(bases):
        mine = call(
            functools.partial(cross_kernel, i),
            "cross",
            like(block_rows // 16 * (2 * width // 128) + 1, 16, 128),
            (kept_own, came_own, swap(far[i], "head", 2), caption),
            [vmem] * 4,
        )
        if base == 0:
            own = mine
        arrived.append(send(mine, base))
    kept, sent = call(
        functools.partial(caption_kernel, bases[::-1]),
        "captions",
        (like(captions, block_rows, width, dtype=F32), like(captions, block_rows, width)),
        (*reversed(arrived), own),
        [vmem] * (1 + len(bases)),
    )
    text_grad = call(
        final_kernel, "final", like(captions, block_rows, width), (kept, swap(sent, "head", 1)), [vmem] * 2
    )
    return query_grad, text_grad


def shards_general(queries, out_grad, tile_mask, slot_caption, caption_cache, key_weight, value_weight):
    highest = lax.Precision.HIGHEST
    rows_here, width = queries.shape
    head_count = width // DH
    tile_count = rows_here // TILE
    slot_count = tile_mask.shape[1]
    inv_root = 1.0 / math.sqrt(DH)
    query_tiles = queries.reshape(tile_count, TILE, head_count, DH)
    grad_tiles = out_grad.reshape(tile_count, TILE, head_count, DH)
    slot_onehot = tile_mask.astype(jnp.float32)
    slot_lo = tile_mask.astype(jnp.bfloat16)
    key_rows = jnp.einsum(
        "ts,sjc->tjc", slot_lo, caption_cache[0], preferred_element_type=jnp.float32
    )
    key_rows = key_rows.astype(jnp.bfloat16).reshape(tile_count, L, head_count, DH)
    value_rows = jnp.einsum(
        "ts,sjc->tjc", slot_lo, caption_cache[1], preferred_element_type=jnp.float32
    )
    value_rows = value_rows.astype(jnp.bfloat16).reshape(tile_count, L, head_count, DH)
    scores = (
        jnp.einsum("tqhe,tjhe->thqj", query_tiles, key_rows, preferred_element_type=jnp.float32)
        * inv_root
    )
    row_max = jnp.max(scores, axis=-1, keepdims=True)
    exp_scores = jnp.exp(scores - row_max)
    attention = exp_scores / jnp.sum(exp_scores, axis=-1, keepdims=True)
    attention_lo = attention.astype(jnp.bfloat16)
    context = jnp.einsum(
        "thqj,tjhe->tqhe", attention_lo, value_rows, preferred_element_type=jnp.float32
    )
    row_dot = jnp.transpose(jnp.sum(grad_tiles.astype(jnp.float32) * context, axis=-1), (0, 2, 1))
    attention_grad = jnp.einsum(
        "tqhe,tjhe->thqj", grad_tiles, value_rows, preferred_element_type=jnp.float32
    )
    score_grad = attention * (attention_grad - row_dot[..., None])
    score_lo = score_grad.astype(jnp.bfloat16)
    query_grad = (
        jnp.einsum("thqj,tjhe->tqhe", score_lo, key_rows, preferred_element_type=jnp.float32)
        * inv_root
    )
    query_grad = query_grad.astype(jnp.bfloat16).reshape(rows_here, width)
    key_pieces = (
        jnp.einsum("thqj,tqhe->tjhe", score_lo, query_tiles, preferred_element_type=jnp.float32)
        * inv_root
    )
    value_pieces = jnp.einsum(
        "thqj,tqhe->tjhe", attention_lo, grad_tiles, preferred_element_type=jnp.float32
    )
    key_part = jnp.einsum("ts,tjhe->sjhe", slot_onehot, key_pieces, precision=highest)
    key_part = key_part.astype(jnp.bfloat16).reshape(slot_count, L, width)
    value_part = jnp.einsum("ts,tjhe->sjhe", slot_onehot, value_pieces, precision=highest)
    value_part = value_part.astype(jnp.bfloat16).reshape(slot_count, L, width)
    seq_count = lax.axis_size("seq")
    caption_count = seq_count // SPAN
    block_rows = L // seq_count
    features = key_weight.shape[0]
    flat_table = slot_caption.T.reshape(1, slot_count * seq_count)
    selector = (flat_table == jnp.arange(caption_count, dtype=jnp.int32)[:, None]).astype(
        jnp.float32
    )
    payload = jnp.stack([key_part, value_part]).reshape(2, slot_count, seq_count, block_rows, width)
    received = lax.all_to_all(payload, "seq", split_axis=2, concat_axis=2, tiled=True)
    received = received.reshape(2, slot_count * seq_count, block_rows * width).astype(jnp.float32)
    merged = jnp.einsum("cm,kmx->kcx", selector, received, precision=highest)
    merged = merged.reshape(2, caption_count * block_rows, width)
    summed = jnp.dot(merged[0], key_weight.astype(jnp.float32).T, precision=highest)
    summed = summed + jnp.dot(merged[1], value_weight.astype(jnp.float32).T, precision=highest)
    summed = summed.reshape(caption_count, block_rows, features)
    text_grad = lax.psum_scatter(summed, "head", scatter_dimension=2, tiled=True).astype(
        jnp.bfloat16
    )
    return (query_grad, text_grad)


def solution(mesh):
    seq_count, head_devices = mesh.shape["seq"], mesh.shape["head"]
    pairs = seq_count // SPAN <= 2 and seq_count in (4, 8, 16, 32) and head_devices == 4
    placed = (
        P("seq", "head"),
        P("seq", "head"),
        P("seq", None),
        P(),
        P(None, "seq", None, "head"),
        P(None, "head"),
        P(None, "head"),
    )
    return jax.shard_map(
        shards_pairs if pairs else shards_general,
        mesh=mesh,
        in_specs=placed,
        out_specs=(P("seq", "head"), P(None, "seq", "head")),
        check_vma=False,
    )
```
